32 devices in a mesh: groups: 2 (over y), leaf: 4 (over z), pair: 2 (over x), rhs: 2 (over core).
Axes of the slice: x: 2, y: 2, z: 4, core: 2. Of those that a mesh axis runs over, the one named last changes fastest.
Arguments:
- points: bfloat16 [128, 512, 64], P(('groups', 'leaf')), parts along dimension 0, may hold values from -6 to 6
- weights: bfloat16 [65536, 32], P(('groups', 'leaf'), 'rhs'), parts along dimension 0, may hold values from -6 to 6
- interp: bfloat16 [128, 256, 256], P(('groups', 'leaf')), parts along dimension 0, may hold values from -0.375 to 0.375
- tree_order: int32 [8, 8192], P(('groups', 'leaf')), parts along dimension 0, may hold values from 0 to 8191, each once within a row
- skel_order: int32 [128, 512], P(('groups', 'leaf')), parts along dimension 0, may hold values from 0 to 511, each once within a row
- near_pairs: int32 [128, 16], P(('groups', 'leaf'), 'pair'), parts along dimension 0, may hold values from 0 to 63, as said below
- far_pairs: int32 [128, 8], P(('groups', 'leaf'), 'pair'), parts along dimension 0, may hold values from 0 to 63, as said below
Outputs:
- product: float32 [65536, 32], P(('groups', 'leaf'), 'rhs'), parts along dimension 0
The draws below stay inside these ranges and needn't reach their ends.
There are 2 independent parts, one for each index of `groups`. The reference program is written for one: setup_inputs(seed, part) draws one part's arguments, and reference() takes and returns one part's arrays. A program takes and returns all parts, laid end to end along the dimension named above; each array names one. Nothing has to cross between parts.
Inputs may be any that keep to these rules, and one draw needn't show every extreme that they name: `tree_order`: each row is a permutation of 0 to 8191. `skel_order`: each row is a permutation of 0 to 511; its first 256 entries are the skeleton points. `near_pairs`: every entry lies within 8 of its row's leaf; every row holds its own leaf and a leaf exactly 8 away. `far_pairs`: take the block of rows b * 16 to (b + 1) * 16 - 1 and columns p * 4 to (p + 1) * 4 - 1: its entries never lie in rows' own leaves b * 16 to (b + 1) * 16 - 1, and every block of leaves c * 16 to (c + 1) * 16 - 1 that its entries name is named by exactly 32 of them.
All inputs are finite; a program needn't handle non-finite values.
Results may differ from the reference program's by a relative error of at most 0.0035.
Values may be sent and summed in bfloat16 or wider, within the bound.
No kernel may reach another device: no remote copies, remote signals or barrier semaphores. Data moves between devices by JAX's collectives and lax.ppermute only.
A program may use at most 128 MiB of HBM per device.

```python
import jax
import jax.numpy as jnp
from jax import lax

LEAF = 512
RANK = 256
DIM = 64
RHS = 32
NEAR = 16
FAR = 8
LEAF_DEV = 16
LEAVES = 64
POINTS = 32768
BLOCKS = 4
SPAN = 8
FAR_DEV = 4
CAP = 32
N_LEAF = 4
N_PAIR = 2


def draw_near_pairs(key, part):
    key = jax.random.fold_in(key, 11)
    first, second, third = jax.random.split(key, 3)
    leaf_rows = jnp.arange(LEAVES, dtype=jnp.int32)
    signs = jax.random.randint(first, (LEAVES,), 0, 2).astype(jnp.int32) * 2 - 1
    others = jax.random.randint(second, (LEAVES, NEAR - 2), 1 - SPAN, SPAN).astype(jnp.int32)
    distances = jnp.concatenate([jnp.zeros((LEAVES, 1), jnp.int32), (signs * SPAN)[:, None], others], axis=1)
    scores = jax.random.randint(third, (LEAVES, NEAR), 0, 2 ** 20).astype(jnp.int32) * NEAR + jnp.arange(NEAR, dtype=jnp.int32)[None, :]
    shuffle = jnp.argsort(scores, axis=1).astype(jnp.int32)
    distances = jnp.take_along_axis(distances, shuffle, axis=1)
    sources = leaf_rows[:, None] + distances
    outside = (sources < 0) | (sources >= LEAVES)
    return jnp.where(outside, leaf_rows[:, None] - distances, sources).astype(jnp.int32)


def draw_far_pairs(key, part):
    key = jax.random.fold_in(key, 23)
    slot_count = LEAF_DEV * FAR_DEV
    used_count = slot_count // CAP

    def one_block(block_key, device):
        first, second, third = jax.random.split(block_key, 3)
        shifts = jax.random.permutation(first, N_LEAF - 1)[:used_count].astype(jnp.int32) + 1
        targets = (device + shifts) % N_LEAF
        slot_order = jax.random.permutation(second, slot_count).astype(jnp.int32)
        chosen = targets[slot_order // CAP]
        within = jax.random.randint(third, (slot_count,), 0, LEAF_DEV).astype(jnp.int32)
        return (chosen * LEAF_DEV + within).reshape(LEAF_DEV, FAR_DEV)
    block_keys = jax.random.split(key, N_LEAF * N_PAIR)
    devices = jnp.repeat(jnp.arange(N_LEAF, dtype=jnp.int32), N_PAIR)
    blocks = jax.vmap(one_block)(block_keys, devices)
    blocks = blocks.reshape(N_LEAF, N_PAIR, LEAF_DEV, FAR_DEV).transpose(0, 2, 1, 3)
    return blocks.reshape(LEAVES, FAR).astype(jnp.int32)


def block_scale(own_key, shape, cuts, low, largest):
    factor_of, own = 1.0, jax.random.fold_in(own_key, 6)
    for dim, parts in cuts:
        steps = jnp.exp(jax.random.uniform(jax.random.fold_in(own, dim), (parts,), jnp.float32, low / len(cuts), largest / len(cuts)))
        factor_of = factor_of * jnp.repeat(steps, shape[dim] // parts).reshape([-1 if axis == dim else 1 for axis in range(len(shape))])
    return factor_of


def centred(own_key, dims, width, bound, cuts=(), kind=jnp.bfloat16):
    result = jax.random.normal(own_key, dims, jnp.float32) * width
    if len(cuts) > 0:
        result = block_scale(own_key, dims, cuts, -0.22, 0.18) * result
    return jnp.clip(result, min=-bound, max=bound).astype(kind)


def setup_inputs(seed: int = 0, part: int = 0) -> dict:
    key_of = jax.random.split(jax.random.key(seed), 8)
    part_splits = jax.random.split(jax.random.fold_in(key_of[7], part), 8)
    return {
        "points": centred(part_splits[0], (LEAVES, LEAF, DIM), 1.0, 6.0, ((0, 4),)),
        "weights": centred(part_splits[1], (POINTS, RHS), 1.0, 6.0, ((0, 4), (1, 2))),
        "interp": centred(part_splits[2], (LEAVES, RANK, LEAF - RANK), (LEAF - RANK) ** -0.5, 0.375, ((0, 4),)),
        "tree_order": jax.vmap(lambda own: jax.random.permutation(own, LEAF_DEV * LEAF))(jax.random.split(part_splits[3], BLOCKS)).reshape((BLOCKS, LEAF_DEV * LEAF)).astype(jnp.int32),
        "skel_order": jax.vmap(lambda own: jax.random.permutation(own, LEAF))(jax.random.split(part_splits[4], LEAVES)).reshape((LEAVES, LEAF)).astype(jnp.int32),
        "near_pairs": draw_near_pairs(jax.random.fold_in(jax.random.fold_in(key_of[7], part), 71), part),
        "far_pairs": draw_far_pairs(jax.random.fold_in(jax.random.fold_in(key_of[7], part), 71), part),
    }


def squares_of(features):
    return jnp.sum(jnp.square(features.astype(jnp.float32)), axis=-1)


def kernel_block(targets, target_sq, sources, source_sq):
    inner = jnp.dot(targets, sources.T, preferred_element_type=jnp.float32)
    exponent = (2.0 * inner - target_sq[:, None] - source_sq[None, :]) * (2.5 / DIM)
    return jnp.exp(exponent).astype(jnp.bfloat16)


def reference(points, weights, interp, tree_order, skel_order, near_pairs, far_pairs):
    block_rows = LEAF_DEV * LEAF
    offsets = jnp.arange(BLOCKS, dtype=jnp.int32) * block_rows
    order = (tree_order + offsets[:, None]).reshape(-1).astype(jnp.int32)
    tree_weights = weights[order].reshape(LEAVES, LEAF, RHS)
    ordered = jnp.take_along_axis(tree_weights, skel_order[:, :, None], axis=1)
    combined = jnp.einsum('lrk,lkc->lrc', interp.astype(jnp.float32), ordered[:, RANK:].astype(jnp.float32))
    skel_weights = (ordered[:, :RANK].astype(jnp.float32) + combined).astype(jnp.bfloat16)
    skel_points = jnp.take_along_axis(points, skel_order[:, :RANK, None], axis=1)
    point_sq = squares_of(points)
    skel_sq = squares_of(skel_points)

    def near_leaf(inputs):
        leaf_index, source_ids = inputs
        sources = points[source_ids].reshape(-1, DIM)
        source_sq = point_sq[source_ids].reshape(-1)
        source_weights = tree_weights[source_ids].reshape(-1, RHS)
        block = kernel_block(points[leaf_index], point_sq[leaf_index], sources, source_sq)
        return jnp.dot(block, source_weights, preferred_element_type=jnp.float32)

    def far_leaf(inputs):
        leaf_index, source_ids = inputs
        sources = skel_points[source_ids].reshape(-1, DIM)
        source_sq = skel_sq[source_ids].reshape(-1)
        source_weights = skel_weights[source_ids].reshape(-1, RHS)
        block = kernel_block(skel_points[leaf_index], skel_sq[leaf_index], sources, source_sq)
        return jnp.dot(block, source_weights, preferred_element_type=jnp.float32)

    leaf_ids = jnp.arange(LEAVES, dtype=jnp.int32)
    near = lax.map(near_leaf, (leaf_ids, near_pairs))
    skel_field = lax.map(far_leaf, (leaf_ids, far_pairs)).astype(jnp.bfloat16)
    rest_field = jnp.einsum('lrk,lrc->lkc', interp.astype(jnp.float32), skel_field.astype(jnp.float32))
    expanded = jnp.concatenate([skel_field.astype(jnp.float32), rest_field], axis=1)
    placed = jnp.zeros((LEAVES, LEAF, RHS), jnp.float32).at[leaf_ids[:, None], skel_order].set(expanded)
    tree_field = near + placed
    return jnp.zeros((POINTS, RHS), jnp.float32).at[order].set(tree_field.reshape(-1, RHS))
```

```python
import functools

import jax
import jax.numpy as jnp
from jax import lax
from jax.experimental import pallas as pl
from jax.experimental.pallas import tpu as pltpu
from jax.sharding import PartitionSpec as P

BF = jnp.bfloat16
F32 = jnp.float32
LOG2E = 1.4426950408889634
EXTRA = 16
VMEM = pl.BlockSpec(memory_space=pltpu.VMEM)
SMEM = pl.BlockSpec(memory_space=pltpu.SMEM)
PARAMS = pltpu.CompilerParams(vmem_limit_bytes=48 << 20)


def call(body, shapes, specs, args, scratch=(), out_specs=None):
    outs = [jax.ShapeDtypeStruct(s, d) for s, d in shapes]
    return pl.pallas_call(
        body,
        out_shape=outs,
        in_specs=specs,
        out_specs=[VMEM] * len(outs) if out_specs is None else out_specs,
        scratch_shapes=list(scratch),
        compiler_params=PARAMS,
    )(*args)


def extra_rows(feat, ones_first):
    wide = feat.astype(F32)
    half = -0.5 * jnp.sum(wide * wide, axis=0, keepdims=True)
    high = half.astype(BF).astype(F32)
    mid = (half - high).astype(BF).astype(F32)
    low = half - high - mid
    row = lax.broadcasted_iota(jnp.int32, (EXTRA, feat.shape[1]), 0)
    at = 3 if ones_first else 0
    ones = (row < 3) if ones_first else (row >= 3) & (row < 6)
    picked = jnp.where(row == at, high, jnp.where(row == at + 1, mid, jnp.where(row == at + 2, low, 0.0)))
    return jnp.where(ones, 1.0, picked).astype(BF)


def as_targets(feat):
    return jnp.concatenate([feat, extra_rows(feat, False)], axis=0)


def as_sources(feat):
    return jnp.concatenate([feat, extra_rows(feat, True)], axis=0).astype(F32).T.astype(BF)


def one_hot(row_ids, count):
    rows = lax.broadcasted_iota(jnp.int32, (count, row_ids.shape[1]), 0)
    return jnp.where(rows == row_ids, 1.0, 0.0).astype(BF)


def dot(a, b):
    return jnp.dot(a, b, preferred_element_type=F32)


def dot_last(a, b):
    return lax.dot_general(a, b, (((1,), (1,)), ((), ())), preferred_element_type=F32)


def gauss(sources, targets, scale):
    return jnp.exp2(dot(sources, targets) * scale).astype(BF)


def skel_points_body(cls_ref, skel_ref, out_ref):
    rank = out_ref.shape[2]
    for j in range(cls_ref.shape[0]):
        hot = one_hot(skel_ref[j, :, :rank], cls_ref.shape[2])
        out_ref[j] = dot(cls_ref[j], hot).astype(BF)


def weights_body(own_ref, other_ref, order_ref, skel_ref, interp_ref, tw_ref, sw_ref, stack):
    cols = own_ref.shape[0]
    step = 2 * cols
    width = stack.shape[1]
    turns = own_ref.shape[1] // width
    rank = sw_ref.shape[2]
    for hi in range(turns):
        span = slice(hi * width, (hi + 1) * width)
        stack[hi * step : hi * step + cols] = own_ref[:, span]
        stack[hi * step + cols : (hi + 1) * step] = other_ref[:, span]

    def leaf(j, _):
        ids = order_ref[j]
        hi_ids = lax.shift_right_logical(ids, width.bit_length() - 1)
        picked = dot(stack[...], one_hot(ids & (width - 1), width))
        total = jnp.zeros((step, ids.shape[1]), F32)
        for hi in range(turns):
            total = total + jnp.where(hi_ids == hi, picked[hi * step : (hi + 1) * step], 0.0)
        tree = total.astype(BF)
        tw_ref[j] = tree
        ordered = dot(tree, one_hot(skel_ref[j], ids.shape[1]))
        combined = dot_last(ordered[:, rank:].astype(BF), interp_ref[j])
        sw_ref[j] = (ordered[:, :rank] + combined).astype(BF)
        return 0

    lax.fori_loop(0, order_ref.shape[0], leaf, 0)


def near_sum(t, first, count, most, scale, cnt_ref, slots, tgt, src, weights, write):
    found = jnp.int32(0)
    for e in range(count):
        slots[found] = jnp.int32(e)
        found = found + jnp.where(cnt_ref[t, first + e] > 0, 1, 0)
    for k in range(1, most + 1):

        @pl.when(found == k)
        def _():
            names = [slots[j] for j in range(k)]
            size = src.shape[1]
            block = gauss(jnp.concatenate([src[s] for s in names], axis=0), tgt[t], scale)
            total = None
            for j, s in enumerate(names):
                times = cnt_ref[t, first + s].astype(F32)
                part = dot(weights[s], block[j * size : (j + 1) * size]) * times
                total = part if total is None else total + part
            write(t, total)

    return found


def near_body(halo, scale, where_ref, cnt_ref, pts_ref, tw_ref, skel_ref, near_ref, tgt_ref, far_tgt_ref, src, slots):
    leaves = pts_ref.shape[0]
    mine = tw_ref.shape[0]
    classes = leaves // mine
    rank = far_tgt_ref.shape[2]

    def sources(j, _):
        src[j] = as_sources(pts_ref[j * classes + where_ref[0]])
        return 0

    lax.fori_loop(0, mine, sources, 0)

    def write(t, value):
        near_ref[t] = value

    def target(t, _):
        tgt_ref[t] = as_targets(pts_ref[t])
        found = near_sum(t, halo, mine, mine, scale, cnt_ref, slots, tgt_ref, src, tw_ref, write)

        @pl.when(found == 0)
        def _():
            near_ref[t] = jnp.zeros(near_ref.shape[1:], F32)

        hot = one_hot(skel_ref[t, :, :rank], pts_ref.shape[2])
        far_tgt_ref[t] = as_targets(dot(pts_ref[t], hot).astype(BF))
        return 0

    lax.fori_loop(0, leaves, target, 0)


def far_body(
    halo, mine, scale, cnt_ref, far_ref, near_ref, tgt_ref, left_p, right_p, left_w, right_w, far_tgt, far_p, far_w,
    interp_ref, skel_ref, own_ref, other_ref, src, wts, far_src, field, slots, far_t, far_s,
):
    leaves, cols2, size = near_ref.shape
    rank = far_tgt.shape[2]
    cols = cols2 // 2
    for j in range(halo):
        src[j] = as_sources(left_p[j])
        src[halo + j] = as_sources(right_p[j])
        wts[j] = left_w[j]
        wts[halo + j] = right_w[j]

    def write(t, value):
        near_ref[t] += value

    def target(t, _):
        half = leaves // 2

        @pl.when(t < half)
        def _():
            near_sum(t, 0, halo, halo, scale, cnt_ref, slots, tgt_ref, src, wts, write)

        @pl.when(t >= half)
        def _():
            near_sum(t, halo + mine, halo, halo, scale, cnt_ref, slots, tgt_ref, src.at[halo:], wts.at[halo:], write)

        field[t] = jnp.zeros(field.shape[1:], F32)
        return 0

    lax.fori_loop(0, leaves, target, 0)

    def far_sources(j, _):
        far_src[j] = as_sources(far_p[j])
        return 0

    lax.fori_loop(0, far_p.shape[0], far_sources, 0)
    slots_per = far_ref.shape[1]

    def listing(i, found):
        t = i // slots_per
        s = far_ref[t, i - t * slots_per]
        far_t[found] = t
        far_s[found] = s
        return found + jnp.where(s >= 0, 1, 0)

    found = lax.fori_loop(0, leaves * slots_per, listing, jnp.int32(0))
    group = 4
    for j in range(group):
        far_t[found + j] = jnp.int32(leaves)
        far_s[found + j] = jnp.int32(0)

    def far_group(g, _):
        for j in range(group):
            t = far_t[g * group + j]
            s = far_s[g * group + j]
            tt = jnp.minimum(t, leaves - 1)
            field[t] += dot(far_w[s], gauss(far_src[s], far_tgt[tt], scale))
        return 0

    lax.fori_loop(0, (found + group - 1) // group, far_group, 0)

    for t in range(leaves):
        skel = field[t].astype(BF)
        rest = dot(skel, interp_ref[t]).astype(BF)
        expanded = jnp.concatenate([skel, rest], axis=1)
        total = near_ref[t] + dot_last(expanded, one_hot(skel_ref[t], size))
        own_ref[:, t * size : (t + 1) * size] = total[:cols]
        other_ref[:, t * size : (t + 1) * size] = total[cols:].astype(BF)


def place_body(count, order_ref, *refs):
    parts, out_ref, acc = refs[:count], refs[count], refs[count + 1]
    cols, total = out_ref.shape
    width = acc.shape[1]
    turns = total // width
    chunk = 1024
    for at in range(0, total, chunk):
        span = slice(at, at + chunk)
        value = parts[0][:, span].astype(F32)
        for part in parts[1:]:
            value = value + part[:, span].astype(F32)
        ids = order_ref[:, span]
        hi_ids = lax.shift_right_logical(ids, width.bit_length() - 1)
        masked = [jnp.where(hi_ids == hi, value, 0.0).astype(BF) for hi in range(turns)]
        part = dot_last(jnp.concatenate(masked, axis=0), one_hot(ids & (width - 1), width))
        acc[...] = part if at == 0 else acc[...] + part
    for hi in range(turns):
        out_ref[:, hi * width : (hi + 1) * width] = acc[hi * cols : (hi + 1) * cols]


def ring(count, by):
    return [(i, (i + by) % count) for i in range(count)]


def from_others(value, axis):
    count = lax.axis_size(axis)
    return [lax.ppermute(value, axis, ring(count, by)) for by in range(1, count)]


def on_device(points, weights, interp, tree_order, skel_order, near_pairs, far_pairs):
    leaves, size, dim = points.shape
    rank = interp.shape[1]
    cols = weights.shape[1]
    blocks, pair_n, rhs_n = (lax.axis_size(a) for a in ("leaf", "pair", "rhs"))
    classes = pair_n * rhs_n
    mine = leaves // classes
    span = min(8, leaves)
    halo = span // classes
    block, mine_id = lax.axis_index("leaf"), lax.axis_index("pair") * rhs_n + lax.axis_index("rhs")
    scale = 2.0 * 2.5 / dim * LOG2E
    slot_n = far_pairs.shape[1] * pair_n

    def of_class(array):
        cut = array.reshape((mine, classes) + array.shape[1:])
        return lax.dynamic_index_in_dim(cut, mine_id, 1, keepdims=False)

    pts = points.transpose(0, 2, 1)
    wts = weights.T
    order = tree_order.reshape(leaves, 1, size)
    skel = skel_order.reshape(leaves, 1, size)
    (other_wts,) = from_others(wts, "rhs")
    cls_pts = of_class(pts)
    up, down = [(i, i + 1) for i in range(blocks - 1)], [(i + 1, i) for i in range(blocks - 1)]
    left_p = lax.ppermute(cls_pts[mine - halo :], "leaf", up)
    right_p = lax.ppermute(cls_pts[:halo], "leaf", down)
    pairs = jnp.concatenate([near_pairs, far_pairs], axis=1)
    every = jnp.stack([pairs] + from_others(pairs, "pair"), axis=1)
    near_n = near_pairs.shape[1]
    near_all = every[:, :, :near_n].reshape(leaves, -1) - (block * leaves - span)
    far_all = every[:, :, near_n:].reshape(leaves, -1)
    table = (jnp.arange(2 * halo + mine, dtype=jnp.int32) * classes + mine_id)[None, :, None]
    cnt = jnp.sum((near_all[:, None, :] == table).astype(jnp.int32), axis=2)
    owner, within = far_all // leaves, far_all % leaves
    piece = (block - owner) % blocks - 1
    far_ids = jnp.where(within % classes == mine_id, piece * mine + within // classes, -1)

    skel_cls, order_cls, interp_cls = of_class(skel), of_class(order), of_class(interp)
    (skel_p,) = call(skel_points_body, [((mine, dim, rank), BF)], [VMEM] * 2, (cls_pts, skel_cls))
    far_p = jnp.concatenate(from_others(skel_p, "leaf"), axis=0)
    tree_w, skel_w = call(
        weights_body,
        [((mine, 2 * cols, size), BF), ((mine, 2 * cols, rank), BF)],
        [VMEM] * 5,
        (wts, other_wts, order_cls, skel_cls, interp_cls),
        [pltpu.VMEM((2 * cols * (leaves * size // 256), 256), BF)],
    )
    left_w = lax.ppermute(tree_w[mine - halo :], "leaf", up)
    right_w = lax.ppermute(tree_w[:halo], "leaf", down)
    far_w = jnp.concatenate(from_others(skel_w, "leaf"), axis=0)
    wide = dim + EXTRA
    near, tgt, far_tgt = call(
        functools.partial(near_body, halo, scale),
        [((leaves, 2 * cols, size), F32), ((leaves, wide, size), BF), ((leaves, wide, rank), BF)],
        [SMEM, SMEM, VMEM, VMEM, VMEM],
        (mine_id.reshape(1), cnt, pts, tree_w, skel),
        [pltpu.VMEM((mine, size, wide), BF), pltpu.SMEM((mine + 1,), jnp.int32)],
    )
    far_n = (blocks - 1) * mine
    own, other = call(
        functools.partial(far_body, halo, mine, scale),
        [((cols, leaves * size), F32), ((cols, leaves * size), BF)],
        [SMEM, SMEM] + [VMEM] * 11,
        (cnt, far_ids, near, tgt, left_p, right_p, left_w, right_w, far_tgt, far_p, far_w, interp, skel),
        [
            pltpu.VMEM((2 * halo, size, wide), BF),
            pltpu.VMEM((2 * halo, 2 * cols, size), BF),
            pltpu.VMEM((far_n, rank, wide), BF),
            pltpu.VMEM((leaves + 1, 2 * cols, rank), F32),
            pltpu.SMEM((halo + 1,), jnp.int32),
            pltpu.SMEM((leaves * slot_n + 8,), jnp.int32),
            pltpu.SMEM((leaves * slot_n + 8,), jnp.int32),
        ],
    )
    (back,) = from_others(other, "rhs")
    both = (own + back.astype(F32)).astype(BF)
    parts = [both] + from_others(both, "pair") if pair_n == 2 else list(lax.all_gather(both, "pair"))
    (out,) = call(
        functools.partial(place_body, len(parts)),
        [((cols, leaves * size), F32)],
        [VMEM] * (1 + len(parts)),
        (tree_order, *parts),
        [pltpu.VMEM((leaves * size // 256 * cols, 256), F32)],
    )
    return out.T


def solution(mesh):
    return jax.shard_map(
        on_device,
        mesh=mesh,
        in_specs=(
            P(("groups", "leaf"), None, None),
            P(("groups", "leaf"), "rhs"),
            P(("groups", "leaf"), None, None),
            P(("groups", "leaf"), None),
            P(("groups", "leaf"), None),
            P(("groups", "leaf"), "pair"),
            P(("groups", "leaf"), "pair"),
        ),
        out_specs=P(("groups", "leaf"), "rhs"),
        check_vma=False,
    )
```

```python
import functools

import jax
import jax.numpy as jnp
from jax import lax
from jax.experimental import pallas as pl
from jax.experimental.pallas import tpu as pltpu
from jax.sharding import PartitionSpec as P

BF = jnp.bfloat16
F32 = jnp.float32
LOG2E = 1.4426950408889634
EXTRA = 16
GROUP = 4
VMEM = pl.BlockSpec(memory_space=pltpu.VMEM)
SMEM = pl.BlockSpec(memory_space=pltpu.SMEM)
PARAMS = pltpu.CompilerParams(vmem_limit_bytes=48 << 20)


def call(body, shapes, specs, args, scratch=(), flops=0, out_specs=None):
    outs = [jax.ShapeDtypeStruct(s, d) for s, d in shapes]
    return pl.pallas_call(
        body,
        out_shape=outs,
        in_specs=specs,
        out_specs=out_specs or [VMEM] * len(outs),
        scratch_shapes=list(scratch),
        compiler_params=PARAMS,
        cost_estimate=pl.CostEstimate(flops=flops, bytes_accessed=1 << 20, transcendentals=0),
    )(*args)


def extra_rows(feat, ones_first):
    wide = feat.astype(F32)
    half = -0.5 * jnp.sum(wide * wide, axis=0, keepdims=True)
    high = half.astype(BF).astype(F32)
    mid = (half - high).astype(BF).astype(F32)
    low = half - high - mid
    row = lax.broadcasted_iota(jnp.int32, (EXTRA, feat.shape[1]), 0)
    at = 3 if ones_first else 0
    ones = (row < 3) if ones_first else (row >= 3) & (row < 6)
    picked = jnp.where(row == at, high, jnp.where(row == at + 1, mid, jnp.where(row == at + 2, low, 0.0)))
    return jnp.where(ones, 1.0, picked).astype(BF)


def as_targets(feat):
    return jnp.concatenate([feat, extra_rows(feat, False)], axis=0)


def as_sources(feat):
    return jnp.concatenate([feat, extra_rows(feat, True)], axis=0).astype(F32).T.astype(BF)


def one_hot(row_ids, count):
    rows = lax.broadcasted_iota(jnp.int32, (count, row_ids.shape[1]), 0)
    return jnp.where(rows == row_ids, 1.0, 0.0).astype(BF)


def dot(a, b):
    return jnp.dot(a, b, preferred_element_type=F32)


def dot_last(a, b):
    return lax.dot_general(a, b, (((1,), (1,)), ((), ())), preferred_element_type=F32)


def gauss(sources, targets, scale):
    return jnp.exp2(dot(sources, targets) * scale).astype(BF)


def halo_body(ids_ref, pts_ref, near_ref, far_ref, up_ref, down_ref, pairs_ref, sems):
    halo = up_ref.shape[0]
    mine = ids_ref[2]
    classes = ids_ref[3]
    copies = []
    for j in range(halo):
        first = mine + j * classes
        last = mine + (pts_ref.shape[0] // 2) + j * classes
        copies.append(pltpu.make_async_copy(pts_ref.at[last], up_ref.at[j], sems.at[j]))
        copies.append(pltpu.make_async_copy(pts_ref.at[first], down_ref.at[j], sems.at[halo + j]))
    for copy in copies:
        copy.start()
    near_n = near_ref.shape[0]
    pairs_ref[:near_n] = near_ref[...]
    pairs_ref[near_n:] = far_ref[...]
    for copy in copies:
        copy.wait()


def weights_body(
    blocks, classes, near_n, ids_ref, own_ref, other_ref, order_ref, skel_ref, interp_ref, pts_ref, *refs
):
    pair_refs = refs[:-7]
    tw_ref, up_ref, down_ref, message_ref, cnt_ref, far_ref, stack = refs[-7:]
    cols = own_ref.shape[0]
    step = 2 * cols
    width = stack.shape[1]
    turns = own_ref.shape[1] // width
    mine, _, size = tw_ref.shape
    halo = up_ref.shape[0]
    rank = message_ref.shape[2]
    dim = pts_ref.shape[1]
    leaves = pts_ref.shape[0]
    block, base, me = ids_ref[0], ids_ref[1], ids_ref[2]
    for hi in range(turns):
        span = slice(hi * width, (hi + 1) * width)
        stack[hi * step : hi * step + cols] = own_ref[:, span]
        stack[hi * step + cols : (hi + 1) * step] = other_ref[:, span]

    for e in range(cnt_ref.shape[0]):
        wanted = base + e * classes + me
        total = None
        for ref in pair_refs:
            part = jnp.sum(jnp.where(ref[:near_n] == wanted, 1, 0), axis=0, keepdims=True)
            total = part if total is None else total + part
        cnt_ref[e : e + 1] = total
    far_n = far_ref.shape[0] // len(pair_refs)
    for k, ref in enumerate(pair_refs):
        named = ref[near_n:]
        owner = lax.div(named, leaves)
        within = lax.rem(named, leaves)
        piece = lax.rem(block - owner + blocks, blocks) - 1
        target = lax.broadcasted_iota(jnp.int32, named.shape, 1)
        code = target * 256 + piece * mine + lax.div(within, classes)
        far_ref[k * far_n : (k + 1) * far_n] = jnp.where(lax.rem(within, classes) == me, code, -1)

    for j in range(mine):
        leaf = j * classes + me
        ids = order_ref[:, pl.ds(pl.multiple_of(leaf * size, size), size)]
        hi_ids = lax.shift_right_logical(ids, width.bit_length() - 1)
        picked = dot(stack[...], one_hot(ids & (width - 1), width))
        total = jnp.zeros((step, size), F32)
        for hi in range(turns):
            total = total + jnp.where(hi_ids == hi, picked[hi * step : (hi + 1) * step], 0.0)
        tree = total.astype(BF)
        tw_ref[j] = tree
        if j < halo:
            down_ref[j] = tree
        if j >= mine - halo:
            up_ref[j - (mine - halo)] = tree
        hot = one_hot(skel_ref[pl.ds(leaf, 1), :], size)
        ordered = dot(tree, hot)
        combined = dot_last(ordered[:, rank:].astype(BF), interp_ref[leaf])
        message_ref[j, :dim] = dot(pts_ref[leaf], hot[:, :rank]).astype(BF)
        message_ref[j, dim:] = (ordered[:, :rank] + combined).astype(BF)


def near_sum(t, first, count, most, scale, cnt_ref, slots, tgt, src, weights, write, shift=0):
    found = jnp.int32(0)
    for e in range(count):
        slots[found] = jnp.int32(e)
        found = found + jnp.where(cnt_ref[first + e, t] > 0, 1, 0)
    for k in range(most + 1):

        @pl.when(found == k)
        def _():
            names = [slots[j] for j in range(k)]
            if k == 0:
                write(t, jnp.zeros((weights.shape[1], tgt.shape[2]), F32))
                return
            size = src.shape[1]
            block = gauss(jnp.concatenate([src[s + shift] for s in names], axis=0), tgt[t], scale)
            total = None
            for j, s in enumerate(names):
                times = cnt_ref[first + s, t].astype(F32)
                part = dot(weights[s + shift], block[j * size : (j + 1) * size]) * times
                total = part if total is None else total + part
            write(t, total)


def near_body(
    halo, scale, ids_ref, cnt_ref, pts_ref, tw_ref, left_p, right_p, near_ref, tgt_ref, edge_src, src, slots
):
    leaves = pts_ref.shape[0]
    mine = tw_ref.shape[0]
    classes = leaves // mine

    def sources(j, _):
        src[j] = as_sources(pts_ref[j * classes + ids_ref[2]])
        return 0

    lax.fori_loop(0, mine, sources, 0)
    for j in range(halo):
        edge_src[j] = as_sources(left_p[j])
        edge_src[halo + j] = as_sources(right_p[j])

    def write(t, value):
        near_ref[t] = value

    def target(t, _):
        tgt_ref[t] = as_targets(pts_ref[t])
        near_sum(t, halo, mine, mine, scale, cnt_ref, slots, tgt_ref, src, tw_ref, write)
        return 0

    lax.fori_loop(0, leaves, target, 0)


def edge_body(
    halo, mine, scale, cnt_ref, near_ref, tgt_ref, src, left_w, right_w, pts_ref, skel_ref, order_ref,
    own_ref, other_ref, far_tgt_ref, comp_ref, wts, slots,
):
    leaves, cols2, size = near_ref.shape
    cols = cols2 // 2
    rank = far_tgt_ref.shape[2]
    for j in range(halo):
        wts[j] = left_w[j]
        wts[halo + j] = right_w[j]

    def write(t, value):
        total = near_ref[t] + value
        own_ref[:, pl.ds(pl.multiple_of(t * size, size), size)] = total[:cols]
        other_ref[:, pl.ds(pl.multiple_of(t * size, size), size)] = total[cols:].astype(BF)

    def target(t, _):
        right = jnp.where(t < leaves // 2, 0, 1)
        near_sum(t, right * (halo + mine), halo, halo, scale, cnt_ref, slots, tgt_ref, src, wts, write, right * halo)
        span = pl.ds(pl.multiple_of(t * size, size), size)
        hot = one_hot(skel_ref[pl.ds(t, 1), :], size)
        far_tgt_ref[t] = as_targets(dot(pts_ref[t], hot[:, :rank]).astype(BF))
        ids = order_ref[:, span]
        row = lax.broadcasted_iota(jnp.int32, (16, size), 0)
        halves = jnp.where(row == 0, lax.shift_right_logical(ids, 8), jnp.where(row == 1, ids & 255, 0))
        moved = dot(halves.astype(F32).astype(BF), hot)
        comp_ref[:, span] = (moved[:1] * 256.0 + moved[1:2]).astype(jnp.int32)
        return 0

    lax.fori_loop(0, leaves, target, 0)


def sources_body(mine, far_ref, *refs):
    pieces = refs[:-3]
    far_src, far_w, names = refs[-3:]
    dim = pieces[0].shape[1] - far_w.shape[1]
    for k, piece in enumerate(pieces):
        for j in range(mine):
            far_src[k * mine + j] = as_sources(piece[j, :dim])
            far_w[k * mine + j] = piece[j, dim:]
    found = jnp.int32(0)
    for t in range(far_ref.shape[1]):
        for i in range(far_ref.shape[0]):
            code = far_ref[i, t]
            names[1 + found] = code
            found = found + jnp.where(code >= 0, 1, 0)
    names[0] = found
    for j in range(GROUP):
        names[1 + found + j] = jnp.int32(far_ref.shape[1] * 256)


def far_body(scale, names, far_src, far_w, far_tgt, after_ref, own_ref, other_ref, field):
    leaves, _, rank = far_tgt.shape
    cols = own_ref.shape[0]
    field[...] = jnp.zeros_like(field)

    def far_group(g, _):
        codes = [names[1 + g * GROUP + j] for j in range(GROUP)]
        targets = [lax.shift_right_logical(c, 8) for c in codes]
        blocks = [gauss(far_src[c & 255], far_tgt[t & (leaves - 1)], scale) for c, t in zip(codes, targets)]
        parts = [dot(far_w[c & 255], block) for c, block in zip(codes, blocks)]
        for t, part in zip(targets, parts):
            field[t] += part
        return 0

    lax.fori_loop(0, lax.div(names[0] + GROUP - 1, GROUP), far_group, 0)
    for t in range(leaves):
        own_ref[:, t * rank : (t + 1) * rank] = field[t, :cols]
        other_ref[:, t * rank : (t + 1) * rank] = field[t, cols:].astype(BF)


def scatter(ids, value, width, turns):
    hi_ids = lax.shift_right_logical(ids, width.bit_length() - 1)
    masked = [jnp.where(hi_ids == hi, value, 0.0).astype(BF) for hi in range(turns)]
    return dot_last(jnp.concatenate(masked, axis=0), one_hot(ids & (width - 1), width))


def place_near_body(order_ref, *refs):
    near, acc = refs[:-1], refs[-1]
    total = order_ref.shape[1]
    width = acc.shape[1]
    chunk = 1024
    for at in range(0, total, chunk):
        span = slice(at, at + chunk)
        value = sum(ref[:, span].astype(F32) for ref in near)
        part = scatter(order_ref[:, span], value, width, total // width)
        acc[...] = part if at == 0 else acc[...] + part


def place_far_body(comp_ref, interp_ref, start_ref, *refs):
    far, out_ref, acc = refs[:-2], refs[-2], refs[-1]
    cols, total = out_ref.shape
    width = acc.shape[1]
    turns = total // width
    leaves, rank, _ = interp_ref.shape
    size = total // leaves
    for t in range(leaves):
        skel = sum(ref[:, t * rank : (t + 1) * rank].astype(F32) for ref in far).astype(BF)
        value = jnp.concatenate([skel.astype(F32), dot(skel, interp_ref[t])], axis=1)
        part = scatter(comp_ref[:, t * size : (t + 1) * size], value, width, turns)
        acc[...] = (start_ref if t == 0 else acc)[...] + part
    for hi in range(turns):
        out_ref[:, hi * width : (hi + 1) * width] = acc[hi * cols : (hi + 1) * cols]


def ring(count, by):
    return [(i, (i + by) % count) for i in range(count)]


def from_others(value, axis):
    count = lax.axis_size(axis)
    return [lax.ppermute(value, axis, ring(count, by)) for by in range(1, count)]


def over_pair(value, pair_n):
    if pair_n == 2:
        return [value] + from_others(value, "pair")
    return list(lax.all_gather(value, "pair"))


def on_device(points, weights, interp, tree_order, skel_order, near_pairs, far_pairs):
    leaves, size, dim = points.shape
    rank = interp.shape[1]
    cols = weights.shape[1]
    blocks, pair_n, rhs_n = (lax.axis_size(a) for a in ("leaf", "pair", "rhs"))
    classes = pair_n * rhs_n
    mine = leaves // classes
    span = min(8, leaves)
    halo = span // classes
    block = lax.axis_index("leaf")
    mine_id = lax.axis_index("pair") * rhs_n + lax.axis_index("rhs")
    scale = 2.0 * 2.5 / dim * LOG2E
    near_n, far_n = near_pairs.shape[1], far_pairs.shape[1]
    wide = dim + EXTRA
    mega = 10 ** 9
    ids = jnp.stack([block, block * leaves - span, mine_id, jnp.int32(classes)]).astype(jnp.int32)
    pts = points.transpose(0, 2, 1)
    wts = weights.T
    up, down = [(i, i + 1) for i in range(blocks - 1)], [(i + 1, i) for i in range(blocks - 1)]
    (other_wts,) = from_others(wts, "rhs")
    up_p, down_p, pairs = call(
        halo_body,
        [((halo, dim, size), BF), ((halo, dim, size), BF), ((near_n + far_n, leaves), jnp.int32)],
        [SMEM, pl.BlockSpec(memory_space=pl.ANY), VMEM, VMEM],
        (ids, pts, near_pairs.T, far_pairs.T),
        [pltpu.SemaphoreType.DMA((2 * halo,))],
    )
    every = [pairs] + from_others(pairs, "pair")
    left_p = lax.ppermute(up_p, "leaf", up)
    right_p = lax.ppermute(down_p, "leaf", down)
    tree_w, up_w, down_w, message, cnt, far_ids = call(
        functools.partial(weights_body, blocks, classes, near_n),
        [
            ((mine, 2 * cols, size), BF),
            ((halo, 2 * cols, size), BF),
            ((halo, 2 * cols, size), BF),
            ((mine, dim + 2 * cols, rank), BF),
            ((2 * halo + mine, leaves), jnp.int32),
            ((pair_n * far_n, leaves), jnp.int32),
        ],
        [SMEM] + [VMEM] * (6 + pair_n),
        (ids, wts, other_wts, tree_order, skel_order, interp, pts, *every),
        [pltpu.VMEM((2 * cols * (leaves * size // 256), 256), BF)],
        flops=3 * mega,
    )
    left_w = lax.ppermute(up_w, "leaf", up)
    right_w = lax.ppermute(down_w, "leaf", down)
    pieces = from_others(message, "leaf")
    near, tgt, edge_src = call(
        functools.partial(near_body, halo, scale),
        [((leaves, 2 * cols, size), F32), ((leaves, wide, size), BF), ((2 * halo, size, wide), BF)],
        [SMEM, SMEM, VMEM, VMEM, VMEM, VMEM],
        (ids, cnt, pts, tree_w, left_p, right_p),
        [pltpu.VMEM((mine, size, wide), BF), pltpu.SMEM((mine + 1,), jnp.int32)],
        flops=14 * mega,
    )
    near_own, near_other, far_tgt, comp = call(
        functools.partial(edge_body, halo, mine, scale),
        [((cols, leaves * size), F32), ((cols, leaves * size), BF), ((leaves, wide, rank), BF), ((1, leaves * size), jnp.int32)],
        [SMEM] + [VMEM] * 8,
        (cnt, near, tgt, edge_src, left_w, right_w, pts, skel_order, tree_order),
        [
            pltpu.VMEM((2 * halo, 2 * cols, size), BF),
            pltpu.SMEM((halo + 1,), jnp.int32),
        ],
        flops=6 * mega,
    )
    (near_back,) = from_others(near_other, "rhs")
    near_sum_own = (near_own + near_back.astype(F32)).astype(BF)
    near_parts = over_pair(near_sum_own, pair_n)
    piece_n = (blocks - 1) * mine
    far_src, far_w, names = call(
        functools.partial(sources_body, mine),
        [((piece_n, rank, wide), BF), ((piece_n, 2 * cols, rank), BF), ((leaves * pair_n * far_n + 16,), jnp.int32)],
        [SMEM] + [VMEM] * (blocks - 1),
        (far_ids, *pieces),
        out_specs=[VMEM, VMEM, SMEM],
        flops=2 * mega,
    )
    far_own, far_other = call(
        functools.partial(far_body, scale),
        [((cols, leaves * rank), F32), ((cols, leaves * rank), BF)],
        [SMEM, VMEM, VMEM, VMEM, pl.BlockSpec(memory_space=pl.ANY)],
        (names, far_src, far_w, far_tgt, near_sum_own),
        [pltpu.VMEM((leaves + 1, 2 * cols, rank), F32)],
        flops=4 * mega,
    )
    (far_back,) = from_others(far_other, "rhs")
    far_parts = over_pair((far_own + far_back.astype(F32)).astype(BF), pair_n)
    acc_shape = (leaves * size // 256 * cols, 256)
    (acc,) = call(
        place_near_body,
        [(acc_shape, F32)],
        [VMEM] * (1 + pair_n),
        (tree_order, *near_parts),
        flops=3 * mega,
    )
    (out,) = call(
        place_far_body,
        [((cols, leaves * size), F32)],
        [VMEM] * (3 + pair_n),
        (comp, interp, acc, *far_parts),
        [pltpu.VMEM(acc_shape, F32)],
        flops=4 * mega,
    )
    return out.T


def solution(mesh):
    return jax.shard_map(
        on_device,
        mesh=mesh,
        in_specs=(
            P(("groups", "leaf"), None, None),
            P(("groups", "leaf"), "rhs"),
            P(("groups", "leaf"), None, None),
            P(("groups", "leaf"), None),
            P(("groups", "leaf"), None),
            P(("groups", "leaf"), "pair"),
            P(("groups", "leaf"), "pair"),
        ),
        out_specs=P(("groups", "leaf"), "rhs"),
        check_vma=False,
    )
```

```python
import functools

import jax
import jax.numpy as jnp
from jax import lax
from jax.experimental import pallas as pl
from jax.experimental.pallas import tpu as pltpu
from jax.sharding import PartitionSpec as P

BF = jnp.bfloat16
F32 = jnp.float32
LOG2E = 1.4426950408889634
EXTRA = 16
GROUP = 8
VMEM = pl.BlockSpec(memory_space=pltpu.VMEM)
SMEM = pl.BlockSpec(memory_space=pltpu.SMEM)


def call(body, shapes, specs, args, scratch=(), flops=0, out_specs=None, grant=48):
    outs = [jax.ShapeDtypeStruct(s, d) for s, d in shapes]
    return pl.pallas_call(
        body,
        out_shape=outs,
        in_specs=specs,
        out_specs=out_specs or [VMEM] * len(outs),
        scratch_shapes=list(scratch),
        compiler_params=pltpu.CompilerParams(vmem_limit_bytes=grant << 20),
        cost_estimate=pl.CostEstimate(flops=flops, bytes_accessed=1 << 20, transcendentals=0),
    )(*args)


def extra_rows(feat, ones_first):
    wide = feat.astype(F32)
    half = -0.5 * jnp.sum(wide * wide, axis=0, keepdims=True)
    high = half.astype(BF).astype(F32)
    mid = (half - high).astype(BF).astype(F32)
    low = half - high - mid
    row = lax.broadcasted_iota(jnp.int32, (EXTRA, feat.shape[1]), 0)
    at = 3 if ones_first else 0
    ones = (row < 3) if ones_first else (row >= 3) & (row < 6)
    picked = jnp.where(row == at, high, jnp.where(row == at + 1, mid, jnp.where(row == at + 2, low, 0.0)))
    return jnp.where(ones, 1.0, picked).astype(BF)


def as_targets(feat):
    return jnp.concatenate([feat, extra_rows(feat, False)], axis=0)


def as_sources(feat):
    return jnp.concatenate([feat, extra_rows(feat, True)], axis=0).astype(F32).T.astype(BF)


def one_hot(row_ids, count):
    rows = lax.broadcasted_iota(jnp.int32, (count, row_ids.shape[1]), 0)
    return jnp.where(rows == row_ids, 1.0, 0.0).astype(BF)


def dot(a, b):
    return jnp.dot(a, b, preferred_element_type=F32)


def dot_last(a, b):
    return lax.dot_general(a, b, (((1,), (1,)), ((), ())), preferred_element_type=F32)


def gauss(sources, targets, scale):
    return jnp.exp2(dot(sources, targets) * scale).astype(BF)


def halo_body(ids_ref, pts_ref, near_ref, far_ref, first_ref, second_ref, pairs_ref, near_buf, far_buf, sems):
    halo = first_ref.shape[0]
    even = 1 - lax.rem(ids_ref[0], 2)
    mine, classes = ids_ref[2], ids_ref[3]
    half = pts_ref.shape[0] // 2
    copies = [
        pltpu.make_async_copy(near_ref, near_buf, sems.at[2 * halo]),
        pltpu.make_async_copy(far_ref, far_buf, sems.at[2 * halo + 1]),
    ]
    for j in range(halo):
        leaf = mine + j * classes
        copies.append(pltpu.make_async_copy(pts_ref.at[leaf + even * half], first_ref.at[j], sems.at[j]))
        copies.append(pltpu.make_async_copy(pts_ref.at[leaf + (1 - even) * half], second_ref.at[j], sems.at[halo + j]))
    for copy in copies:
        copy.start()
    for copy in copies:
        copy.wait()
    near_n = near_ref.shape[0]
    pairs_ref[:near_n] = near_buf[...]
    pairs_ref[near_n:] = far_buf[...]


def weights_body(
    blocks, classes, near_n, ids_ref, own_ref, other_ref, order_ref, skel_ref, interp_ref, pts_ref, *refs
):
    pair_refs = refs[:-13]
    tw_ref, up_ref, mid_ref, down_ref, cnt_ref, far_ref = refs[-13:-7]
    stack, own_buf, order_buf, skel_buf, interp_buf, pts_buf, sems = refs[-7:]
    cols = own_ref.shape[0]
    step = 2 * cols
    width = stack.shape[1]
    turns = own_ref.shape[1] // width
    mine, _, size = tw_ref.shape
    rank = mid_ref.shape[1]
    dim = pts_ref.shape[1]
    tall = dim + step
    cuts = size // rank
    halo = (up_ref.shape[0] - mid_ref.shape[0]) // (cuts * step)
    leaves = pts_ref.shape[0]
    block, base, me = ids_ref[0], ids_ref[1], ids_ref[2]
    copies = [
        pltpu.make_async_copy(own_ref, own_buf, sems.at[0]),
        pltpu.make_async_copy(order_ref, order_buf, sems.at[1]),
        pltpu.make_async_copy(skel_ref, skel_buf, sems.at[2]),
    ]
    for j in range(mine):
        leaf = j * classes + me
        copies.append(pltpu.make_async_copy(interp_ref.at[leaf], interp_buf.at[j], sems.at[3 + 2 * j]))
        copies.append(pltpu.make_async_copy(pts_ref.at[leaf], pts_buf.at[j], sems.at[4 + 2 * j]))
    for copy in copies:
        copy.start()
    for e in range(cnt_ref.shape[0]):
        wanted = base + e * classes + me
        total = None
        for ref in pair_refs:
            part = jnp.sum(jnp.where(ref[:near_n] == wanted, 1, 0), axis=0, keepdims=True)
            total = part if total is None else total + part
        cnt_ref[e : e + 1] = total
    far_n = far_ref.shape[0] // len(pair_refs)
    for k, ref in enumerate(pair_refs):
        named = ref[near_n:]
        owner = lax.div(named, leaves)
        within = lax.rem(named, leaves)
        piece = lax.rem(block - owner + blocks, blocks) - 1
        target = lax.broadcasted_iota(jnp.int32, named.shape, 1)
        code = target * 256 + piece * mine + lax.div(within, classes)
        far_ref[k * far_n : (k + 1) * far_n] = jnp.where(lax.rem(within, classes) == me, code, -1)

    for copy in copies:
        copy.wait()
    for hi in range(turns):
        span = slice(hi * width, (hi + 1) * width)
        stack[hi * step : hi * step + cols] = own_buf[:, span]
        stack[hi * step + cols : (hi + 1) * step] = other_ref[:, span]
    for j in range(mine):
        leaf = j * classes + me
        ids = order_buf[:, pl.ds(pl.multiple_of(leaf * size, size), size)]
        hi_ids = lax.shift_right_logical(ids, width.bit_length() - 1)
        picked = dot(stack[...], one_hot(ids & (width - 1), width))
        total = jnp.zeros((step, size), F32)
        for hi in range(turns):
            total = total + jnp.where(hi_ids == hi, picked[hi * step : (hi + 1) * step], 0.0)
        tree = total.astype(BF)
        tw_ref[j] = tree
        for ref, place in ((down_ref, j), (up_ref, j - (mine - halo))):
            if 0 <= place < halo:
                for cut in range(cuts):
                    at = mine * tall + (place * cuts + cut) * step
                    ref[at : at + step] = tree[:, cut * rank : (cut + 1) * rank]
        hot = one_hot(skel_buf[pl.ds(leaf, 1), :], size)
        ordered = dot(tree, hot)
        combined = dot_last(ordered[:, rank:].astype(BF), interp_buf[j])
        skel_p = dot(pts_buf[j], hot[:, :rank]).astype(BF)
        skel_w = (ordered[:, :rank] + combined).astype(BF)
        for ref in (up_ref, mid_ref, down_ref):
            ref[j * tall : j * tall + dim] = skel_p
            ref[j * tall + dim : (j + 1) * tall] = skel_w


def near_sum(t, first, count, most, scale, cnt_ref, slots, tgt, src, weights, write, shift=0):
    found = jnp.int32(0)
    for e in range(count):
        slots[found] = jnp.int32(e)
        found = found + jnp.where(cnt_ref[first + e, t] > 0, 1, 0)
    for k in range(most + 1):

        @pl.when(found == k)
        def _():
            names = [slots[j] for j in range(k)]
            if k == 0:
                write(t, jnp.zeros((weights.shape[1], tgt.shape[2]), F32))
                return
            size = src.shape[1]
            block = gauss(jnp.concatenate([src[s + shift] for s in names], axis=0), tgt[t], scale)
            total = None
            for j, s in enumerate(names):
                times = cnt_ref[first + s, t].astype(F32)
                part = dot(weights[s + shift], block[j * size : (j + 1) * size]) * times
                total = part if total is None else total + part
            write(t, total)


def near_body(
    halo, scale, ids_ref, cnt_ref, pts_ref, tw_ref, first_p, second_p, near_ref, tgt_ref, edge_src, src, slots
):
    leaves = pts_ref.shape[0]
    mine = tw_ref.shape[0]
    classes = leaves // mine

    def sources(j, _):
        src[j] = as_sources(pts_ref[j * classes + ids_ref[2]])
        return 0

    lax.fori_loop(0, mine, sources, 0)
    odd = lax.rem(ids_ref[0], 2)
    for j in range(halo):
        edge_src[(1 - odd) * halo + j] = as_sources(first_p[j])
        edge_src[odd * halo + j] = as_sources(second_p[j])

    def write(t, value):
        near_ref[t] = value

    def target(t, _):
        tgt_ref[t] = as_targets(pts_ref[t])
        near_sum(t, halo, mine, mine, scale, cnt_ref, slots, tgt_ref, src, tw_ref, write)
        return 0

    lax.fori_loop(0, leaves, target, 0)


def edge_body(
    halo, mine, scale, cnt_ref, near_ref, tgt_ref, src, left_m, right_m, pts_ref, skel_ref,
    own_ref, other_ref, far_tgt_ref, wts, slots,
):
    leaves, cols2, size = near_ref.shape
    cols = cols2 // 2
    rank = far_tgt_ref.shape[2]
    for j in range(halo):
        for side, ref in enumerate((left_m, right_m)):
            for cut in range(size // rank):
                at = ref.shape[0] - (halo * (size // rank) - j * (size // rank) - cut) * cols2
                wts[side * halo + j, :, cut * rank : (cut + 1) * rank] = ref[at : at + cols2]

    def write(t, value):
        total = near_ref[t] + value
        own_ref[:, pl.ds(pl.multiple_of(t * size, size), size)] = total[:cols]
        other_ref[:, pl.ds(pl.multiple_of(t * size, size), size)] = total[cols:].astype(BF)

    def target(t, _):
        right = jnp.where(t < leaves // 2, 0, 1)
        near_sum(t, right * (halo + mine), halo, halo, scale, cnt_ref, slots, tgt_ref, src, wts, write, right * halo)
        hot = one_hot(skel_ref[pl.ds(t, 1), :rank], size)
        far_tgt_ref[t] = as_targets(dot(pts_ref[t], hot).astype(BF))
        return 0

    lax.fori_loop(0, leaves, target, 0)


def sources_body(mine, far_ref, *refs):
    pieces = refs[:-3]
    far_src, far_w, names = refs[-3:]
    cols2 = far_w.shape[1]
    dim = far_src.shape[2] - EXTRA
    tall = dim + cols2
    for k, piece in enumerate(pieces):
        for j in range(mine):
            far_src[k * mine + j] = as_sources(piece[j * tall : j * tall + dim])
            far_w[k * mine + j] = piece[j * tall + dim : (j + 1) * tall]
    found = jnp.int32(0)
    for t in range(far_ref.shape[1]):
        for i in range(far_ref.shape[0]):
            code = far_ref[i, t]
            names[1 + found] = code
            found = found + jnp.where(code >= 0, 1, 0)
    names[0] = found
    for j in range(GROUP):
        names[1 + found + j] = jnp.int32(far_ref.shape[1] * 256)


def sum_body(own_ref, back_ref, *refs):
    refs[-1][...] = (own_ref[...] + back_ref[...].astype(F32)).astype(BF)


def far_body(scale, names, far_src, far_w, far_tgt, after_ref, own_ref, other_ref, field):
    leaves, _, rank = far_tgt.shape
    cols = own_ref.shape[0]
    field[...] = jnp.zeros_like(field)

    def far_group(g, _):
        codes = [names[1 + g * GROUP + j] for j in range(GROUP)]
        targets = [lax.shift_right_logical(c, 8) for c in codes]
        blocks = [gauss(far_src[c & 255], far_tgt[t & (leaves - 1)], scale) for c, t in zip(codes, targets)]
        parts = [dot(far_w[c & 255], block) for c, block in zip(codes, blocks)]
        for t, part in zip(targets, parts):
            field[t] += part
        return 0

    lax.fori_loop(0, lax.div(names[0] + GROUP - 1, GROUP), far_group, 0)
    for t in range(leaves):
        own_ref[:, t * rank : (t + 1) * rank] = field[t, :cols]
        other_ref[:, t * rank : (t + 1) * rank] = field[t, cols:].astype(BF)


def scatter(ids, value, width, turns):
    hi_ids = lax.shift_right_logical(ids, width.bit_length() - 1)
    masked = [jnp.where(hi_ids == hi, value, 0.0).astype(BF) for hi in range(turns)]
    return dot_last(jnp.concatenate(masked, axis=0), one_hot(ids & (width - 1), width))


def place_near_body(order_ref, skel_ref, *refs):
    near, acc, comp_ref = refs[:-2], refs[-2], refs[-1]
    total = order_ref.shape[1]
    width = acc.shape[1]
    chunk = 1024
    for at in range(0, total, chunk):
        span = slice(at, at + chunk)
        value = sum(ref[:, span].astype(F32) for ref in near)
        part = scatter(order_ref[:, span], value, width, total // width)
        acc[...] = part if at == 0 else acc[...] + part
    leaves, size = skel_ref.shape
    for t in range(leaves):
        span = slice(t * size, (t + 1) * size)
        ids = order_ref[:, span]
        row = lax.broadcasted_iota(jnp.int32, (16, size), 0)
        halves = jnp.where(row == 0, lax.shift_right_logical(ids, 8), jnp.where(row == 1, ids & 255, 0))
        moved = dot(halves.astype(F32).astype(BF), one_hot(skel_ref[t : t + 1], size))
        comp_ref[:, span] = (moved[:1] * 256.0 + moved[1:2]).astype(jnp.int32)


def place_far_body(comp_ref, interp_ref, start_ref, *refs):
    far, out_ref, acc, buf = refs[:-3], refs[-3], refs[-2], refs[-1]
    cols, total = out_ref.shape
    width = acc.shape[1]
    turns = total // width
    leaves, rank, _ = interp_ref.shape
    size = total // leaves
    for t in range(leaves):
        skel = sum(ref[:, t * rank : (t + 1) * rank].astype(F32) for ref in far).astype(BF)
        buf[:, t * size : t * size + rank] = skel.astype(F32)
        buf[:, t * size + rank : (t + 1) * size] = dot(skel, interp_ref[t])
    chunk = 1024
    for at in range(0, total, chunk):
        span = slice(at, at + chunk)
        part = scatter(comp_ref[:, span], buf[:, span], width, turns)
        acc[...] = (start_ref if at == 0 else acc)[...] + part
    for hi in range(turns):
        out_ref[:, hi * width : (hi + 1) * width] = acc[hi * cols : (hi + 1) * cols]


def ring(count, by):
    return [(i, (i + by) % count) for i in range(count)]


def from_others(value, axis):
    count = lax.axis_size(axis)
    return [lax.ppermute(value, axis, ring(count, by)) for by in range(1, count)]


def over_pair(value, pair_n):
    if pair_n == 2:
        return [value] + from_others(value, "pair")
    return list(lax.all_gather(value, "pair"))


def on_device(points, weights, interp, tree_order, skel_order, near_pairs, far_pairs):
    leaves, size, dim = points.shape
    rank = interp.shape[1]
    cols = weights.shape[1]
    blocks, pair_n, rhs_n = (lax.axis_size(a) for a in ("leaf", "pair", "rhs"))
    classes = pair_n * rhs_n
    mine = leaves // classes
    span = min(8, leaves)
    halo = span // classes
    block = lax.axis_index("leaf")
    mine_id = lax.axis_index("pair") * rhs_n + lax.axis_index("rhs")
    scale = 2.0 * 2.5 / dim * LOG2E
    near_n, far_n = near_pairs.shape[1], far_pairs.shape[1]
    wide = dim + EXTRA
    mega = 10 ** 9
    ids = jnp.stack([block, block * leaves - span, mine_id, jnp.int32(classes)]).astype(jnp.int32)
    pts = points.transpose(0, 2, 1)
    wts = weights.T
    (other_wts,) = from_others(wts, "rhs")
    swaps = []
    for start in (0, 1):
        swap = {i: i for i in range(blocks)}
        for i in range(start, blocks - 1, 2):
            swap[i], swap[i + 1] = i + 1, i
        swaps.append(list(swap.items()))
    hbm = pl.BlockSpec(memory_space=pltpu.HBM)
    first_p, second_p, pairs = call(
        halo_body,
        [((halo, dim, size), BF), ((halo, dim, size), BF), ((near_n + far_n, leaves), jnp.int32)],
        [SMEM, hbm, hbm, hbm],
        (ids, pts, near_pairs.T, far_pairs.T),
        [
            pltpu.VMEM((near_n, leaves), jnp.int32),
            pltpu.VMEM((far_n, leaves), jnp.int32),
            pltpu.SemaphoreType.DMA((2 * halo + 2,)),
        ],
        grant=60,
    )
    every = [pairs] + from_others(pairs, "pair")
    first_p = lax.ppermute(first_p, "leaf", swaps[0])
    second_p = lax.ppermute(second_p, "leaf", swaps[1])
    tall = mine * (dim + 2 * cols)
    extra = halo * (size // rank) * 2 * cols
    tree_w, up_m, mid_m, down_m, cnt, far_ids = call(
        functools.partial(weights_body, blocks, classes, near_n),
        [
            ((mine, 2 * cols, size), BF),
            ((tall + extra, rank), BF),
            ((tall, rank), BF),
            ((tall + extra, rank), BF),
            ((2 * halo + mine, leaves), jnp.int32),
            ((pair_n * far_n, leaves), jnp.int32),
        ],
        [SMEM, hbm, VMEM] + [hbm] * 4 + [VMEM] * pair_n,
        (ids, wts, other_wts, tree_order, skel_order, interp, pts, *every),
        [
            pltpu.VMEM((2 * cols * (leaves * size // 256), 256), BF),
            pltpu.VMEM((cols, leaves * size), BF),
            pltpu.VMEM((1, leaves * size), jnp.int32),
            pltpu.VMEM((leaves, size), jnp.int32),
            pltpu.VMEM((mine, rank, size - rank), BF),
            pltpu.VMEM((mine, dim, size), BF),
            pltpu.SemaphoreType.DMA((3 + 2 * mine,)),
        ],
        flops=3 * mega,
        grant=60,
    )
    outgoing = {by: mid_m for by in range(1, blocks)} | {1: up_m, blocks - 1: down_m}
    pieces = [lax.ppermute(outgoing[by], "leaf", ring(blocks, by)) for by in range(1, blocks)]
    near, tgt, edge_src = call(
        functools.partial(near_body, halo, scale),
        [((leaves, 2 * cols, size), F32), ((leaves, wide, size), BF), ((2 * halo, size, wide), BF)],
        [SMEM, SMEM, VMEM, VMEM, VMEM, VMEM],
        (ids, cnt, pts, tree_w, first_p, second_p),
        [pltpu.VMEM((mine, size, wide), BF), pltpu.SMEM((mine + 1,), jnp.int32)],
        flops=14 * mega,
    )
    near_own, near_other, far_tgt = call(
        functools.partial(edge_body, halo, mine, scale),
        [((cols, leaves * size), F32), ((cols, leaves * size), BF), ((leaves, wide, rank), BF)],
        [SMEM] + [VMEM] * 7,
        (cnt, near, tgt, edge_src, pieces[0], pieces[-1], pts, skel_order),
        [
            pltpu.VMEM((2 * halo, 2 * cols, size), BF),
            pltpu.SMEM((halo + 1,), jnp.int32),
        ],
        flops=6 * mega,
    )
    (near_back,) = from_others(near_other, "rhs")
    near_sum_own = (near_own + near_back.astype(F32)).astype(BF)
    near_parts = over_pair(near_sum_own, pair_n)
    piece_n = (blocks - 1) * mine
    far_src, far_w, names = call(
        functools.partial(sources_body, mine),
        [((piece_n, rank, wide), BF), ((piece_n, 2 * cols, rank), BF), ((leaves * pair_n * far_n + 16,), jnp.int32)],
        [SMEM] + [VMEM] * (blocks - 1),
        (far_ids, *pieces),
        out_specs=[VMEM, VMEM, SMEM],
        flops=2 * mega,
    )
    far_own, far_other = call(
        functools.partial(far_body, scale),
        [((cols, leaves * rank), F32), ((cols, leaves * rank), BF)],
        [SMEM, VMEM, VMEM, VMEM, pl.BlockSpec(memory_space=pl.ANY)],
        (names, far_src, far_w, far_tgt, near_sum_own),
        [pltpu.VMEM((leaves + 1, 2 * cols, rank), F32)],
        flops=4 * mega,
    )
    (far_back,) = from_others(far_other, "rhs")
    (far_sum_own,) = call(
        sum_body,
        [((cols, leaves * rank), BF)],
        [VMEM, VMEM] + [pl.BlockSpec(memory_space=pl.ANY)] * (pair_n - 1),
        (far_own, far_back, *near_parts[1:]),
    )
    far_parts = over_pair(far_sum_own, pair_n)
    acc_shape = (leaves * size // 256 * cols, 256)
    acc, comp = call(
        place_near_body,
        [(acc_shape, F32), ((1, leaves * size), jnp.int32)],
        [VMEM] * (2 + pair_n),
        (tree_order, skel_order, *near_parts),
        flops=5 * mega,
    )
    (out,) = call(
        place_far_body,
        [((cols, leaves * size), F32)],
        [VMEM] * (3 + pair_n),
        (comp, interp, acc, *far_parts),
        [pltpu.VMEM(acc_shape, F32), pltpu.VMEM((cols, leaves * size), F32)],
        flops=4 * mega,
    )
    return out.T


def solution(mesh):
    return jax.shard_map(
        on_device,
        mesh=mesh,
        in_specs=(
            P(("groups", "leaf"), None, None),
            P(("groups", "leaf"), "rhs"),
            P(("groups", "leaf"), None, None),
            P(("groups", "leaf"), None),
            P(("groups", "leaf"), None),
            P(("groups", "leaf"), "pair"),
            P(("groups", "leaf"), "pair"),
        ),
        out_specs=P(("groups", "leaf"), "rhs"),
        check_vma=False,
    )
```

```python
import functools

import jax
import jax.numpy as jnp
from jax import lax
from jax.experimental import pallas as pl
from jax.experimental.pallas import tpu as pltpu
from jax.sharding import PartitionSpec as P

BF = jnp.bfloat16
F32 = jnp.float32
LOG2E = 1.4426950408889634
EXTRA = 16
GROUP = 8
VMEM = pl.BlockSpec(memory_space=pltpu.VMEM)
SMEM = pl.BlockSpec(memory_space=pltpu.SMEM)


def call(body, shapes, specs, args, scratch=(), flops=0, out_specs=None, grant=48):
    outs = [jax.ShapeDtypeStruct(s, d) for s, d in shapes]
    return pl.pallas_call(
        body,
        out_shape=outs,
        in_specs=specs,
        out_specs=out_specs or [VMEM] * len(outs),
        scratch_shapes=list(scratch),
        compiler_params=pltpu.CompilerParams(vmem_limit_bytes=grant << 20),
        cost_estimate=pl.CostEstimate(flops=flops, bytes_accessed=1 << 20, transcendentals=0),
    )(*args)


def extra_rows(feat, ones_first):
    wide = feat.astype(F32)
    half = -0.5 * jnp.sum(wide * wide, axis=0, keepdims=True)
    high = half.astype(BF).astype(F32)
    mid = (half - high).astype(BF).astype(F32)
    low = half - high - mid
    row = lax.broadcasted_iota(jnp.int32, (EXTRA, feat.shape[1]), 0)
    at = 3 if ones_first else 0
    ones = (row < 3) if ones_first else (row >= 3) & (row < 6)
    picked = jnp.where(row == at, high, jnp.where(row == at + 1, mid, jnp.where(row == at + 2, low, 0.0)))
    return jnp.where(ones, 1.0, picked).astype(BF)


def as_targets(feat):
    return jnp.concatenate([feat, extra_rows(feat, False)], axis=0)


def as_sources(feat):
    return jnp.concatenate([feat, extra_rows(feat, True)], axis=0).astype(F32).T.astype(BF)


def one_hot(row_ids, count):
    rows = lax.broadcasted_iota(jnp.int32, (count, row_ids.shape[1]), 0)
    return jnp.where(rows == row_ids, 1.0, 0.0).astype(BF)


def dot(a, b):
    return jnp.dot(a, b, preferred_element_type=F32)


def dot_last(a, b):
    return lax.dot_general(a, b, (((1,), (1,)), ((), ())), preferred_element_type=F32)


def gauss(sources, targets, scale):
    return jnp.exp2(dot(sources, targets) * scale).astype(BF)


def class_of():
    return lax.axis_index("pair") * lax.axis_size("rhs") + lax.axis_index("rhs")


def halo_body(classes, pts_ref, near_ref, far_ref, up_ref, down_ref, pairs_ref, near_buf, far_buf, sems):
    halo = up_ref.shape[0]
    half = pts_ref.shape[0] // 2
    copies = [
        pltpu.make_async_copy(near_ref, near_buf, sems.at[2 * halo]),
        pltpu.make_async_copy(far_ref, far_buf, sems.at[2 * halo + 1]),
    ]
    for j in range(halo):
        leaf = class_of() + j * classes
        copies.append(pltpu.make_async_copy(pts_ref.at[leaf + half], up_ref.at[j], sems.at[j]))
        copies.append(pltpu.make_async_copy(pts_ref.at[leaf], down_ref.at[j], sems.at[halo + j]))
    for copy in copies:
        copy.start()
    for copy in copies:
        copy.wait()
    near_n = near_ref.shape[0]
    pairs_ref[:near_n] = near_buf[...]
    pairs_ref[near_n:] = far_buf[...]


def weights_body(
    blocks, classes, near_n, span, own_ref, other_ref, order_ref, skel_ref, interp_ref, pts_ref, *refs
):
    pair_refs = refs[:-13]
    tw_ref, up_ref, mid_ref, down_ref, cnt_ref, far_ref = refs[-13:-7]
    stack, own_buf, order_buf, skel_buf, interp_buf, pts_buf, sems = refs[-7:]
    cols = own_ref.shape[0]
    step = 2 * cols
    width = stack.shape[1]
    turns = own_ref.shape[1] // width
    mine, _, size = tw_ref.shape
    rank = mid_ref.shape[1]
    dim = pts_ref.shape[1]
    tall = dim + step
    cuts = size // rank
    halo = (up_ref.shape[0] - mid_ref.shape[0]) // (cuts * step)
    leaves = pts_ref.shape[0]
    block, me = lax.axis_index("leaf"), class_of()
    base = block * leaves - span
    copies = [
        pltpu.make_async_copy(own_ref, own_buf, sems.at[0]),
        pltpu.make_async_copy(order_ref, order_buf, sems.at[1]),
        pltpu.make_async_copy(skel_ref, skel_buf, sems.at[2]),
    ]
    for j in range(mine):
        leaf = j * classes + me
        copies.append(pltpu.make_async_copy(interp_ref.at[leaf], interp_buf.at[j], sems.at[3 + 2 * j]))
        copies.append(pltpu.make_async_copy(pts_ref.at[leaf], pts_buf.at[j], sems.at[4 + 2 * j]))
    for copy in copies:
        copy.start()
    for e in range(cnt_ref.shape[0]):
        wanted = base + e * classes + me
        total = None
        for ref in pair_refs:
            part = jnp.sum(jnp.where(ref[:near_n] == wanted, 1, 0), axis=0, keepdims=True)
            total = part if total is None else total + part
        cnt_ref[e : e + 1] = total
    far_n = far_ref.shape[0] // len(pair_refs)
    for k, ref in enumerate(pair_refs):
        named = ref[near_n:]
        owner = lax.div(named, leaves)
        within = lax.rem(named, leaves)
        piece = lax.rem(block - owner + blocks, blocks) - 1
        target = lax.broadcasted_iota(jnp.int32, named.shape, 1)
        code = target * 256 + piece * mine + lax.div(within, classes)
        far_ref[k * far_n : (k + 1) * far_n] = jnp.where(lax.rem(within, classes) == me, code, -1)

    copies[0].wait()
    copies[1].wait()
    for hi in range(turns):
        span = slice(hi * width, (hi + 1) * width)
        stack[hi * step : hi * step + cols] = own_buf[:, span]
        stack[hi * step + cols : (hi + 1) * step] = other_ref[:, span]
    for j in range(mine):
        leaf = j * classes + me
        ids = order_buf[:, pl.ds(pl.multiple_of(leaf * size, size), size)]
        hi_ids = lax.shift_right_logical(ids, width.bit_length() - 1)
        picked = dot(stack[...], one_hot(ids & (width - 1), width))
        total = jnp.zeros((step, size), F32)
        for hi in range(turns):
            total = total + jnp.where(hi_ids == hi, picked[hi * step : (hi + 1) * step], 0.0)
        tree = total.astype(BF)
        tw_ref[j] = tree
        for ref, place in ((down_ref, j), (up_ref, j - (mine - halo))):
            if 0 <= place < halo:
                for cut in range(cuts):
                    at = mine * tall + (place * cuts + cut) * step
                    ref[at : at + step] = tree[:, cut * rank : (cut + 1) * rank]
        if j == 0:
            for copy in copies[2:]:
                copy.wait()
        hot = one_hot(skel_buf[pl.ds(leaf, 1), :], size)
        ordered = dot(tree, hot)
        combined = dot_last(ordered[:, rank:].astype(BF), interp_buf[j])
        skel_p = dot(pts_buf[j], hot[:, :rank]).astype(BF)
        skel_w = (ordered[:, :rank] + combined).astype(BF)
        for ref in (up_ref, mid_ref, down_ref):
            ref[j * tall : j * tall + dim] = skel_p
            ref[j * tall + dim : (j + 1) * tall] = skel_w


def list_named(t, first, count, cnt_ref, slots, at):
    found = jnp.int32(0)
    for e in range(count):
        slots[at + found] = jnp.int32(e)
        found = found + jnp.where(cnt_ref[first + e, t] > 0, 1, 0)
    return found


def named_sum(t, k, first, scale, cnt_ref, slots, at, tgt, src, weights, shift):
    if k == 0:
        return jnp.zeros((weights.shape[1], tgt.shape[2]), F32)
    names = [slots[at + j] for j in range(k)]
    size = src.shape[1]
    block = gauss(jnp.concatenate([src[s + shift] for s in names], axis=0), tgt[t], scale)
    total = None
    for j, s in enumerate(names):
        times = cnt_ref[first + s, t].astype(F32)
        part = dot(weights[s + shift], block[j * size : (j + 1) * size]) * times
        total = part if total is None else total + part
    return total


def near_body(
    halo, scale, cnt_ref, pts_ref, tw_ref, left_p, right_p, skel_ref,
    near_ref, tgt_ref, edge_src, far_tgt_ref, src, slots,
):
    leaves, _, size = pts_ref.shape
    mine = tw_ref.shape[0]
    classes = leaves // mine
    rank = far_tgt_ref.shape[2]

    def sources(j, _):
        src[j] = as_sources(pts_ref[j * classes + class_of()])
        return 0

    lax.fori_loop(0, mine, sources, 0)
    tgt_ref[0] = as_targets(pts_ref[0])

    def target(t, _):
        found = list_named(t, halo, mine, cnt_ref, slots, 0)
        for k in range(mine + 1):

            @pl.when(found == k)
            def _():
                total = named_sum(t, k, halo, scale, cnt_ref, slots, 0, tgt_ref, src, tw_ref, 0)
                hot = one_hot(skel_ref[pl.ds(t, 1), :rank], size)
                far_tgt = as_targets(dot(pts_ref[t], hot).astype(BF))
                later = jnp.minimum(t + 1, leaves - 1)
                following = as_targets(pts_ref[later])
                near_ref[t] = total
                far_tgt_ref[t] = far_tgt
                tgt_ref[later] = following

        return 0

    lax.fori_loop(0, leaves, target, 0)
    for j in range(halo):
        edge_src[j] = as_sources(left_p[j])
        edge_src[halo + j] = as_sources(right_p[j])


def edge_body(
    halo, mine, rank, scale, cnt_ref, near_ref, tgt_ref, src, left_m, right_m, own_ref, other_ref, wts, slots
):
    leaves, cols2, size = near_ref.shape
    cols = cols2 // 2
    quarter = leaves // 4
    cuts = size // rank
    for side, message in enumerate((left_m, right_m)):
        for j in range(halo):
            for cut in range(cuts):
                at = message.shape[0] - (halo * cuts - j * cuts - cut) * cols2
                wts[side * halo + j, :, cut * rank : (cut + 1) * rank] = message[at : at + cols2]

    def targets(i, _):
        right = lax.div(i, quarter)
        first = right * (halo + mine)
        pair = (right * quarter + i, right * quarter + i + quarter)
        founds = [list_named(t, first, halo, cnt_ref, slots, n * (halo + 1)) for n, t in enumerate(pair)]
        for k in range((halo + 1) ** 2):
            counts = divmod(k, halo + 1)

            @pl.when((founds[0] == counts[0]) & (founds[1] == counts[1]))
            def _():
                sums = [
                    named_sum(t, c, first, scale, cnt_ref, slots, n * (halo + 1), tgt_ref, src, wts, right * halo)
                    for n, (t, c) in enumerate(zip(pair, counts))
                ]
                totals = [near_ref[t] + part for t, part in zip(pair, sums)]
                for t, total in zip(pair, totals):
                    span = pl.ds(pl.multiple_of(t * size, size), size)
                    own_ref[:, span] = total[:cols]
                    other_ref[:, span] = total[cols:].astype(BF)

        return 0

    lax.fori_loop(0, 2 * quarter, targets, 0)


def sources_body(mine, far_ref, *refs):
    pieces = refs[:-3]
    far_src, far_w, names = refs[-3:]
    cols2 = far_w.shape[1]
    dim = far_src.shape[2] - EXTRA
    tall = dim + cols2
    for k, piece in enumerate(pieces):
        for j in range(mine):
            far_src[k * mine + j] = as_sources(piece[j * tall : j * tall + dim])
            far_w[k * mine + j] = piece[j * tall + dim : (j + 1) * tall]
    found = jnp.int32(0)
    for t in range(far_ref.shape[1]):
        for i in range(far_ref.shape[0]):
            code = far_ref[i, t]
            names[1 + found] = code
            found = found + jnp.where(code >= 0, 1, 0)
    names[0] = found
    for j in range(GROUP):
        names[1 + found + j] = jnp.int32(far_ref.shape[1] * 256)


def sum_body(own_ref, back_ref, *refs):
    refs[-1][...] = (own_ref[...] + back_ref[...].astype(F32)).astype(BF)


def far_body(scale, names, far_src, far_w, far_tgt, after_ref, own_ref, other_ref, field):
    leaves, _, rank = far_tgt.shape
    cols = own_ref.shape[0]
    field[...] = jnp.zeros_like(field)

    def far_group(g, _):
        codes = [names[1 + g * GROUP + j] for j in range(GROUP)]
        targets = [lax.shift_right_logical(c, 8) for c in codes]
        blocks = [gauss(far_src[c & 255], far_tgt[t & (leaves - 1)], scale) for c, t in zip(codes, targets)]
        parts = [dot(far_w[c & 255], block) for c, block in zip(codes, blocks)]
        for t, part in zip(targets, parts):
            field[t] += part
        return 0

    lax.fori_loop(0, lax.div(names[0] + GROUP - 1, GROUP), far_group, 0)
    for t in range(leaves):
        own_ref[:, t * rank : (t + 1) * rank] = field[t, :cols]
        other_ref[:, t * rank : (t + 1) * rank] = field[t, cols:].astype(BF)


def scatter(ids, value, width, turns):
    hi_ids = lax.shift_right_logical(ids, width.bit_length() - 1)
    masked = [jnp.where(hi_ids == hi, value, 0.0).astype(BF) for hi in range(turns)]
    return dot_last(jnp.concatenate(masked, axis=0), one_hot(ids & (width - 1), width))


def place_near_body(order_ref, skel_ref, *refs):
    near, acc, comp_ref = refs[:-2], refs[-2], refs[-1]
    total = order_ref.shape[1]
    width = acc.shape[1]
    chunk = 1024
    for at in range(0, total, chunk):
        span = slice(at, at + chunk)
        value = sum(ref[:, span].astype(F32) for ref in near)
        part = scatter(order_ref[:, span], value, width, total // width)
        acc[...] = part if at == 0 else acc[...] + part
    leaves, size = skel_ref.shape
    for t in range(leaves):
        span = slice(t * size, (t + 1) * size)
        ids = order_ref[:, span]
        row = lax.broadcasted_iota(jnp.int32, (16, size), 0)
        halves = jnp.where(row == 0, lax.shift_right_logical(ids, 8), jnp.where(row == 1, ids & 255, 0))
        moved = dot(halves.astype(F32).astype(BF), one_hot(skel_ref[t : t + 1], size))
        comp_ref[:, span] = (moved[:1] * 256.0 + moved[1:2]).astype(jnp.int32)


def place_far_body(comp_ref, interp_ref, start_ref, *refs):
    far, out_ref, acc, buf = refs[:-3], refs[-3], refs[-2], refs[-1]
    cols, total = out_ref.shape
    width = acc.shape[1]
    turns = total // width
    leaves, rank, _ = interp_ref.shape
    size = total // leaves
    for t in range(leaves):
        skel = sum(ref[:, t * rank : (t + 1) * rank].astype(F32) for ref in far).astype(BF)
        buf[:, t * size : t * size + rank] = skel.astype(F32)
        buf[:, t * size + rank : (t + 1) * size] = dot(skel, interp_ref[t])
    chunk = 1024
    for at in range(0, total, chunk):
        span = slice(at, at + chunk)
        part = scatter(comp_ref[:, span], buf[:, span], width, turns)
        acc[...] = (start_ref if at == 0 else acc)[...] + part
    for hi in range(turns):
        out_ref[:, hi * width : (hi + 1) * width] = acc[hi * cols : (hi + 1) * cols]


def pin(value):
    return pltpu.with_memory_space_constraint(value, pltpu.HBM)


def ring(count, by):
    return [(i, (i + by) % count) for i in range(count)]


def from_others(value, axis):
    count = lax.axis_size(axis)
    return [lax.ppermute(value, axis, ring(count, by)) for by in range(1, count)]


def over_pair(value, pair_n):
    if pair_n == 2:
        return [value] + from_others(value, "pair")
    return list(lax.all_gather(value, "pair"))


def on_device(points, weights, interp, tree_order, skel_order, near_pairs, far_pairs):
    leaves, size, dim = points.shape
    rank = interp.shape[1]
    cols = weights.shape[1]
    blocks, pair_n, rhs_n = (lax.axis_size(a) for a in ("leaf", "pair", "rhs"))
    classes = pair_n * rhs_n
    mine = leaves // classes
    span = min(8, leaves)
    halo = span // classes
    scale = 2.0 * 2.5 / dim * LOG2E
    near_n, far_n = near_pairs.shape[1], far_pairs.shape[1]
    wide = dim + EXTRA
    mega = 10 ** 9
    pts = points.transpose(0, 2, 1)
    wts = weights.T
    (other_wts,) = from_others(wts, "rhs")
    hbm = pl.BlockSpec(memory_space=pltpu.HBM)
    up_p, down_p, pairs = call(
        functools.partial(halo_body, classes),
        [((halo, dim, size), BF), ((halo, dim, size), BF), ((near_n + far_n, leaves), jnp.int32)],
        [hbm, hbm, hbm],
        (pin(pts), pin(near_pairs.T), pin(far_pairs.T)),
        [
            pltpu.VMEM((near_n, leaves), jnp.int32),
            pltpu.VMEM((far_n, leaves), jnp.int32),
            pltpu.SemaphoreType.DMA((2 * halo + 2,)),
        ],
        out_specs=[hbm, hbm, VMEM],
        grant=48,
    )
    every = [pairs] + from_others(pairs, "pair")
    left_p = lax.ppermute(up_p, "leaf", ring(blocks, 1))
    right_p = lax.ppermute(down_p, "leaf", ring(blocks, blocks - 1))
    tall = mine * (dim + 2 * cols)
    extra = halo * (size // rank) * 2 * cols
    tree_w, up_m, mid_m, down_m, cnt, far_ids = call(
        functools.partial(weights_body, blocks, classes, near_n, span),
        [
            ((mine, 2 * cols, size), BF),
            ((tall + extra, rank), BF),
            ((tall, rank), BF),
            ((tall + extra, rank), BF),
            ((2 * halo + mine, leaves), jnp.int32),
            ((pair_n * far_n, leaves), jnp.int32),
        ],
        [hbm, VMEM] + [hbm] * 4 + [VMEM] * pair_n,
        (pin(wts), other_wts, pin(tree_order), pin(skel_order), pin(interp), pin(pts), *every),
        [
            pltpu.VMEM((2 * cols * (leaves * size // 256), 256), BF),
            pltpu.VMEM((cols, leaves * size), BF),
            pltpu.VMEM((1, leaves * size), jnp.int32),
            pltpu.VMEM((leaves, size), jnp.int32),
            pltpu.VMEM((mine, rank, size - rank), BF),
            pltpu.VMEM((mine, dim, size), BF),
            pltpu.SemaphoreType.DMA((3 + 2 * mine,)),
        ],
        flops=3 * mega,
        grant=48,
    )
    outgoing = {by: mid_m for by in range(1, blocks)} | {1: up_m, blocks - 1: down_m}
    pieces = [lax.ppermute(outgoing[by], "leaf", ring(blocks, by)) for by in range(1, blocks)]
    near, tgt, edge_src, far_tgt = call(
        functools.partial(near_body, halo, scale),
        [
            ((leaves, 2 * cols, size), F32),
            ((leaves, wide, size), BF),
            ((2 * halo, size, wide), BF),
            ((leaves, wide, rank), BF),
        ],
        [SMEM] + [VMEM] * 5,
        (cnt, pts, tree_w, left_p, right_p, skel_order),
        [pltpu.VMEM((mine, size, wide), BF), pltpu.SMEM((mine + 1,), jnp.int32)],
        flops=14 * mega,
    )

    near_own, near_other = call(
        functools.partial(edge_body, halo, mine, rank, scale),
        [((cols, leaves * size), F32), ((cols, leaves * size), BF)],
        [SMEM] + [VMEM] * 5,
        (cnt, near, tgt, edge_src, pieces[0], pieces[-1]),
        [pltpu.VMEM((2 * halo, 2 * cols, size), BF), pltpu.SMEM((2 * halo + 2,), jnp.int32)],
        flops=6 * mega,
    )
    (near_back,) = from_others(near_other, "rhs")
    near_sum_own = (near_own + near_back.astype(F32)).astype(BF)
    near_parts = over_pair(near_sum_own, pair_n)
    piece_n = (blocks - 1) * mine
    far_src, far_w, names = call(
        functools.partial(sources_body, mine),
        [((piece_n, rank, wide), BF), ((piece_n, 2 * cols, rank), BF), ((leaves * pair_n * far_n + 16,), jnp.int32)],
        [SMEM] + [VMEM] * (blocks - 1),
        (far_ids, *pieces),
        out_specs=[VMEM, VMEM, SMEM],
        flops=2 * mega,
    )
    far_src, far_w, names = call(
        functools.partial(sources_body, mine),
        [((piece_n, rank, wide), BF), ((piece_n, 2 * cols, rank), BF), ((leaves * pair_n * far_n + 16,), jnp.int32)],
        [SMEM] + [VMEM] * (blocks - 1),
        (far_ids, *pieces),
        out_specs=[VMEM, VMEM, SMEM],
        flops=2 * mega,
    )
    far_own, far_other = call(
        functools.partial(far_body, scale),
        [((cols, leaves * rank), F32), ((cols, leaves * rank), BF)],
        [SMEM, VMEM, VMEM, VMEM, pl.BlockSpec(memory_space=pl.ANY)],
        (names, far_src, far_w, far_tgt, near_sum_own),
        [pltpu.VMEM((leaves + 1, 2 * cols, rank), F32)],
        flops=4 * mega,
    )
    (far_back,) = from_others(far_other, "rhs")
    (far_sum_own,) = call(
        sum_body,
        [((cols, leaves * rank), BF)],
        [VMEM, VMEM] + [pl.BlockSpec(memory_space=pl.ANY)] * (pair_n - 1),
        (far_own, far_back, *near_parts[1:]),
    )
    far_parts = over_pair(far_sum_own, pair_n)
    acc_shape = (leaves * size // 256 * cols, 256)
    acc, comp = call(
        place_near_body,
        [(acc_shape, F32), ((1, leaves * size), jnp.int32)],
        [VMEM] * (2 + pair_n),
        (tree_order, skel_order, *near_parts),
        flops=5 * mega,
    )
    (out,) = call(
        place_far_body,
        [((cols, leaves * size), F32)],
        [VMEM] * (3 + pair_n),
        (comp, interp, acc, *far_parts),
        [pltpu.VMEM(acc_shape, F32), pltpu.VMEM((cols, leaves * size), F32)],
        flops=4 * mega,
    )
    return out.T


def solution(mesh):
    return jax.shard_map(
        on_device,
        mesh=mesh,
        in_specs=(
            P(("groups", "leaf"), None, None),
            P(("groups", "leaf"), "rhs"),
            P(("groups", "leaf"), None, None),
            P(("groups", "leaf"), None),
            P(("groups", "leaf"), None),
            P(("groups", "leaf"), "pair"),
            P(("groups", "leaf"), "pair"),
        ),
        out_specs=P(("groups", "leaf"), "rhs"),
        check_vma=False,
    )
```

```python
import functools

import jax
import jax.numpy as jnp
from jax import lax
from jax.experimental import pallas as pl
from jax.experimental.pallas import tpu as pltpu
from jax.sharding import PartitionSpec as P

BF = jnp.bfloat16
F32 = jnp.float32
LOG2E = 1.4426950408889634
EXTRA = 16
GROUP = 8
VMEM = pl.BlockSpec(memory_space=pltpu.VMEM)
SMEM = pl.BlockSpec(memory_space=pltpu.SMEM)


def call(body, shapes, specs, args, scratch=(), flops=0, out_specs=None, grant=48):
    outs = [jax.ShapeDtypeStruct(s, d) for s, d in shapes]
    return pl.pallas_call(
        body,
        out_shape=outs,
        in_specs=specs,
        out_specs=out_specs or [VMEM] * len(outs),
        scratch_shapes=list(scratch),
        compiler_params=pltpu.CompilerParams(vmem_limit_bytes=grant << 20),
        cost_estimate=pl.CostEstimate(flops=flops, bytes_accessed=1 << 20, transcendentals=0),
    )(*args)


def extra_rows(feat, ones_first):
    wide = feat.astype(F32)
    half = -0.5 * jnp.sum(wide * wide, axis=0, keepdims=True)
    high = half.astype(BF).astype(F32)
    mid = (half - high).astype(BF).astype(F32)
    low = half - high - mid
    row = lax.broadcasted_iota(jnp.int32, (EXTRA, feat.shape[1]), 0)
    at = 3 if ones_first else 0
    ones = (row < 3) if ones_first else (row >= 3) & (row < 6)
    picked = jnp.where(row == at, high, jnp.where(row == at + 1, mid, jnp.where(row == at + 2, low, 0.0)))
    return jnp.where(ones, 1.0, picked).astype(BF)


def as_targets(feat):
    return jnp.concatenate([feat, extra_rows(feat, False)], axis=0)


def as_sources(feat):
    return jnp.concatenate([feat, extra_rows(feat, True)], axis=0).astype(F32).T.astype(BF)


def one_hot(row_ids, count):
    rows = lax.broadcasted_iota(jnp.int32, (count, row_ids.shape[1]), 0)
    return jnp.where(rows == row_ids, 1.0, 0.0).astype(BF)


def dot(a, b):
    return jnp.dot(a, b, preferred_element_type=F32)


def dot_last(a, b):
    return lax.dot_general(a, b, (((1,), (1,)), ((), ())), preferred_element_type=F32)


def gauss(sources, targets, scale):
    return jnp.exp2(dot(sources, targets) * scale).astype(BF)


def class_of():
    return lax.axis_index("pair") * lax.axis_size("rhs") + lax.axis_index("rhs")


def halo_body(classes, pts_ref, near_ref, far_ref, up_ref, down_ref, pairs_ref, near_buf, far_buf, sems):
    halo = up_ref.shape[0]
    half = pts_ref.shape[0] // 2
    copies = [
        pltpu.make_async_copy(near_ref, near_buf, sems.at[2 * halo]),
        pltpu.make_async_copy(far_ref, far_buf, sems.at[2 * halo + 1]),
    ]
    for j in range(halo):
        leaf = class_of() + j * classes
        copies.append(pltpu.make_async_copy(pts_ref.at[leaf + half], up_ref.at[j], sems.at[j]))
        copies.append(pltpu.make_async_copy(pts_ref.at[leaf], down_ref.at[j], sems.at[halo + j]))
    for copy in copies:
        copy.start()
    for copy in copies:
        copy.wait()
    near_n = near_ref.shape[0]
    pairs_ref[:near_n] = near_buf[...]
    pairs_ref[near_n:] = far_buf[...]


def weights_body(
    blocks, classes, near_n, span, halo, own_ref, other_ref, order_ref, skel_ref, interp_ref, pts_ref, *refs
):
    pair_refs = refs[:-13]
    tw_ref, up_ref, mid_ref, down_ref, cnt_ref, far_ref = refs[-13:-7]
    stack, own_buf, order_buf, skel_buf, interp_buf, pts_buf, sems = refs[-7:]
    cols = own_ref.shape[0]
    step = 2 * cols
    width = stack.shape[1]
    turns = own_ref.shape[1] // width
    mine, _, size = tw_ref.shape
    rank = mid_ref.shape[1]
    dim = pts_ref.shape[1]
    cuts = size // rank
    leaves = pts_ref.shape[0]
    block, me = lax.axis_index("leaf"), class_of()
    base = block * leaves - span
    copies = [
        pltpu.make_async_copy(own_ref, own_buf, sems.at[0]),
        pltpu.make_async_copy(order_ref, order_buf, sems.at[1]),
        pltpu.make_async_copy(skel_ref, skel_buf, sems.at[2]),
    ]
    for j in range(mine):
        leaf = j * classes + me
        copies.append(pltpu.make_async_copy(interp_ref.at[leaf], interp_buf.at[j], sems.at[3 + 2 * j]))
        copies.append(pltpu.make_async_copy(pts_ref.at[leaf], pts_buf.at[j], sems.at[4 + 2 * j]))
    for copy in copies:
        copy.start()
    for e in range(cnt_ref.shape[0]):
        wanted = base + e * classes + me
        total = None
        for ref in pair_refs:
            part = jnp.sum(jnp.where(ref[:near_n] == wanted, 1, 0), axis=0, keepdims=True)
            total = part if total is None else total + part
        cnt_ref[e : e + 1] = total
    far_n = far_ref.shape[0] // len(pair_refs)
    for k, ref in enumerate(pair_refs):
        named = ref[near_n:]
        owner = lax.div(named, leaves)
        within = lax.rem(named, leaves)
        piece = lax.rem(block - owner + blocks, blocks) - 1
        target = lax.broadcasted_iota(jnp.int32, named.shape, 1)
        code = target * 256 + piece * mine + lax.div(within, classes)
        far_ref[k * far_n : (k + 1) * far_n] = jnp.where(lax.rem(within, classes) == me, code, -1)

    copies[0].wait()
    copies[1].wait()
    for hi in range(turns):
        span = slice(hi * width, (hi + 1) * width)
        stack[hi * step : hi * step + cols] = own_buf[:, span]
        stack[hi * step + cols : (hi + 1) * step] = other_ref[:, span]
    orders = {}
    for j in range(mine):
        leaf = j * classes + me
        ids = order_buf[:, pl.ds(pl.multiple_of(leaf * size, size), size)]
        hi_ids = lax.shift_right_logical(ids, width.bit_length() - 1)
        picked = dot(stack[...], one_hot(ids & (width - 1), width))
        total = jnp.zeros((step, size), F32)
        for hi in range(turns):
            total = total + jnp.where(hi_ids == hi, picked[hi * step : (hi + 1) * step], 0.0)
        tree = total.astype(BF)
        tw_ref[j] = tree
        if j == 0:
            for copy in copies[2:]:
                copy.wait()
        hot = one_hot(skel_buf[pl.ds(leaf, 1), :], size)
        ordered = dot(tree, hot)
        combined = dot_last(ordered[:, rank:].astype(BF), interp_buf[j])
        skel_p = dot(pts_buf[j], hot[:, :rank]).astype(BF)
        skel_w = (ordered[:, :rank] + combined).astype(BF)
        for ref, low, high in ((up_ref, 0, mine - halo), (mid_ref, 0, mine), (down_ref, halo, mine)):
            weights_at, halo_at = (high - low) * dim, (high - low) * dim + mine * step
            if low <= j < high:
                ref[(j - low) * dim : (j - low + 1) * dim] = skel_p
            elif ref is not mid_ref:
                place = j - (mine - halo) if low == 0 else j
                for cut in range(cuts):
                    at = halo_at + (place * cuts + cut) * step
                    ref[at : at + step] = tree[:, cut * rank : (cut + 1) * rank]
                row = lax.broadcasted_iota(jnp.int32, (EXTRA, rank), 0)
                picks = skel_buf[pl.ds(leaf, 1), :rank]
                high_half = jnp.where(row == 2 * place, lax.shift_right_logical(picks, 8), 0)
                halves = jnp.where(row == 2 * place + 1, picks & 255, high_half).astype(F32)
                before = orders.get(id(ref))
                orders[id(ref)] = halves if before is None else before + halves
                ref[halo_at + halo * cuts * step :] = orders[id(ref)].astype(BF)
            ref[weights_at + j * step : weights_at + (j + 1) * step] = skel_w


def list_named(t, first, count, cnt_ref, slots, at):
    found = jnp.int32(0)
    for e in range(count):
        slots[at + found] = jnp.int32(e)
        found = found + jnp.where(cnt_ref[first + e, t] > 0, 1, 0)
    return found


def named_sum(t, k, first, scale, cnt_ref, slots, at, tgt, src, weights, shift):
    if k == 0:
        return jnp.zeros((weights.shape[1], tgt.shape[2]), F32)
    names = [slots[at + j] for j in range(k)]
    size = src.shape[1]
    block = gauss(jnp.concatenate([src[s + shift] for s in names], axis=0), tgt[t], scale)
    total = None
    for j, s in enumerate(names):
        times = cnt_ref[first + s, t].astype(F32)
        part = dot(weights[s + shift], block[j * size : (j + 1) * size]) * times
        total = part if total is None else total + part
    return total


def near_body(
    halo, scale, cnt_ref, pts_ref, tw_ref, left_p, right_p, skel_ref,
    near_ref, tgt_ref, edge_src, far_tgt_ref, src, slots,
):
    leaves, _, size = pts_ref.shape
    mine = tw_ref.shape[0]
    classes = leaves // mine
    rank = far_tgt_ref.shape[2]

    def sources(j, _):
        src[j] = as_sources(pts_ref[j * classes + class_of()])
        return 0

    lax.fori_loop(0, mine, sources, 0)
    tgt_ref[0] = as_targets(pts_ref[0])

    def target(t, _):
        found = list_named(t, halo, mine, cnt_ref, slots, 0)
        for k in range(mine + 1):

            @pl.when(found == k)
            def _():
                total = named_sum(t, k, halo, scale, cnt_ref, slots, 0, tgt_ref, src, tw_ref, 0)
                hot = one_hot(skel_ref[pl.ds(t, 1), :rank], size)
                far_tgt = as_targets(dot(pts_ref[t], hot).astype(BF))
                later = jnp.minimum(t + 1, leaves - 1)
                following = as_targets(pts_ref[later])
                near_ref[t] = total
                far_tgt_ref[t] = far_tgt
                tgt_ref[later] = following

        return 0

    lax.fori_loop(0, leaves, target, 0)
    for j in range(halo):
        edge_src[j] = as_sources(left_p[j])
        edge_src[halo + j] = as_sources(right_p[j])


def edge_body(
    halo, mine, rank, scale, cnt_ref, near_ref, tgt_ref, src, left_m, right_m, own_ref, other_ref, wts, slots
):
    leaves, cols2, size = near_ref.shape
    cols = cols2 // 2
    quarter = leaves // 4
    cuts = size // rank
    for side, message in enumerate((left_m, right_m)):
        for j in range(halo):
            for cut in range(cuts):
                at = message.shape[0] - EXTRA - (halo * cuts - j * cuts - cut) * cols2
                wts[side * halo + j, :, cut * rank : (cut + 1) * rank] = message[at : at + cols2]

    def targets(i, _):
        right = lax.div(i, quarter)
        first = right * (halo + mine)
        pair = (right * quarter + i, right * quarter + i + quarter)
        founds = [list_named(t, first, halo, cnt_ref, slots, n * (halo + 1)) for n, t in enumerate(pair)]
        for k in range((halo + 1) ** 2):
            counts = divmod(k, halo + 1)

            @pl.when((founds[0] == counts[0]) & (founds[1] == counts[1]))
            def _():
                sums = [
                    named_sum(t, c, first, scale, cnt_ref, slots, n * (halo + 1), tgt_ref, src, wts, right * halo)
                    for n, (t, c) in enumerate(zip(pair, counts))
                ]
                totals = [near_ref[t] + part for t, part in zip(pair, sums)]
                for t, total in zip(pair, totals):
                    span = pl.ds(pl.multiple_of(t * size, size), size)
                    own_ref[:, span] = total[:cols]
                    other_ref[:, span] = total[cols:].astype(BF)

        return 0

    lax.fori_loop(0, 2 * quarter, targets, 0)


def sources_body(mine, far_ref, left_p, right_p, *refs):
    pieces = refs[:-3]
    far_src, far_w, names = refs[-3:]
    halo, dim, size = left_p.shape
    _, cols2, rank = far_w.shape
    for k, piece in enumerate(pieces):
        low, high, points = 0, mine, None
        if k == 0:
            high, points = mine - halo, left_p
        elif k == len(pieces) - 1:
            low, points = halo, right_p
        weights_at = (high - low) * dim
        for j in range(mine):
            if low <= j < high:
                skel_p = piece[(j - low) * dim : (j - low + 1) * dim]
            else:
                place = j - (mine - halo) if k == 0 else j
                order = piece[piece.shape[0] - EXTRA :].astype(F32)
                picks = (order[2 * place : 2 * place + 1] * 256.0 + order[2 * place + 1 : 2 * place + 2]).astype(jnp.int32)
                skel_p = dot(points[place], one_hot(picks, size)).astype(BF)
            far_src[k * mine + j] = as_sources(skel_p)
            far_w[k * mine + j] = piece[weights_at + j * cols2 : weights_at + (j + 1) * cols2]
    found = jnp.int32(0)
    for t in range(far_ref.shape[1]):
        for i in range(far_ref.shape[0]):
            code = far_ref[i, t]
            names[1 + found] = code
            found = found + jnp.where(code >= 0, 1, 0)
    names[0] = found
    for j in range(GROUP):
        names[1 + found + j] = jnp.int32(far_ref.shape[1] * 256)


def sum_body(own_ref, back_ref, *refs):
    refs[-1][...] = (own_ref[...] + back_ref[...].astype(F32)).astype(BF)


def far_body(scale, names, far_src, far_w, far_tgt, after_ref, own_ref, other_ref, field):
    leaves, _, rank = far_tgt.shape
    cols = own_ref.shape[0]
    field[...] = jnp.zeros_like(field)

    def far_group(g, _):
        codes = [names[1 + g * GROUP + j] for j in range(GROUP)]
        targets = [lax.shift_right_logical(c, 8) for c in codes]
        blocks = [gauss(far_src[c & 255], far_tgt[t & (leaves - 1)], scale) for c, t in zip(codes, targets)]
        parts = [dot(far_w[c & 255], block) for c, block in zip(codes, blocks)]
        for t, part in zip(targets, parts):
            field[t] += part
        return 0

    lax.fori_loop(0, lax.div(names[0] + GROUP - 1, GROUP), far_group, 0)
    for t in range(leaves):
        own_ref[:, t * rank : (t + 1) * rank] = field[t, :cols]
        other_ref[:, t * rank : (t + 1) * rank] = field[t, cols:].astype(BF)


def scatter(ids, value, width, turns):
    hi_ids = lax.shift_right_logical(ids, width.bit_length() - 1)
    masked = [jnp.where(hi_ids == hi, value, 0.0).astype(BF) for hi in range(turns)]
    return dot_last(jnp.concatenate(masked, axis=0), one_hot(ids & (width - 1), width))


def place_near_body(order_ref, skel_ref, *refs):
    near, acc, comp_ref = refs[:-2], refs[-2], refs[-1]
    total = order_ref.shape[1]
    width = acc.shape[1]
    chunk = 1024
    for at in range(0, total, chunk):
        span = slice(at, at + chunk)
        value = sum(ref[:, span].astype(F32) for ref in near)
        part = scatter(order_ref[:, span], value, width, total // width)
        acc[...] = part if at == 0 else acc[...] + part
    leaves, size = skel_ref.shape
    for t in range(leaves):
        span = slice(t * size, (t + 1) * size)
        ids = order_ref[:, span]
        row = lax.broadcasted_iota(jnp.int32, (16, size), 0)
        halves = jnp.where(row == 0, lax.shift_right_logical(ids, 8), jnp.where(row == 1, ids & 255, 0))
        moved = dot(halves.astype(F32).astype(BF), one_hot(skel_ref[t : t + 1], size))
        comp_ref[:, span] = (moved[:1] * 256.0 + moved[1:2]).astype(jnp.int32)


def place_far_body(comp_ref, interp_ref, start_ref, *refs):
    far, out_ref, acc, buf = refs[:-3], refs[-3], refs[-2], refs[-1]
    cols, total = out_ref.shape
    width = acc.shape[1]
    turns = total // width
    leaves, rank, _ = interp_ref.shape
    size = total // leaves
    for t in range(leaves):
        skel = sum(ref[:, t * rank : (t + 1) * rank].astype(F32) for ref in far).astype(BF)
        buf[:, t * size : t * size + rank] = skel.astype(F32)
        buf[:, t * size + rank : (t + 1) * size] = dot(skel, interp_ref[t])
    chunk = 1024
    for at in range(0, total, chunk):
        span = slice(at, at + chunk)
        part = scatter(comp_ref[:, span], buf[:, span], width, turns)
        acc[...] = (start_ref if at == 0 else acc)[...] + part
    for hi in range(turns):
        out_ref[:, hi * width : (hi + 1) * width] = acc[hi * cols : (hi + 1) * cols]


def pin(value):
    return pltpu.with_memory_space_constraint(value, pltpu.HBM)


def ring(count, by):
    return [(i, (i + by) % count) for i in range(count)]


def from_others(value, axis):
    count = lax.axis_size(axis)
    return [lax.ppermute(value, axis, ring(count, by)) for by in range(1, count)]


def over_pair(value, pair_n):
    if pair_n == 2:
        return [value] + from_others(value, "pair")
    return list(lax.all_gather(value, "pair"))


def on_device(points, weights, interp, tree_order, skel_order, near_pairs, far_pairs):
    leaves, size, dim = points.shape
    rank = interp.shape[1]
    cols = weights.shape[1]
    blocks, pair_n, rhs_n = (lax.axis_size(a) for a in ("leaf", "pair", "rhs"))
    classes = pair_n * rhs_n
    mine = leaves // classes
    span = min(8, leaves)
    halo = span // classes
    scale = 2.0 * 2.5 / dim * LOG2E
    near_n, far_n = near_pairs.shape[1], far_pairs.shape[1]
    wide = dim + EXTRA
    mega = 10 ** 9
    pts = points.transpose(0, 2, 1)
    wts = weights.T
    (other_wts,) = from_others(wts, "rhs")
    hbm = pl.BlockSpec(memory_space=pltpu.HBM)
    up_p, down_p, pairs = call(
        functools.partial(halo_body, classes),
        [((halo, dim, size), BF), ((halo, dim, size), BF), ((near_n + far_n, leaves), jnp.int32)],
        [hbm, hbm, hbm],
        (pin(pts), pin(near_pairs.T), pin(far_pairs.T)),
        [
            pltpu.VMEM((near_n, leaves), jnp.int32),
            pltpu.VMEM((far_n, leaves), jnp.int32),
            pltpu.SemaphoreType.DMA((2 * halo + 2,)),
        ],
        out_specs=[hbm, hbm, VMEM],
        grant=48,
    )
    every = [pairs] + from_others(pairs, "pair")
    left_p = lax.ppermute(up_p, "leaf", ring(blocks, 1))
    right_p = lax.ppermute(down_p, "leaf", ring(blocks, blocks - 1))
    tall = mine * (dim + 2 * cols)
    ends = tall - halo * dim + halo * (size // rank) * 2 * cols + EXTRA
    tree_w, up_m, mid_m, down_m, cnt, far_ids = call(
        functools.partial(weights_body, blocks, classes, near_n, span, halo),
        [
            ((mine, 2 * cols, size), BF),
            ((ends, rank), BF),
            ((tall, rank), BF),
            ((ends, rank), BF),
            ((2 * halo + mine, leaves), jnp.int32),
            ((pair_n * far_n, leaves), jnp.int32),
        ],
        [hbm, VMEM] + [hbm] * 4 + [VMEM] * pair_n,
        (pin(wts), other_wts, pin(tree_order), pin(skel_order), pin(interp), pin(pts), *every),
        [
            pltpu.VMEM((2 * cols * (leaves * size // 256), 256), BF),
            pltpu.VMEM((cols, leaves * size), BF),
            pltpu.VMEM((1, leaves * size), jnp.int32),
            pltpu.VMEM((leaves, size), jnp.int32),
            pltpu.VMEM((mine, rank, size - rank), BF),
            pltpu.VMEM((mine, dim, size), BF),
            pltpu.SemaphoreType.DMA((3 + 2 * mine,)),
        ],
        flops=3 * mega,
        grant=48,
    )
    outgoing = {by: mid_m for by in range(1, blocks)} | {1: up_m, blocks - 1: down_m}
    pieces = [lax.ppermute(outgoing[by], "leaf", ring(blocks, by)) for by in range(1, blocks)]
    near, tgt, edge_src, far_tgt = call(
        functools.partial(near_body, halo, scale),
        [
            ((leaves, 2 * cols, size), F32),
            ((leaves, wide, size), BF),
            ((2 * halo, size, wide), BF),
            ((leaves, wide, rank), BF),
        ],
        [SMEM] + [VMEM] * 5,
        (cnt, pts, tree_w, left_p, right_p, skel_order),
        [pltpu.VMEM((mine, size, wide), BF), pltpu.SMEM((mine + 1,), jnp.int32)],
        flops=14 * mega,
    )

    near_own, near_other = call(
        functools.partial(edge_body, halo, mine, rank, scale),
        [((cols, leaves * size), F32), ((cols, leaves * size), BF)],
        [SMEM] + [VMEM] * 5,
        (cnt, near, tgt, edge_src, pieces[0], pieces[-1]),
        [pltpu.VMEM((2 * halo, 2 * cols, size), BF), pltpu.SMEM((2 * halo + 2,), jnp.int32)],
        flops=6 * mega,
    )
    (near_back,) = from_others(near_other, "rhs")
    near_sum_own = (near_own + near_back.astype(F32)).astype(BF)
    near_parts = over_pair(near_sum_own, pair_n)
    piece_n = (blocks - 1) * mine
    far_src, far_w, names = call(
        functools.partial(sources_body, mine),
        [((piece_n, rank, wide), BF), ((piece_n, 2 * cols, rank), BF), ((leaves * pair_n * far_n + 16,), jnp.int32)],
        [SMEM] + [VMEM] * (blocks + 1),
        (far_ids, left_p, right_p, *pieces),
        out_specs=[VMEM, VMEM, SMEM],
        flops=2 * mega,
    )
    far_src, far_w, names = call(
        functools.partial(sources_body, mine),
        [((piece_n, rank, wide), BF), ((piece_n, 2 * cols, rank), BF), ((leaves * pair_n * far_n + 16,), jnp.int32)],
        [SMEM] + [VMEM] * (blocks + 1),
        (far_ids, left_p, right_p, *pieces),
        out_specs=[VMEM, VMEM, SMEM],
        flops=2 * mega,
    )
    far_own, far_other = call(
        functools.partial(far_body, scale),
        [((cols, leaves * rank), F32), ((cols, leaves * rank), BF)],
        [SMEM, VMEM, VMEM, VMEM, pl.BlockSpec(memory_space=pl.ANY)],
        (names, far_src, far_w, far_tgt, near_sum_own),
        [pltpu.VMEM((leaves + 1, 2 * cols, rank), F32)],
        flops=4 * mega,
    )
    (far_back,) = from_others(far_other, "rhs")
    (far_sum_own,) = call(
        sum_body,
        [((cols, leaves * rank), BF)],
        [VMEM, VMEM] + [pl.BlockSpec(memory_space=pl.ANY)] * (pair_n - 1),
        (far_own, far_back, *near_parts[1:]),
    )
    far_parts = over_pair(far_sum_own, pair_n)
    acc_shape = (leaves * size // 256 * cols, 256)
    acc, comp = call(
        place_near_body,
        [(acc_shape, F32), ((1, leaves * size), jnp.int32)],
        [VMEM] * (2 + pair_n),
        (tree_order, skel_order, *near_parts),
        flops=5 * mega,
    )
    (out,) = call(
        place_far_body,
        [((cols, leaves * size), F32)],
        [VMEM] * (3 + pair_n),
        (comp, interp, acc, *far_parts),
        [pltpu.VMEM(acc_shape, F32), pltpu.VMEM((cols, leaves * size), F32)],
        flops=4 * mega,
    )
    return out.T


def solution(mesh):
    return jax.shard_map(
        on_device,
        mesh=mesh,
        in_specs=(
            P(("groups", "leaf"), None, None),
            P(("groups", "leaf"), "rhs"),
            P(("groups", "leaf"), None, None),
            P(("groups", "leaf"), None),
            P(("groups", "leaf"), None),
            P(("groups", "leaf"), "pair"),
            P(("groups", "leaf"), "pair"),
        ),
        out_specs=P(("groups", "leaf"), "rhs"),
        check_vma=False,
    )
```

```python
import functools

import jax
import jax.numpy as jnp
from jax import lax
from jax.experimental import pallas as pl
from jax.experimental.pallas import tpu as pltpu
from jax.sharding import PartitionSpec as P

BF = jnp.bfloat16
F32 = jnp.float32
LOG2E = 1.4426950408889634
EXTRA = 16
GROUP = 8
VMEM = pl.BlockSpec(memory_space=pltpu.VMEM)
SMEM = pl.BlockSpec(memory_space=pltpu.SMEM)


def call(body, shapes, specs, args, scratch=(), flops=0, out_specs=None, grant=48):
    outs = [jax.ShapeDtypeStruct(s, d) for s, d in shapes]
    return pl.pallas_call(
        body,
        out_shape=outs,
        in_specs=specs,
        out_specs=out_specs or [VMEM] * len(outs),
        scratch_shapes=list(scratch),
        compiler_params=pltpu.CompilerParams(vmem_limit_bytes=grant << 20),
        cost_estimate=pl.CostEstimate(flops=flops, bytes_accessed=1 << 20, transcendentals=0),
    )(*args)


def extra_rows(feat, ones_first):
    wide = feat.astype(F32)
    half = -0.5 * jnp.sum(wide * wide, axis=0, keepdims=True)
    high = half.astype(BF).astype(F32)
    mid = (half - high).astype(BF).astype(F32)
    low = half - high - mid
    row = lax.broadcasted_iota(jnp.int32, (EXTRA, feat.shape[1]), 0)
    at = 3 if ones_first else 0
    ones = (row < 3) if ones_first else (row >= 3) & (row < 6)
    picked = jnp.where(row == at, high, jnp.where(row == at + 1, mid, jnp.where(row == at + 2, low, 0.0)))
    return jnp.where(ones, 1.0, picked).astype(BF)


def as_targets(feat):
    return jnp.concatenate([feat, extra_rows(feat, False)], axis=0)


def as_sources(feat):
    return jnp.concatenate([feat, extra_rows(feat, True)], axis=0).astype(F32).T.astype(BF)


def one_hot(row_ids, count):
    rows = lax.broadcasted_iota(jnp.int32, (count, row_ids.shape[1]), 0)
    return jnp.where(rows == row_ids, 1.0, 0.0).astype(BF)


def dot(a, b):
    return jnp.dot(a, b, preferred_element_type=F32)


def dot_last(a, b):
    return lax.dot_general(a, b, (((1,), (1,)), ((), ())), preferred_element_type=F32)


def gauss(sources, targets, scale):
    return jnp.exp2(dot(sources, targets) * scale).astype(BF)


def class_of():
    return lax.axis_index("pair") * lax.axis_size("rhs") + lax.axis_index("rhs")


def halo_body(classes, pts_ref, near_ref, far_ref, up_ref, down_ref, pairs_ref, near_buf, far_buf, sems):
    halo = up_ref.shape[0]
    half = pts_ref.shape[0] // 2
    copies = [
        pltpu.make_async_copy(near_ref, near_buf, sems.at[2 * halo]),
        pltpu.make_async_copy(far_ref, far_buf, sems.at[2 * halo + 1]),
    ]
    for j in range(halo):
        leaf = class_of() + j * classes
        copies.append(pltpu.make_async_copy(pts_ref.at[leaf + half], up_ref.at[j], sems.at[j]))
        copies.append(pltpu.make_async_copy(pts_ref.at[leaf], down_ref.at[j], sems.at[halo + j]))
    for copy in copies:
        copy.start()
    for copy in copies:
        copy.wait()
    near_n = near_ref.shape[0]
    pairs_ref[:near_n] = near_buf[...]
    pairs_ref[near_n:] = far_buf[...]


def weights_body(
    blocks, classes, near_n, span, halo, own_ref, other_ref, order_ref, skel_ref, interp_ref, pts_ref, *refs
):
    pair_refs = refs[:-13]
    tw_ref, up_ref, mid_ref, down_ref, cnt_ref, far_ref = refs[-13:-7]
    stack, own_buf, order_buf, skel_buf, interp_buf, pts_buf, sems = refs[-7:]
    cols = own_ref.shape[0]
    step = 2 * cols
    width = stack.shape[1]
    turns = own_ref.shape[1] // width
    mine, _, size = tw_ref.shape
    rank = mid_ref.shape[1]
    dim = pts_ref.shape[1]
    cuts = size // rank
    leaves = pts_ref.shape[0]
    block, me = lax.axis_index("leaf"), class_of()
    base = block * leaves - span
    copies = [
        pltpu.make_async_copy(own_ref, own_buf, sems.at[0]),
        pltpu.make_async_copy(order_ref, order_buf, sems.at[1]),
        pltpu.make_async_copy(skel_ref, skel_buf, sems.at[2]),
    ]
    for j in range(mine):
        leaf = j * classes + me
        copies.append(pltpu.make_async_copy(interp_ref.at[leaf], interp_buf.at[j], sems.at[3 + 2 * j]))
        copies.append(pltpu.make_async_copy(pts_ref.at[leaf], pts_buf.at[j], sems.at[4 + 2 * j]))
    for copy in copies:
        copy.start()
    for e in range(cnt_ref.shape[0]):
        wanted = base + e * classes + me
        total = None
        for ref in pair_refs:
            part = jnp.sum(jnp.where(ref[:near_n] == wanted, 1, 0), axis=0, keepdims=True)
            total = part if total is None else total + part
        cnt_ref[e : e + 1] = total
    far_n = far_ref.shape[0] // len(pair_refs)
    for k, ref in enumerate(pair_refs):
        named = ref[near_n:]
        owner = lax.div(named, leaves)
        within = lax.rem(named, leaves)
        piece = lax.rem(block - owner + blocks, blocks) - 1
        target = lax.broadcasted_iota(jnp.int32, named.shape, 1)
        code = target * 256 + piece * mine + lax.div(within, classes)
        far_ref[k * far_n : (k + 1) * far_n] = jnp.where(lax.rem(within, classes) == me, code, -1)

    copies[0].wait()
    copies[1].wait()
    for hi in range(turns):
        span = slice(hi * width, (hi + 1) * width)
        stack[hi * step : hi * step + cols] = own_buf[:, span]
        stack[hi * step + cols : (hi + 1) * step] = other_ref[:, span]
    orders = {}
    for j in range(mine):
        leaf = j * classes + me
        ids = order_buf[:, pl.ds(pl.multiple_of(leaf * size, size), size)]
        hi_ids = lax.shift_right_logical(ids, width.bit_length() - 1)
        picked = dot(stack[...], one_hot(ids & (width - 1), width))
        total = jnp.zeros((step, size), F32)
        for hi in range(turns):
            total = total + jnp.where(hi_ids == hi, picked[hi * step : (hi + 1) * step], 0.0)
        tree = total.astype(BF)
        tw_ref[j] = tree
        if j == 0:
            for copy in copies[2:]:
                copy.wait()
        hot = one_hot(skel_buf[pl.ds(leaf, 1), :], size)
        ordered = dot(tree, hot)
        combined = dot_last(ordered[:, rank:].astype(BF), interp_buf[j])
        skel_p = dot(pts_buf[j], hot[:, :rank]).astype(BF)
        skel_w = (ordered[:, :rank] + combined).astype(BF)
        for ref, low, high in ((up_ref, 0, mine - halo), (mid_ref, 0, mine), (down_ref, halo, mine)):
            weights_at, halo_at = (high - low) * dim, (high - low) * dim + mine * step
            if low <= j < high:
                ref[(j - low) * dim : (j - low + 1) * dim] = skel_p
            elif ref is not mid_ref:
                place = j - (mine - halo) if low == 0 else j
                for cut in range(cuts):
                    at = halo_at + (place * cuts + cut) * step
                    ref[at : at + step] = tree[:, cut * rank : (cut + 1) * rank]
                row = lax.broadcasted_iota(jnp.int32, (EXTRA, rank), 0)
                picks = skel_buf[pl.ds(leaf, 1), :rank]
                high_half = jnp.where(row == 2 * place, lax.shift_right_logical(picks, 8), 0)
                halves = jnp.where(row == 2 * place + 1, picks & 255, high_half).astype(F32)
                before = orders.get(id(ref))
                orders[id(ref)] = halves if before is None else before + halves
                ref[halo_at + halo * cuts * step :] = orders[id(ref)].astype(BF)
            ref[weights_at + j * step : weights_at + (j + 1) * step] = skel_w


def list_named(t, first, count, cnt_ref, slots, at):
    found = jnp.int32(0)
    for e in range(count):
        slots[at + found] = jnp.int32(e)
        found = found + jnp.where(cnt_ref[first + e, t] > 0, 1, 0)
    return found


def named_sum(t, k, first, scale, cnt_ref, slots, at, tgt, src, weights, shift):
    if k == 0:
        return jnp.zeros((weights.shape[1], tgt.shape[2]), F32)
    names = [slots[at + j] for j in range(k)]
    size = src.shape[1]
    block = gauss(jnp.concatenate([src[s + shift] for s in names], axis=0), tgt[t], scale)
    total = None
    for j, s in enumerate(names):
        times = cnt_ref[first + s, t].astype(F32)
        part = dot(weights[s + shift], block[j * size : (j + 1) * size]) * times
        total = part if total is None else total + part
    return total


def near_body(
    halo, scale, cnt_ref, pts_ref, tw_ref, left_p, right_p, skel_ref,
    near_ref, tgt_ref, edge_src, far_tgt_ref, src, slots,
):
    leaves, _, size = pts_ref.shape
    mine = tw_ref.shape[0]
    classes = leaves // mine
    rank = far_tgt_ref.shape[2]

    def sources(j, _):
        src[j] = as_sources(pts_ref[j * classes + class_of()])
        return 0

    lax.fori_loop(0, mine, sources, 0)
    tgt_ref[0] = as_targets(pts_ref[0])

    def target(t, _):
        found = list_named(t, halo, mine, cnt_ref, slots, 0)
        for k in range(mine + 1):

            @pl.when(found == k)
            def _():
                total = named_sum(t, k, halo, scale, cnt_ref, slots, 0, tgt_ref, src, tw_ref, 0)
                hot = one_hot(skel_ref[pl.ds(t, 1), :rank], size)
                far_tgt = as_targets(dot(pts_ref[t], hot).astype(BF))
                later = jnp.minimum(t + 1, leaves - 1)
                following = as_targets(pts_ref[later])
                near_ref[t] = total
                far_tgt_ref[t] = far_tgt
                tgt_ref[later] = following

        return 0

    lax.fori_loop(0, leaves, target, 0)
    for j in range(halo):
        edge_src[j] = as_sources(left_p[j])
        edge_src[halo + j] = as_sources(right_p[j])


def edge_body(
    halo, mine, rank, scale, cnt_ref, near_ref, tgt_ref, src, left_m, right_m, own_ref, other_ref, wts, slots
):
    leaves, cols2, size = near_ref.shape
    cols = cols2 // 2
    quarter = leaves // 4
    cuts = size // rank
    for side, message in enumerate((left_m, right_m)):
        for j in range(halo):
            for cut in range(cuts):
                at = message.shape[0] - EXTRA - (halo * cuts - j * cuts - cut) * cols2
                wts[side * halo + j, :, cut * rank : (cut + 1) * rank] = message[at : at + cols2]

    def targets(i, _):
        right = lax.div(i, quarter)
        first = right * (halo + mine)
        pair = (right * quarter + i, right * quarter + i + quarter)
        founds = [list_named(t, first, halo, cnt_ref, slots, n * (halo + 1)) for n, t in enumerate(pair)]
        for k in range((halo + 1) ** 2):
            counts = divmod(k, halo + 1)

            @pl.when((founds[0] == counts[0]) & (founds[1] == counts[1]))
            def _():
                sums = [
                    named_sum(t, c, first, scale, cnt_ref, slots, n * (halo + 1), tgt_ref, src, wts, right * halo)
                    for n, (t, c) in enumerate(zip(pair, counts))
                ]
                totals = [near_ref[t] + part for t, part in zip(pair, sums)]
                for t, total in zip(pair, totals):
                    span = pl.ds(pl.multiple_of(t * size, size), size)
                    own_ref[:, span] = total[:cols]
                    other_ref[:, span] = total[cols:].astype(BF)

        return 0

    lax.fori_loop(0, 2 * quarter, targets, 0)


def sources_body(mine, left_p, right_p, *refs):
    pieces = refs[:-2]
    far_src, far_w = refs[-2:]
    halo, dim, size = left_p.shape
    _, cols2, rank = far_w.shape
    for k, piece in enumerate(pieces):
        low, high, points = 0, mine, None
        if k == 0:
            high, points = mine - halo, left_p
        elif k == len(pieces) - 1:
            low, points = halo, right_p
        weights_at = (high - low) * dim
        for j in range(mine):
            if low <= j < high:
                skel_p = piece[(j - low) * dim : (j - low + 1) * dim]
            else:
                place = j - (mine - halo) if k == 0 else j
                order = piece[piece.shape[0] - EXTRA :].astype(F32)
                picks = (order[2 * place : 2 * place + 1] * 256.0 + order[2 * place + 1 : 2 * place + 2]).astype(jnp.int32)
                skel_p = dot(points[place], one_hot(picks, size)).astype(BF)
            far_src[k * mine + j] = as_sources(skel_p)
            far_w[k * mine + j] = piece[weights_at + j * cols2 : weights_at + (j + 1) * cols2]


def sum_body(own_ref, back_ref, *refs):
    first_ref, last_ref = refs[-2:]
    half = first_ref.shape[1]
    for ref, span in ((first_ref, slice(0, half)), (last_ref, slice(half, 2 * half))):
        ref[...] = (own_ref[:, span] + back_ref[:, span].astype(F32)).astype(BF)


def far_body(scale, far_ref, far_src, far_w, far_tgt, after_ref, own_ref, other_ref, field, names):
    found = jnp.int32(0)
    for t in range(far_ref.shape[1]):
        for i in range(far_ref.shape[0]):
            code = far_ref[i, t]
            names[1 + found] = code
            found = found + jnp.where(code >= 0, 1, 0)
    names[0] = found
    for j in range(GROUP):
        names[1 + found + j] = jnp.int32(far_ref.shape[1] * 256)
    leaves, _, rank = far_tgt.shape
    cols = own_ref.shape[0]
    field[...] = jnp.zeros_like(field)

    def far_group(g, _):
        codes = [names[1 + g * GROUP + j] for j in range(GROUP)]
        targets = [lax.shift_right_logical(c, 8) for c in codes]
        blocks = [gauss(far_src[c & 255], far_tgt[t & (leaves - 1)], scale) for c, t in zip(codes, targets)]
        parts = [dot(far_w[c & 255], block) for c, block in zip(codes, blocks)]
        for t, part in zip(targets, parts):
            field[t] += part
        return 0

    lax.fori_loop(0, lax.div(names[0] + GROUP - 1, GROUP), far_group, 0)
    for t in range(leaves):
        own_ref[:, t * rank : (t + 1) * rank] = field[t, :cols]
        other_ref[:, t * rank : (t + 1) * rank] = field[t, cols:].astype(BF)


def scatter(ids, value, width, turns):
    hi_ids = lax.shift_right_logical(ids, width.bit_length() - 1)
    masked = [jnp.where(hi_ids == hi, value, 0.0).astype(BF) for hi in range(turns)]
    return dot_last(jnp.concatenate(masked, axis=0), one_hot(ids & (width - 1), width))


def place_near_body(order_ref, *refs):
    near, acc = refs[:-1], refs[-1]
    total = order_ref.shape[1]
    width = acc.shape[1]
    chunk = 1024
    for at in range(0, total, chunk):
        span = slice(at, at + chunk)
        value = sum(ref[:, span].astype(F32) for ref in near)
        part = scatter(order_ref[:, span], value, width, total // width)
        acc[...] = part if at == 0 else acc[...] + part


def comp_body(order_ref, skel_ref, comp_ref):
    leaves, size = skel_ref.shape
    for t in range(leaves):
        span = slice(t * size, (t + 1) * size)
        ids = order_ref[:, span]
        row = lax.broadcasted_iota(jnp.int32, (16, size), 0)
        halves = jnp.where(row == 0, lax.shift_right_logical(ids, 8), jnp.where(row == 1, ids & 255, 0))
        moved = dot(halves.astype(F32).astype(BF), one_hot(skel_ref[t : t + 1], size))
        comp_ref[:, span] = (moved[:1] * 256.0 + moved[1:2]).astype(jnp.int32)


def place_far(first, comp_ref, interp_ref, start_ref, far, acc, buf):
    cols = far[0].shape[0]
    width = acc.shape[1]
    turns = acc.shape[0] // cols
    _, rank, rest = interp_ref.shape
    size = rank + rest
    for t in range(far[0].shape[1] // rank):
        skel = sum(ref[:, t * rank : (t + 1) * rank].astype(F32) for ref in far).astype(BF)
        buf[:, t * size : t * size + rank] = skel.astype(F32)
        buf[:, t * size + rank : (t + 1) * size] = dot(skel, interp_ref[first + t])
    chunk = 1024
    for at in range(0, buf.shape[1], chunk):
        ids = comp_ref[:, first * size + at : first * size + at + chunk]
        part = scatter(ids, buf[:, at : at + chunk], width, turns)
        acc[...] = (start_ref if at == 0 else acc)[...] + part


def place_first_body(comp_ref, interp_ref, start_ref, *refs):
    place_far(0, comp_ref, interp_ref, start_ref, refs[:-2], refs[-2], refs[-1])


def place_last_body(comp_ref, interp_ref, start_ref, *refs):
    far, out_ref, acc, buf = refs[:-3], refs[-3], refs[-2], refs[-1]
    place_far(interp_ref.shape[0] // 2, comp_ref, interp_ref, start_ref, far, acc, buf)
    cols, total = out_ref.shape
    width = acc.shape[1]
    for hi in range(total // width):
        out_ref[:, hi * width : (hi + 1) * width] = acc[hi * cols : (hi + 1) * cols]


def pin(value):
    return pltpu.with_memory_space_constraint(value, pltpu.HBM)


def ring(count, by):
    return [(i, (i + by) % count) for i in range(count)]


def from_others(value, axis):
    count = lax.axis_size(axis)
    return [lax.ppermute(value, axis, ring(count, by)) for by in range(1, count)]


def over_pair(value, pair_n):
    if pair_n == 2:
        return [value] + from_others(value, "pair")
    return list(lax.all_gather(value, "pair"))


def on_device(points, weights, interp, tree_order, skel_order, near_pairs, far_pairs):
    leaves, size, dim = points.shape
    rank = interp.shape[1]
    cols = weights.shape[1]
    blocks, pair_n, rhs_n = (lax.axis_size(a) for a in ("leaf", "pair", "rhs"))
    classes = pair_n * rhs_n
    mine = leaves // classes
    span = min(8, leaves)
    halo = span // classes
    scale = 2.0 * 2.5 / dim * LOG2E
    near_n, far_n = near_pairs.shape[1], far_pairs.shape[1]
    wide = dim + EXTRA
    mega = 10 ** 9
    pts = points.transpose(0, 2, 1)
    wts = weights.T
    (other_wts,) = from_others(wts, "rhs")
    hbm = pl.BlockSpec(memory_space=pltpu.HBM)
    up_p, down_p, pairs = call(
        functools.partial(halo_body, classes),
        [((halo, dim, size), BF), ((halo, dim, size), BF), ((near_n + far_n, leaves), jnp.int32)],
        [hbm, hbm, hbm],
        (pin(pts), pin(near_pairs.T), pin(far_pairs.T)),
        [
            pltpu.VMEM((near_n, leaves), jnp.int32),
            pltpu.VMEM((far_n, leaves), jnp.int32),
            pltpu.SemaphoreType.DMA((2 * halo + 2,)),
        ],
        out_specs=[hbm, hbm, VMEM],
        grant=48,
    )
    every = [pairs] + from_others(pairs, "pair")
    left_p = lax.ppermute(up_p, "leaf", ring(blocks, 1))
    right_p = lax.ppermute(down_p, "leaf", ring(blocks, blocks - 1))
    tall = mine * (dim + 2 * cols)
    ends = tall - halo * dim + halo * (size // rank) * 2 * cols + EXTRA
    tree_w, up_m, mid_m, down_m, cnt, far_ids = call(
        functools.partial(weights_body, blocks, classes, near_n, span, halo),
        [
            ((mine, 2 * cols, size), BF),
            ((ends, rank), BF),
            ((tall, rank), BF),
            ((ends, rank), BF),
            ((2 * halo + mine, leaves), jnp.int32),
            ((pair_n * far_n, leaves), jnp.int32),
        ],
        [hbm, VMEM] + [hbm] * 4 + [VMEM] * pair_n,
        (pin(wts), other_wts, pin(tree_order), pin(skel_order), pin(interp), pin(pts), *every),
        [
            pltpu.VMEM((2 * cols * (leaves * size // 256), 256), BF),
            pltpu.VMEM((cols, leaves * size), BF),
            pltpu.VMEM((1, leaves * size), jnp.int32),
            pltpu.VMEM((leaves, size), jnp.int32),
            pltpu.VMEM((mine, rank, size - rank), BF),
            pltpu.VMEM((mine, dim, size), BF),
            pltpu.SemaphoreType.DMA((3 + 2 * mine,)),
        ],
        flops=3 * mega,
        grant=48,
    )
    outgoing = {by: mid_m for by in range(1, blocks)} | {1: up_m, blocks - 1: down_m}
    pieces = [lax.ppermute(outgoing[by], "leaf", ring(blocks, by)) for by in range(1, blocks)]
    near, tgt, edge_src, far_tgt = call(
        functools.partial(near_body, halo, scale),
        [
            ((leaves, 2 * cols, size), F32),
            ((leaves, wide, size), BF),
            ((2 * halo, size, wide), BF),
            ((leaves, wide, rank), BF),
        ],
        [SMEM] + [VMEM] * 5,
        (cnt, pts, tree_w, left_p, right_p, skel_order),
        [pltpu.VMEM((mine, size, wide), BF), pltpu.SMEM((mine + 1,), jnp.int32)],
        flops=14 * mega,
    )

    near_own, near_other = call(
        functools.partial(edge_body, halo, mine, rank, scale),
        [((cols, leaves * size), F32), ((cols, leaves * size), BF)],
        [SMEM] + [VMEM] * 5,
        (cnt, near, tgt, edge_src, pieces[0], pieces[-1]),
        [pltpu.VMEM((2 * halo, 2 * cols, size), BF), pltpu.SMEM((2 * halo + 2,), jnp.int32)],
        flops=6 * mega,
    )
    (near_back,) = from_others(near_other, "rhs")
    near_sum_own = (near_own + near_back.astype(F32)).astype(BF)
    near_parts = over_pair(near_sum_own, pair_n)
    piece_n = (blocks - 1) * mine
    far_src, far_w = call(
        functools.partial(sources_body, mine),
        [((piece_n, rank, wide), BF), ((piece_n, 2 * cols, rank), BF)],
        [VMEM] * (blocks + 1),
        (left_p, right_p, *pieces),
        flops=2 * mega,
    )
    far_own, far_other = call(
        functools.partial(far_body, scale),
        [((cols, leaves * rank), F32), ((cols, leaves * rank), BF)],
        [SMEM, VMEM, VMEM, VMEM, pl.BlockSpec(memory_space=pl.ANY)],
        (far_ids, far_src, far_w, far_tgt, near_sum_own),
        [pltpu.VMEM((leaves + 1, 2 * cols, rank), F32), pltpu.SMEM((leaves * pair_n * far_n + 16,), jnp.int32)],
        flops=4 * mega,
    )
    (far_back,) = from_others(far_other, "rhs")
    (comp,) = call(
        comp_body, [((1, leaves * size), jnp.int32)], [VMEM] * 2, (tree_order, skel_order), flops=mega
    )
    halves = call(
        sum_body,
        [((cols, leaves // 2 * rank), BF)] * 2,
        [VMEM, VMEM] + [pl.BlockSpec(memory_space=pl.ANY)] * pair_n,
        (far_own, far_back, comp, *near_parts[1:]),
    )
    first_parts, last_parts = (over_pair(half, pair_n) for half in halves)
    acc_shape = (leaves * size // 256 * cols, 256)
    (acc,) = call(
        place_near_body,
        [(acc_shape, F32)],
        [VMEM] * (1 + pair_n),
        (tree_order, *near_parts),
        flops=3 * mega,
    )
    (acc,) = call(
        place_first_body,
        [(acc_shape, F32)],
        [VMEM] * (3 + pair_n),
        (comp, interp, acc, *first_parts),
        [pltpu.VMEM((cols, leaves // 2 * size), F32)],
        flops=2 * mega,
    )
    (out,) = call(
        place_last_body,
        [((cols, leaves * size), F32)],
        [VMEM] * (3 + pair_n),
        (comp, interp, acc, *last_parts),
        [pltpu.VMEM(acc_shape, F32), pltpu.VMEM((cols, leaves // 2 * size), F32)],
        flops=2 * mega,
    )
    return out.T


def solution(mesh):
    return jax.shard_map(
        on_device,
        mesh=mesh,
        in_specs=(
            P(("groups", "leaf"), None, None),
            P(("groups", "leaf"), "rhs"),
            P(("groups", "leaf"), None, None),
            P(("groups", "leaf"), None),
            P(("groups", "leaf"), None),
            P(("groups", "leaf"), "pair"),
            P(("groups", "leaf"), "pair"),
        ),
        out_specs=P(("groups", "leaf"), "rhs"),
        check_vma=False,
    )
```

```python
import functools

import jax
import jax.numpy as jnp
from jax import lax
from jax.experimental import pallas as pl
from jax.experimental.pallas import tpu as pltpu
from jax.sharding import PartitionSpec as P

BF = jnp.bfloat16
F32 = jnp.float32
LOG2E = 1.4426950408889634
EXTRA = 16
GROUP = 8
VMEM = pl.BlockSpec(memory_space=pltpu.VMEM)
SMEM = pl.BlockSpec(memory_space=pltpu.SMEM)


def call(body, shapes, specs, args, scratch=(), flops=0, out_specs=None, grant=48):
    outs = [jax.ShapeDtypeStruct(s, d) for s, d in shapes]
    return pl.pallas_call(
        body,
        out_shape=outs,
        in_specs=specs,
        out_specs=out_specs or [VMEM] * len(outs),
        scratch_shapes=list(scratch),
        compiler_params=pltpu.CompilerParams(vmem_limit_bytes=grant << 20),
        cost_estimate=pl.CostEstimate(flops=flops, bytes_accessed=1 << 20, transcendentals=0),
    )(*args)


def extra_rows(feat, ones_first):
    wide = feat.astype(F32)
    half = -0.5 * jnp.sum(wide * wide, axis=0, keepdims=True)
    high = half.astype(BF).astype(F32)
    mid = (half - high).astype(BF).astype(F32)
    low = half - high - mid
    row = lax.broadcasted_iota(jnp.int32, (EXTRA, feat.shape[1]), 0)
    at = 3 if ones_first else 0
    ones = (row < 3) if ones_first else (row >= 3) & (row < 6)
    picked = jnp.where(row == at, high, jnp.where(row == at + 1, mid, jnp.where(row == at + 2, low, 0.0)))
    return jnp.where(ones, 1.0, picked).astype(BF)


def as_targets(feat):
    return jnp.concatenate([feat, extra_rows(feat, False)], axis=0)


def as_sources(feat):
    return jnp.concatenate([feat, extra_rows(feat, True)], axis=0).astype(F32).T.astype(BF)


def one_hot(row_ids, count):
    rows = lax.broadcasted_iota(jnp.int32, (count, row_ids.shape[1]), 0)
    return jnp.where(rows == row_ids, 1.0, 0.0).astype(BF)


def dot(a, b):
    return jnp.dot(a, b, preferred_element_type=F32)


def dot_last(a, b):
    return lax.dot_general(a, b, (((1,), (1,)), ((), ())), preferred_element_type=F32)


def gauss(sources, targets, scale):
    return jnp.exp2(dot(sources, targets) * scale).astype(BF)


def class_of():
    return lax.axis_index("pair") * lax.axis_size("rhs") + lax.axis_index("rhs")


def halo_body(classes, pts_ref, near_ref, far_ref, up_ref, down_ref, pairs_ref, near_buf, far_buf, sems):
    halo = up_ref.shape[0]
    half = pts_ref.shape[0] // 2
    copies = [
        pltpu.make_async_copy(near_ref, near_buf, sems.at[2 * halo]),
        pltpu.make_async_copy(far_ref, far_buf, sems.at[2 * halo + 1]),
    ]
    for j in range(halo):
        leaf = class_of() + j * classes
        copies.append(pltpu.make_async_copy(pts_ref.at[leaf + half], up_ref.at[j], sems.at[j]))
        copies.append(pltpu.make_async_copy(pts_ref.at[leaf], down_ref.at[j], sems.at[halo + j]))
    for copy in copies:
        copy.start()
    for copy in copies:
        copy.wait()
    near_n = near_ref.shape[0]
    pairs_ref[:near_n] = near_buf[...]
    pairs_ref[near_n:] = far_buf[...]


def weights_body(
    blocks, classes, near_n, span, halo, own_ref, other_ref, order_ref, skel_ref, interp_ref, pts_ref, *refs
):
    pair_refs = refs[:-14]
    tw_ref, up_ref, mid_ref, down_ref, cnt_ref, far_ref = refs[-14:-8]
    stack, own_buf, order_buf, skel_buf, interp_buf, pts_buf, hots, sems = refs[-8:]
    cols = own_ref.shape[0]
    step = 2 * cols
    width = stack.shape[1]
    turns = own_ref.shape[1] // width
    mine, _, size = tw_ref.shape
    rank = mid_ref.shape[1]
    dim = pts_ref.shape[1]
    cuts = size // rank
    leaves = pts_ref.shape[0]
    block, me = lax.axis_index("leaf"), class_of()
    base = block * leaves - span
    copies = [
        pltpu.make_async_copy(own_ref, own_buf, sems.at[0]),
        pltpu.make_async_copy(order_ref, order_buf, sems.at[1]),
        pltpu.make_async_copy(skel_ref, skel_buf, sems.at[2]),
    ]
    for j in range(mine):
        leaf = j * classes + me
        copies.append(pltpu.make_async_copy(interp_ref.at[leaf], interp_buf.at[j], sems.at[3 + 2 * j]))
        copies.append(pltpu.make_async_copy(pts_ref.at[leaf], pts_buf.at[j], sems.at[4 + 2 * j]))
    for copy in copies:
        copy.start()
    for e in range(cnt_ref.shape[0]):
        wanted = base + e * classes + me
        total = None
        for ref in pair_refs:
            part = jnp.sum(jnp.where(ref[:near_n] == wanted, 1, 0), axis=0, keepdims=True)
            total = part if total is None else total + part
        cnt_ref[e : e + 1] = total
    far_n = far_ref.shape[0] // len(pair_refs)
    for k, ref in enumerate(pair_refs):
        named = ref[near_n:]
        owner = lax.div(named, leaves)
        within = lax.rem(named, leaves)
        piece = lax.rem(block - owner + blocks, blocks) - 1
        target = lax.broadcasted_iota(jnp.int32, named.shape, 1)
        code = target * 256 + piece * mine + lax.div(within, classes)
        far_ref[k * far_n : (k + 1) * far_n] = jnp.where(lax.rem(within, classes) == me, code, -1)

    copies[0].wait()
    copies[1].wait()
    for hi in range(turns):
        span = slice(hi * width, (hi + 1) * width)
        stack[hi * step : hi * step + cols] = own_buf[:, span]
        stack[hi * step + cols : (hi + 1) * step] = other_ref[:, span]
    orders = {}
    for j in range(mine):
        leaf = j * classes + me
        ids = order_buf[:, pl.ds(pl.multiple_of(leaf * size, size), size)]
        hi_ids = lax.shift_right_logical(ids, width.bit_length() - 1)
        picked = dot(stack[...], one_hot(ids & (width - 1), width))
        total = jnp.zeros((step, size), F32)
        for hi in range(turns):
            total = total + jnp.where(hi_ids == hi, picked[hi * step : (hi + 1) * step], 0.0)
        tw_ref[j] = total.astype(BF)
    for copy in copies[2:]:
        copy.wait()
    for j in range(mine):
        hots[j] = one_hot(skel_buf[pl.ds(j * classes + me, 1), :], size)
    skel_ps = [dot(pts_buf[j], hots[j, :, :rank]).astype(BF) for j in range(mine)]
    ordereds = [dot(tw_ref[j], hots[j]) for j in range(mine)]
    combineds = [dot_last(ordereds[j][:, rank:].astype(BF), interp_buf[j]) for j in range(mine)]
    for j in range(mine):
        leaf = j * classes + me
        tree = tw_ref[j]
        skel_p = skel_ps[j]
        skel_w = (ordereds[j][:, :rank] + combineds[j]).astype(BF)
        for ref, low, high in ((up_ref, 0, mine - halo), (mid_ref, 0, mine), (down_ref, halo, mine)):
            weights_at, halo_at = (high - low) * dim, (high - low) * dim + mine * step
            if low <= j < high:
                ref[(j - low) * dim : (j - low + 1) * dim] = skel_p
            elif ref is not mid_ref:
                place = j - (mine - halo) if low == 0 else j
                for cut in range(cuts):
                    at = halo_at + (place * cuts + cut) * step
                    ref[at : at + step] = tree[:, cut * rank : (cut + 1) * rank]
                row = lax.broadcasted_iota(jnp.int32, (EXTRA, rank), 0)
                picks = skel_buf[pl.ds(leaf, 1), :rank]
                high_half = jnp.where(row == 2 * place, lax.shift_right_logical(picks, 8), 0)
                halves = jnp.where(row == 2 * place + 1, picks & 255, high_half).astype(F32)
                before = orders.get(id(ref))
                orders[id(ref)] = halves if before is None else before + halves
                ref[halo_at + halo * cuts * step :] = orders[id(ref)].astype(BF)
            ref[weights_at + j * step : weights_at + (j + 1) * step] = skel_w


def list_named(t, first, count, cnt_ref, slots, at):
    found = jnp.int32(0)
    for e in range(count):
        slots[at + found] = jnp.int32(e)
        found = found + jnp.where(cnt_ref[first + e, t] > 0, 1, 0)
    return found


def named_sum(t, k, first, scale, cnt_ref, slots, at, tgt, src, weights, shift):
    if k == 0:
        return jnp.zeros((weights.shape[1], tgt.shape[2]), F32)
    names = [slots[at + j] for j in range(k)]
    size = src.shape[1]
    block = gauss(jnp.concatenate([src[s + shift] for s in names], axis=0), tgt[t], scale)
    total = None
    for j, s in enumerate(names):
        times = cnt_ref[first + s, t].astype(F32)
        part = dot(weights[s + shift], block[j * size : (j + 1) * size]) * times
        total = part if total is None else total + part
    return total


def near_body(
    halo, scale, cnt_ref, pts_ref, tw_ref, left_p, right_p, skel_ref,
    near_ref, tgt_ref, edge_src, far_tgt_ref, src, slots,
):
    leaves, _, size = pts_ref.shape
    mine = tw_ref.shape[0]
    classes = leaves // mine
    rank = far_tgt_ref.shape[2]

    def sources(j, _):
        src[j] = as_sources(pts_ref[j * classes + class_of()])
        return 0

    lax.fori_loop(0, mine, sources, 0)
    tgt_ref[0] = as_targets(pts_ref[0])

    def target(t, _):
        found = list_named(t, halo, mine, cnt_ref, slots, 0)
        for k in range(mine + 1):

            @pl.when(found == k)
            def _():
                total = named_sum(t, k, halo, scale, cnt_ref, slots, 0, tgt_ref, src, tw_ref, 0)
                hot = one_hot(skel_ref[pl.ds(t, 1), :rank], size)
                far_tgt = as_targets(dot(pts_ref[t], hot).astype(BF))
                later = jnp.minimum(t + 1, leaves - 1)
                following = as_targets(pts_ref[later])
                near_ref[t] = total
                far_tgt_ref[t] = far_tgt
                tgt_ref[later] = following

        return 0

    lax.fori_loop(0, leaves, target, 0)
    for j in range(halo):
        edge_src[j] = as_sources(left_p[j])
        edge_src[halo + j] = as_sources(right_p[j])


def edge_body(
    halo, mine, rank, scale, cnt_ref, near_ref, tgt_ref, src, left_m, right_m, own_ref, other_ref, wts, slots
):
    leaves, cols2, size = near_ref.shape
    cols = cols2 // 2
    quarter = leaves // 4
    cuts = size // rank
    for side, message in enumerate((left_m, right_m)):
        for j in range(halo):
            for cut in range(cuts):
                at = message.shape[0] - EXTRA - (halo * cuts - j * cuts - cut) * cols2
                wts[side * halo + j, :, cut * rank : (cut + 1) * rank] = message[at : at + cols2]

    def targets(i, _):
        right = lax.div(i, quarter)
        first = right * (halo + mine)
        pair = (right * quarter + i, right * quarter + i + quarter)
        founds = [list_named(t, first, halo, cnt_ref, slots, n * (halo + 1)) for n, t in enumerate(pair)]
        for k in range((halo + 1) ** 2):
            counts = divmod(k, halo + 1)

            @pl.when((founds[0] == counts[0]) & (founds[1] == counts[1]))
            def _():
                sums = [
                    named_sum(t, c, first, scale, cnt_ref, slots, n * (halo + 1), tgt_ref, src, wts, right * halo)
                    for n, (t, c) in enumerate(zip(pair, counts))
                ]
                totals = [near_ref[t] + part for t, part in zip(pair, sums)]
                for t, total in zip(pair, totals):
                    span = pl.ds(pl.multiple_of(t * size, size), size)
                    own_ref[:, span] = total[:cols]
                    other_ref[:, span] = total[cols:].astype(BF)

        return 0

    lax.fori_loop(0, 2 * quarter, targets, 0)


def sources_body(mine, left_p, right_p, *refs):
    pieces = refs[:-2]
    far_src, far_w = refs[-2:]
    halo, dim, size = left_p.shape
    _, cols2, rank = far_w.shape
    for k, piece in enumerate(pieces):
        low, high, points = 0, mine, None
        if k == 0:
            high, points = mine - halo, left_p
        elif k == len(pieces) - 1:
            low, points = halo, right_p
        weights_at = (high - low) * dim
        for j in range(mine):
            if low <= j < high:
                skel_p = piece[(j - low) * dim : (j - low + 1) * dim]
            else:
                place = j - (mine - halo) if k == 0 else j
                order = piece[piece.shape[0] - EXTRA :].astype(F32)
                picks = (order[2 * place : 2 * place + 1] * 256.0 + order[2 * place + 1 : 2 * place + 2]).astype(jnp.int32)
                skel_p = dot(points[place], one_hot(picks, size)).astype(BF)
            far_src[k * mine + j] = as_sources(skel_p)
            far_w[k * mine + j] = piece[weights_at + j * cols2 : weights_at + (j + 1) * cols2]


def sum_body(own_ref, back_ref, *refs):
    first_ref, last_ref = refs[-2:]
    half = first_ref.shape[1]
    for ref, span in ((first_ref, slice(0, half)), (last_ref, slice(half, 2 * half))):
        ref[...] = (own_ref[:, span] + back_ref[:, span].astype(F32)).astype(BF)


def far_body(scale, far_ref, far_src, far_w, far_tgt, after_ref, own_ref, other_ref, field, names):
    found = jnp.int32(0)
    for t in range(far_ref.shape[1]):
        for i in range(far_ref.shape[0]):
            code = far_ref[i, t]
            names[1 + found] = code
            found = found + jnp.where(code >= 0, 1, 0)
    names[0] = found
    for j in range(GROUP):
        names[1 + found + j] = jnp.int32(far_ref.shape[1] * 256)
    leaves, _, rank = far_tgt.shape
    cols = own_ref.shape[0]
    field[...] = jnp.zeros_like(field)

    def far_group(g, _):
        codes = [names[1 + g * GROUP + j] for j in range(GROUP)]
        targets = [lax.shift_right_logical(c, 8) for c in codes]
        blocks = [gauss(far_src[c & 255], far_tgt[t & (leaves - 1)], scale) for c, t in zip(codes, targets)]
        parts = [dot(far_w[c & 255], block) for c, block in zip(codes, blocks)]
        for t, part in zip(targets, parts):
            field[t] += part
        return 0

    lax.fori_loop(0, lax.div(names[0] + GROUP - 1, GROUP), far_group, 0)
    for t in range(leaves):
        own_ref[:, t * rank : (t + 1) * rank] = field[t, :cols]
        other_ref[:, t * rank : (t + 1) * rank] = field[t, cols:].astype(BF)


def scatter(ids, value, width, turns):
    hi_ids = lax.shift_right_logical(ids, width.bit_length() - 1)
    masked = [jnp.where(hi_ids == hi, value, 0.0).astype(BF) for hi in range(turns)]
    return dot_last(jnp.concatenate(masked, axis=0), one_hot(ids & (width - 1), width))


def place_near_body(order_ref, *refs):
    near, acc = refs[:-1], refs[-1]
    total = order_ref.shape[1]
    width = acc.shape[1]
    chunk = 1024
    for at in range(0, total, chunk):
        span = slice(at, at + chunk)
        value = sum(ref[:, span].astype(F32) for ref in near)
        part = scatter(order_ref[:, span], value, width, total // width)
        acc[...] = part if at == 0 else acc[...] + part


def comp_body(order_ref, skel_ref, comp_ref):
    leaves, size = skel_ref.shape
    for t in range(leaves):
        span = slice(t * size, (t + 1) * size)
        ids = order_ref[:, span]
        row = lax.broadcasted_iota(jnp.int32, (16, size), 0)
        halves = jnp.where(row == 0, lax.shift_right_logical(ids, 8), jnp.where(row == 1, ids & 255, 0))
        moved = dot(halves.astype(F32).astype(BF), one_hot(skel_ref[t : t + 1], size))
        comp_ref[:, span] = (moved[:1] * 256.0 + moved[1:2]).astype(jnp.int32)


def place_far(first, comp_ref, interp_ref, start_ref, far, acc, buf):
    cols = far[0].shape[0]
    width = acc.shape[1]
    turns = acc.shape[0] // cols
    _, rank, rest = interp_ref.shape
    size = rank + rest
    for t in range(far[0].shape[1] // rank):
        skel = sum(ref[:, t * rank : (t + 1) * rank].astype(F32) for ref in far).astype(BF)
        buf[:, t * size : t * size + rank] = skel.astype(F32)
        buf[:, t * size + rank : (t + 1) * size] = dot(skel, interp_ref[first + t])
    chunk = 1024
    for at in range(0, buf.shape[1], chunk):
        ids = comp_ref[:, first * size + at : first * size + at + chunk]
        part = scatter(ids, buf[:, at : at + chunk], width, turns)
        acc[...] = (start_ref if at == 0 else acc)[...] + part


def place_first_body(comp_ref, interp_ref, start_ref, *refs):
    place_far(0, comp_ref, interp_ref, start_ref, refs[:-2], refs[-2], refs[-1])


def place_last_body(comp_ref, interp_ref, start_ref, *refs):
    far, out_ref, acc, buf = refs[:-3], refs[-3], refs[-2], refs[-1]
    place_far(interp_ref.shape[0] // 2, comp_ref, interp_ref, start_ref, far, acc, buf)
    cols, total = out_ref.shape
    width = acc.shape[1]
    for hi in range(total // width):
        out_ref[:, hi * width : (hi + 1) * width] = acc[hi * cols : (hi + 1) * cols]


def pin(value):
    return pltpu.with_memory_space_constraint(value, pltpu.HBM)


def ring(count, by):
    return [(i, (i + by) % count) for i in range(count)]


def from_others(value, axis):
    count = lax.axis_size(axis)
    return [lax.ppermute(value, axis, ring(count, by)) for by in range(1, count)]


def over_pair(value, pair_n):
    if pair_n == 2:
        return [value] + from_others(value, "pair")
    return list(lax.all_gather(value, "pair"))


def on_device(points, weights, interp, tree_order, skel_order, near_pairs, far_pairs):
    leaves, size, dim = points.shape
    rank = interp.shape[1]
    cols = weights.shape[1]
    blocks, pair_n, rhs_n = (lax.axis_size(a) for a in ("leaf", "pair", "rhs"))
    classes = pair_n * rhs_n
    mine = leaves // classes
    span = min(8, leaves)
    halo = span // classes
    scale = 2.0 * 2.5 / dim * LOG2E
    near_n, far_n = near_pairs.shape[1], far_pairs.shape[1]
    wide = dim + EXTRA
    mega = 10 ** 9
    pts = points.transpose(0, 2, 1)
    wts = weights.T
    (other_wts,) = from_others(wts, "rhs")
    hbm = pl.BlockSpec(memory_space=pltpu.HBM)
    up_p, down_p, pairs = call(
        functools.partial(halo_body, classes),
        [((halo, dim, size), BF), ((halo, dim, size), BF), ((near_n + far_n, leaves), jnp.int32)],
        [hbm, hbm, hbm],
        (pin(pts), pin(near_pairs.T), pin(far_pairs.T)),
        [
            pltpu.VMEM((near_n, leaves), jnp.int32),
            pltpu.VMEM((far_n, leaves), jnp.int32),
            pltpu.SemaphoreType.DMA((2 * halo + 2,)),
        ],
        out_specs=[hbm, hbm, VMEM],
        grant=48,
    )
    every = [pairs] + from_others(pairs, "pair")
    left_p = lax.ppermute(up_p, "leaf", ring(blocks, 1))
    right_p = lax.ppermute(down_p, "leaf", ring(blocks, blocks - 1))
    tall = mine * (dim + 2 * cols)
    ends = tall - halo * dim + halo * (size // rank) * 2 * cols + EXTRA
    tree_w, up_m, mid_m, down_m, cnt, far_ids = call(
        functools.partial(weights_body, blocks, classes, near_n, span, halo),
        [
            ((mine, 2 * cols, size), BF),
            ((ends, rank), BF),
            ((tall, rank), BF),
            ((ends, rank), BF),
            ((2 * halo + mine, leaves), jnp.int32),
            ((pair_n * far_n, leaves), jnp.int32),
        ],
        [hbm, VMEM] + [hbm] * 4 + [VMEM] * pair_n,
        (pin(wts), other_wts, pin(tree_order), pin(skel_order), pin(interp), pin(pts), *every),
        [
            pltpu.VMEM((2 * cols * (leaves * size // 256), 256), BF),
            pltpu.VMEM((cols, leaves * size), BF),
            pltpu.VMEM((1, leaves * size), jnp.int32),
            pltpu.VMEM((leaves, size), jnp.int32),
            pltpu.VMEM((mine, rank, size - rank), BF),
            pltpu.VMEM((mine, dim, size), BF),
            pltpu.VMEM((mine, size, size), BF),
            pltpu.SemaphoreType.DMA((3 + 2 * mine,)),
        ],
        flops=3 * mega,
        grant=48,
    )
    outgoing = {by: mid_m for by in range(1, blocks)} | {1: up_m, blocks - 1: down_m}
    pieces = [lax.ppermute(outgoing[by], "leaf", ring(blocks, by)) for by in range(1, blocks)]
    near, tgt, edge_src, far_tgt = call(
        functools.partial(near_body, halo, scale),
        [
            ((leaves, 2 * cols, size), F32),
            ((leaves, wide, size), BF),
            ((2 * halo, size, wide), BF),
            ((leaves, wide, rank), BF),
        ],
        [SMEM] + [VMEM] * 5,
        (cnt, pts, tree_w, left_p, right_p, skel_order),
        [pltpu.VMEM((mine, size, wide), BF), pltpu.SMEM((mine + 1,), jnp.int32)],
        flops=14 * mega,
    )

    near_own, near_other = call(
        functools.partial(edge_body, halo, mine, rank, scale),
        [((cols, leaves * size), F32), ((cols, leaves * size), BF)],
        [SMEM] + [VMEM] * 5,
        (cnt, near, tgt, edge_src, pieces[0], pieces[-1]),
        [pltpu.VMEM((2 * halo, 2 * cols, size), BF), pltpu.SMEM((2 * halo + 2,), jnp.int32)],
        flops=6 * mega,
    )
    (near_back,) = from_others(near_other, "rhs")
    near_sum_own = (near_own + near_back.astype(F32)).astype(BF)
    near_parts = over_pair(near_sum_own, pair_n)
    piece_n = (blocks - 1) * mine
    far_src, far_w = call(
        functools.partial(sources_body, mine),
        [((piece_n, rank, wide), BF), ((piece_n, 2 * cols, rank), BF)],
        [VMEM] * (blocks + 1),
        (left_p, right_p, *pieces),
        flops=2 * mega,
    )
    far_own, far_other = call(
        functools.partial(far_body, scale),
        [((cols, leaves * rank), F32), ((cols, leaves * rank), BF)],
        [SMEM, VMEM, VMEM, VMEM, pl.BlockSpec(memory_space=pl.ANY)],
        (far_ids, far_src, far_w, far_tgt, near_sum_own),
        [pltpu.VMEM((leaves + 1, 2 * cols, rank), F32), pltpu.SMEM((leaves * pair_n * far_n + 16,), jnp.int32)],
        flops=4 * mega,
    )
    (far_back,) = from_others(far_other, "rhs")
    (comp,) = call(
        comp_body, [((1, leaves * size), jnp.int32)], [VMEM] * 2, (tree_order, skel_order), flops=mega
    )
    halves = call(
        sum_body,
        [((cols, leaves // 2 * rank), BF)] * 2,
        [VMEM, VMEM] + [pl.BlockSpec(memory_space=pl.ANY)] * pair_n,
        (far_own, far_back, comp, *near_parts[1:]),
    )
    first_parts, last_parts = (over_pair(half, pair_n) for half in halves)
    acc_shape = (leaves * size // 256 * cols, 256)
    (acc,) = call(
        place_near_body,
        [(acc_shape, F32)],
        [VMEM] * (1 + pair_n),
        (tree_order, *near_parts),
        flops=3 * mega,
    )
    (acc,) = call(
        place_first_body,
        [(acc_shape, F32)],
        [VMEM] * (3 + pair_n),
        (comp, interp, acc, *first_parts),
        [pltpu.VMEM((cols, leaves // 2 * size), F32)],
        flops=2 * mega,
    )
    (out,) = call(
        place_last_body,
        [((cols, leaves * size), F32)],
        [VMEM] * (3 + pair_n),
        (comp, interp, acc, *last_parts),
        [pltpu.VMEM(acc_shape, F32), pltpu.VMEM((cols, leaves // 2 * size), F32)],
        flops=2 * mega,
    )
    return out.T


def solution(mesh):
    return jax.shard_map(
        on_device,
        mesh=mesh,
        in_specs=(
            P(("groups", "leaf"), None, None),
            P(("groups", "leaf"), "rhs"),
            P(("groups", "leaf"), None, None),
            P(("groups", "leaf"), None),
            P(("groups", "leaf"), None),
            P(("groups", "leaf"), "pair"),
            P(("groups", "leaf"), "pair"),
        ),
        out_specs=P(("groups", "leaf"), "rhs"),
        check_vma=False,
    )
```

```python
import functools

import jax
import jax.numpy as jnp
from jax import lax
from jax.experimental import pallas as pl
from jax.experimental.pallas import tpu as pltpu
from jax.sharding import PartitionSpec as P

BF = jnp.bfloat16
F32 = jnp.float32
LOG2E = 1.4426950408889634
EXTRA = 16
GROUP = 8
VMEM = pl.BlockSpec(memory_space=pltpu.VMEM)
SMEM = pl.BlockSpec(memory_space=pltpu.SMEM)


def call(body, shapes, specs, args, scratch=(), flops=0, out_specs=None, grant=48):
    outs = [jax.ShapeDtypeStruct(s, d) for s, d in shapes]
    return pl.pallas_call(
        body,
        out_shape=outs,
        in_specs=specs,
        out_specs=out_specs or [VMEM] * len(outs),
        scratch_shapes=list(scratch),
        compiler_params=pltpu.CompilerParams(vmem_limit_bytes=grant << 20),
        cost_estimate=pl.CostEstimate(flops=flops, bytes_accessed=1 << 20, transcendentals=0),
    )(*args)


def extra_rows(feat, ones_first):
    wide = feat.astype(F32)
    half = -0.5 * jnp.sum(wide * wide, axis=0, keepdims=True)
    high = half.astype(BF).astype(F32)
    mid = (half - high).astype(BF).astype(F32)
    low = half - high - mid
    row = lax.broadcasted_iota(jnp.int32, (EXTRA, feat.shape[1]), 0)
    at = 3 if ones_first else 0
    ones = (row < 3) if ones_first else (row >= 3) & (row < 6)
    picked = jnp.where(row == at, high, jnp.where(row == at + 1, mid, jnp.where(row == at + 2, low, 0.0)))
    return jnp.where(ones, 1.0, picked).astype(BF)


def as_targets(feat):
    return jnp.concatenate([feat, extra_rows(feat, False)], axis=0)


def as_sources(feat):
    return jnp.concatenate([feat, extra_rows(feat, True)], axis=0).astype(F32).T.astype(BF)


def one_hot(row_ids, count):
    rows = lax.broadcasted_iota(jnp.int32, (count, row_ids.shape[1]), 0)
    return jnp.where(rows == row_ids, 1.0, 0.0).astype(BF)


def dot(a, b):
    return jnp.dot(a, b, preferred_element_type=F32)


def dot_last(a, b):
    return lax.dot_general(a, b, (((1,), (1,)), ((), ())), preferred_element_type=F32)


def gauss(sources, targets, scale):
    return jnp.exp2(dot(sources, targets) * scale).astype(BF)


def class_of():
    return lax.axis_index("pair") * lax.axis_size("rhs") + lax.axis_index("rhs")


def halo_body(classes, pts_ref, near_ref, far_ref, up_ref, down_ref, pairs_ref, near_buf, far_buf, sems):
    halo = up_ref.shape[0]
    half = pts_ref.shape[0] // 2
    copies = [
        pltpu.make_async_copy(near_ref, near_buf, sems.at[2 * halo]),
        pltpu.make_async_copy(far_ref, far_buf, sems.at[2 * halo + 1]),
    ]
    for j in range(halo):
        leaf = class_of() + j * classes
        copies.append(pltpu.make_async_copy(pts_ref.at[leaf + half], up_ref.at[j], sems.at[j]))
        copies.append(pltpu.make_async_copy(pts_ref.at[leaf], down_ref.at[j], sems.at[halo + j]))
    for copy in copies:
        copy.start()
    for copy in copies:
        copy.wait()
    near_n = near_ref.shape[0]
    pairs_ref[:near_n] = near_buf[...]
    pairs_ref[near_n:] = far_buf[...]


def weights_body(
    blocks, classes, near_n, span, halo, own_ref, other_ref, order_ref, skel_ref, interp_ref, pts_ref, *refs
):
    pair_refs = refs[:-14]
    tw_ref, up_ref, mid_ref, down_ref, cnt_ref, far_ref = refs[-14:-8]
    stack, own_buf, order_buf, skel_buf, interp_buf, pts_buf, hots, sems = refs[-8:]
    cols = own_ref.shape[0]
    step = 2 * cols
    width = stack.shape[1]
    turns = own_ref.shape[1] // width
    mine, _, size = tw_ref.shape
    rank = mid_ref.shape[1]
    dim = pts_ref.shape[1]
    cuts = size // rank
    leaves = pts_ref.shape[0]
    block, me = lax.axis_index("leaf"), class_of()
    base = block * leaves - span
    copies = [
        pltpu.make_async_copy(own_ref, own_buf, sems.at[0]),
        pltpu.make_async_copy(order_ref, order_buf, sems.at[1]),
        pltpu.make_async_copy(skel_ref, skel_buf, sems.at[2]),
    ]
    for j in range(mine):
        leaf = j * classes + me
        copies.append(pltpu.make_async_copy(interp_ref.at[leaf], interp_buf.at[j], sems.at[3 + 2 * j]))
        copies.append(pltpu.make_async_copy(pts_ref.at[leaf], pts_buf.at[j], sems.at[4 + 2 * j]))
    for copy in copies:
        copy.start()
    for e in range(cnt_ref.shape[0]):
        wanted = base + e * classes + me
        total = None
        for ref in pair_refs:
            part = jnp.sum(jnp.where(ref[:near_n] == wanted, 1, 0), axis=0, keepdims=True)
            total = part if total is None else total + part
        cnt_ref[e : e + 1] = total
    far_n = far_ref.shape[0] // len(pair_refs)
    for k, ref in enumerate(pair_refs):
        named = ref[near_n:]
        owner = lax.div(named, leaves)
        within = lax.rem(named, leaves)
        piece = lax.rem(block - owner + blocks, blocks) - 1
        target = lax.broadcasted_iota(jnp.int32, named.shape, 1)
        code = target * 256 + piece * mine + lax.div(within, classes)
        far_ref[k * far_n : (k + 1) * far_n] = jnp.where(lax.rem(within, classes) == me, code, -1)

    copies[0].wait()
    copies[1].wait()
    for hi in range(turns):
        span = slice(hi * width, (hi + 1) * width)
        stack[hi * step : hi * step + cols] = own_buf[:, span]
        stack[hi * step + cols : (hi + 1) * step] = other_ref[:, span]
    orders = {}
    for j in range(mine):
        leaf = j * classes + me
        ids = order_buf[:, pl.ds(pl.multiple_of(leaf * size, size), size)]
        hi_ids = lax.shift_right_logical(ids, width.bit_length() - 1)
        picked = dot(stack[...], one_hot(ids & (width - 1), width))
        total = jnp.zeros((step, size), F32)
        for hi in range(turns):
            total = total + jnp.where(hi_ids == hi, picked[hi * step : (hi + 1) * step], 0.0)
        tw_ref[j] = total.astype(BF)
    for copy in copies[2:]:
        copy.wait()
    for j in range(mine):
        hots[j] = one_hot(skel_buf[pl.ds(j * classes + me, 1), :], size)
    skel_ps = [dot(pts_buf[j], hots[j, :, :rank]).astype(BF) for j in range(mine)]
    ordereds = [dot(tw_ref[j], hots[j]) for j in range(mine)]
    combineds = [dot_last(ordereds[j][:, rank:].astype(BF), interp_buf[j]) for j in range(mine)]
    for j in range(mine):
        leaf = j * classes + me
        tree = tw_ref[j]
        skel_p = skel_ps[j]
        skel_w = (ordereds[j][:, :rank] + combineds[j]).astype(BF)
        for ref, low, high in ((up_ref, 0, mine - halo), (mid_ref, 0, mine), (down_ref, halo, mine)):
            weights_at, halo_at = (high - low) * dim, (high - low) * dim + mine * step
            if low <= j < high:
                ref[(j - low) * dim : (j - low + 1) * dim] = skel_p
            elif ref is not mid_ref:
                place = j - (mine - halo) if low == 0 else j
                for cut in range(cuts):
                    at = halo_at + (place * cuts + cut) * step
                    ref[at : at + step] = tree[:, cut * rank : (cut + 1) * rank]
                row = lax.broadcasted_iota(jnp.int32, (EXTRA, rank), 0)
                picks = skel_buf[pl.ds(leaf, 1), :rank]
                high_half = jnp.where(row == 2 * place, lax.shift_right_logical(picks, 8), 0)
                halves = jnp.where(row == 2 * place + 1, picks & 255, high_half).astype(F32)
                before = orders.get(id(ref))
                orders[id(ref)] = halves if before is None else before + halves
                ref[halo_at + halo * cuts * step :] = orders[id(ref)].astype(BF)
            ref[weights_at + j * step : weights_at + (j + 1) * step] = skel_w


def list_named(t, first, count, cnt_ref, slots, at):
    found = jnp.int32(0)
    for e in range(count):
        slots[at + found] = jnp.int32(e)
        found = found + jnp.where(cnt_ref[first + e, t] > 0, 1, 0)
    return found


def named_block(t, k, scale, slots, at, tgt, src, shift):
    names = [slots[at + j] for j in range(k)]
    return names, gauss(jnp.concatenate([src[s + shift] for s in names], axis=0), tgt[t], scale) if k else None


def named_product(t, first, cnt_ref, names, block, weights, shift, wide):
    total = jnp.zeros((weights.shape[1], wide), F32) if not names else None
    for j, s in enumerate(names):
        size = weights.shape[2]
        times = cnt_ref[first + s, t].astype(F32)
        part = dot(weights[s + shift], block[j * size : (j + 1) * size]) * times
        total = part if total is None else total + part
    return total


def named_sum(t, k, first, scale, cnt_ref, slots, at, tgt, src, weights, shift):
    names, block = named_block(t, k, scale, slots, at, tgt, src, shift)
    return named_product(t, first, cnt_ref, names, block, weights, shift, tgt.shape[2])


def near_body(
    halo, scale, cnt_ref, pts_ref, tw_ref, left_p, right_p, skel_ref,
    near_ref, tgt_ref, edge_src, far_tgt_ref, src, slots,
):
    leaves, _, size = pts_ref.shape
    mine = tw_ref.shape[0]
    classes = leaves // mine
    rank = far_tgt_ref.shape[2]

    def sources(j, _):
        src[j] = as_sources(pts_ref[j * classes + class_of()])
        return 0

    lax.fori_loop(0, mine, sources, 0)
    tgt_ref[0] = as_targets(pts_ref[0])

    def target(t, _):
        found = list_named(t, halo, mine, cnt_ref, slots, 0)
        for k in range(mine + 1):

            @pl.when(found == k)
            def _():
                total = named_sum(t, k, halo, scale, cnt_ref, slots, 0, tgt_ref, src, tw_ref, 0)
                hot = one_hot(skel_ref[pl.ds(t, 1), :rank], size)
                far_tgt = as_targets(dot(pts_ref[t], hot).astype(BF))
                later = jnp.minimum(t + 1, leaves - 1)
                following = as_targets(pts_ref[later])
                near_ref[t] = total
                far_tgt_ref[t] = far_tgt
                tgt_ref[later] = following

        return 0

    lax.fori_loop(0, leaves, target, 0)
    for j in range(halo):
        edge_src[j] = as_sources(left_p[j])
        edge_src[halo + j] = as_sources(right_p[j])


def edge_body(
    halo, mine, rank, scale, cnt_ref, near_ref, tgt_ref, src, left_m, right_m, own_ref, other_ref, wts, slots
):
    leaves, cols2, size = near_ref.shape
    cols = cols2 // 2
    quarter = leaves // 4
    cuts = size // rank
    for side, message in enumerate((left_m, right_m)):
        for j in range(halo):
            for cut in range(cuts):
                at = message.shape[0] - EXTRA - (halo * cuts - j * cuts - cut) * cols2
                wts[side * halo + j, :, cut * rank : (cut + 1) * rank] = message[at : at + cols2]

    def targets(i, _):
        right = lax.div(i, quarter)
        first = right * (halo + mine)
        pair = (right * quarter + i, right * quarter + i + quarter)
        founds = [list_named(t, first, halo, cnt_ref, slots, n * (halo + 1)) for n, t in enumerate(pair)]
        for k in range((halo + 1) ** 2):
            counts = divmod(k, halo + 1)

            @pl.when((founds[0] == counts[0]) & (founds[1] == counts[1]))
            def _():
                blocks = [
                    named_block(t, c, scale, slots, n * (halo + 1), tgt_ref, src, right * halo)
                    for n, (t, c) in enumerate(zip(pair, counts))
                ]
                sums = [
                    named_product(t, first, cnt_ref, names, block, wts, right * halo, size)
                    for t, (names, block) in zip(pair, blocks)
                ]
                totals = [near_ref[t] + part for t, part in zip(pair, sums)]
                for t, total in zip(pair, totals):
                    span = pl.ds(pl.multiple_of(t * size, size), size)
                    own_ref[:, span] = total[:cols]
                    other_ref[:, span] = total[cols:].astype(BF)

        return 0

    lax.fori_loop(0, 2 * quarter, targets, 0)


def sources_body(mine, left_p, right_p, *refs):
    pieces = refs[:-2]
    far_src, far_w = refs[-2:]
    halo, dim, size = left_p.shape
    _, cols2, rank = far_w.shape
    for k, piece in enumerate(pieces):
        low, high, points = 0, mine, None
        if k == 0:
            high, points = mine - halo, left_p
        elif k == len(pieces) - 1:
            low, points = halo, right_p
        weights_at = (high - low) * dim
        for j in range(mine):
            if low <= j < high:
                skel_p = piece[(j - low) * dim : (j - low + 1) * dim]
            else:
                place = j - (mine - halo) if k == 0 else j
                order = piece[piece.shape[0] - EXTRA :].astype(F32)
                picks = (order[2 * place : 2 * place + 1] * 256.0 + order[2 * place + 1 : 2 * place + 2]).astype(jnp.int32)
                skel_p = dot(points[place], one_hot(picks, size)).astype(BF)
            far_src[k * mine + j] = as_sources(skel_p)
            far_w[k * mine + j] = piece[weights_at + j * cols2 : weights_at + (j + 1) * cols2]


def sum_body(own_ref, back_ref, *refs):
    first_ref, last_ref = refs[-2:]
    half = first_ref.shape[1]
    for ref, span in ((first_ref, slice(0, half)), (last_ref, slice(half, 2 * half))):
        ref[...] = (own_ref[:, span] + back_ref[:, span].astype(F32)).astype(BF)


def far_body(scale, far_ref, far_src, far_w, far_tgt, after_ref, own_ref, other_ref, field, names):
    found = jnp.int32(0)
    for t in range(far_ref.shape[1]):
        for i in range(far_ref.shape[0]):
            code = far_ref[i, t]
            names[1 + found] = code
            found = found + jnp.where(code >= 0, 1, 0)
    names[0] = found
    for j in range(GROUP):
        names[1 + found + j] = jnp.int32(far_ref.shape[1] * 256)
    leaves, _, rank = far_tgt.shape
    cols = own_ref.shape[0]
    field[...] = jnp.zeros_like(field)

    def far_group(g, _):
        codes = [names[1 + g * GROUP + j] for j in range(GROUP)]
        targets = [lax.shift_right_logical(c, 8) for c in codes]
        blocks = [gauss(far_src[c & 255], far_tgt[t & (leaves - 1)], scale) for c, t in zip(codes, targets)]
        parts = [dot(far_w[c & 255], block) for c, block in zip(codes, blocks)]
        for t, part in zip(targets, parts):
            field[t] += part
        return 0

    lax.fori_loop(0, lax.div(names[0] + GROUP - 1, GROUP), far_group, 0)
    for t in range(leaves):
        own_ref[:, t * rank : (t + 1) * rank] = field[t, :cols]
        other_ref[:, t * rank : (t + 1) * rank] = field[t, cols:].astype(BF)


def scatter(ids, value, width, turns):
    hi_ids = lax.shift_right_logical(ids, width.bit_length() - 1)
    masked = [jnp.where(hi_ids == hi, value, 0.0).astype(BF) for hi in range(turns)]
    return dot_last(jnp.concatenate(masked, axis=0), one_hot(ids & (width - 1), width))


def place_near_body(order_ref, *refs):
    near, acc = refs[:-1], refs[-1]
    total = order_ref.shape[1]
    width = acc.shape[1]
    chunk = 1024
    for at in range(0, total, chunk):
        span = slice(at, at + chunk)
        value = sum(ref[:, span].astype(F32) for ref in near)
        part = scatter(order_ref[:, span], value, width, total // width)
        acc[...] = part if at == 0 else acc[...] + part


def comp_body(order_ref, skel_ref, comp_ref):
    leaves, size = skel_ref.shape
    for t in range(leaves):
        span = slice(t * size, (t + 1) * size)
        ids = order_ref[:, span]
        row = lax.broadcasted_iota(jnp.int32, (16, size), 0)
        halves = jnp.where(row == 0, lax.shift_right_logical(ids, 8), jnp.where(row == 1, ids & 255, 0))
        moved = dot(halves.astype(F32).astype(BF), one_hot(skel_ref[t : t + 1], size))
        comp_ref[:, span] = (moved[:1] * 256.0 + moved[1:2]).astype(jnp.int32)


def place_far(first, comp_ref, interp_ref, start_ref, far, acc, buf):
    cols = far[0].shape[0]
    width = acc.shape[1]
    turns = acc.shape[0] // cols
    _, rank, rest = interp_ref.shape
    size = rank + rest
    for t in range(far[0].shape[1] // rank):
        skel = sum(ref[:, t * rank : (t + 1) * rank].astype(F32) for ref in far).astype(BF)
        buf[:, t * size : t * size + rank] = skel.astype(F32)
        buf[:, t * size + rank : (t + 1) * size] = dot(skel, interp_ref[first + t])
    chunk = 1024
    for at in range(0, buf.shape[1], chunk):
        ids = comp_ref[:, first * size + at : first * size + at + chunk]
        part = scatter(ids, buf[:, at : at + chunk], width, turns)
        acc[...] = (start_ref if at == 0 else acc)[...] + part


def place_first_body(comp_ref, interp_ref, start_ref, *refs):
    place_far(0, comp_ref, interp_ref, start_ref, refs[:-2], refs[-2], refs[-1])


def place_last_body(comp_ref, interp_ref, start_ref, *refs):
    far, out_ref, acc, buf = refs[:-3], refs[-3], refs[-2], refs[-1]
    place_far(interp_ref.shape[0] // 2, comp_ref, interp_ref, start_ref, far, acc, buf)
    cols, total = out_ref.shape
    width = acc.shape[1]
    for hi in range(total // width):
        out_ref[:, hi * width : (hi + 1) * width] = acc[hi * cols : (hi + 1) * cols]


def pin(value):
    return pltpu.with_memory_space_constraint(value, pltpu.HBM)


def ring(count, by):
    return [(i, (i + by) % count) for i in range(count)]


def from_others(value, axis):
    count = lax.axis_size(axis)
    return [lax.ppermute(value, axis, ring(count, by)) for by in range(1, count)]


def over_pair(value, pair_n):
    if pair_n == 2:
        return [value] + from_others(value, "pair")
    return list(lax.all_gather(value, "pair"))


def on_device(points, weights, interp, tree_order, skel_order, near_pairs, far_pairs):
    leaves, size, dim = points.shape
    rank = interp.shape[1]
    cols = weights.shape[1]
    blocks, pair_n, rhs_n = (lax.axis_size(a) for a in ("leaf", "pair", "rhs"))
    classes = pair_n * rhs_n
    mine = leaves // classes
    span = min(8, leaves)
    halo = span // classes
    scale = 2.0 * 2.5 / dim * LOG2E
    near_n, far_n = near_pairs.shape[1], far_pairs.shape[1]
    wide = dim + EXTRA
    mega = 10 ** 9
    pts = points.transpose(0, 2, 1)
    wts = weights.T
    (other_wts,) = from_others(wts, "rhs")
    hbm = pl.BlockSpec(memory_space=pltpu.HBM)
    up_p, down_p, pairs = call(
        functools.partial(halo_body, classes),
        [((halo, dim, size), BF), ((halo, dim, size), BF), ((near_n + far_n, leaves), jnp.int32)],
        [hbm, hbm, hbm],
        (pin(pts), pin(near_pairs.T), pin(far_pairs.T)),
        [
            pltpu.VMEM((near_n, leaves), jnp.int32),
            pltpu.VMEM((far_n, leaves), jnp.int32),
            pltpu.SemaphoreType.DMA((2 * halo + 2,)),
        ],
        out_specs=[hbm, hbm, VMEM],
        grant=48,
    )
    every = [pairs] + from_others(pairs, "pair")
    left_p = lax.ppermute(up_p, "leaf", ring(blocks, 1))
    right_p = lax.ppermute(down_p, "leaf", ring(blocks, blocks - 1))
    tall = mine * (dim + 2 * cols)
    ends = tall - halo * dim + halo * (size // rank) * 2 * cols + EXTRA
    tree_w, up_m, mid_m, down_m, cnt, far_ids = call(
        functools.partial(weights_body, blocks, classes, near_n, span, halo),
        [
            ((mine, 2 * cols, size), BF),
            ((ends, rank), BF),
            ((tall, rank), BF),
            ((ends, rank), BF),
            ((2 * halo + mine, leaves), jnp.int32),
            ((pair_n * far_n, leaves), jnp.int32),
        ],
        [hbm, VMEM] + [hbm] * 4 + [VMEM] * pair_n,
        (pin(wts), other_wts, pin(tree_order), pin(skel_order), pin(interp), pin(pts), *every),
        [
            pltpu.VMEM((2 * cols * (leaves * size // 256), 256), BF),
            pltpu.VMEM((cols, leaves * size), BF),
            pltpu.VMEM((1, leaves * size), jnp.int32),
            pltpu.VMEM((leaves, size), jnp.int32),
            pltpu.VMEM((mine, rank, size - rank), BF),
            pltpu.VMEM((mine, dim, size), BF),
            pltpu.VMEM((mine, size, size), BF),
            pltpu.SemaphoreType.DMA((3 + 2 * mine,)),
        ],
        flops=3 * mega,
        grant=48,
    )
    outgoing = {by: mid_m for by in range(1, blocks)} | {1: up_m, blocks - 1: down_m}
    pieces = [lax.ppermute(outgoing[by], "leaf", ring(blocks, by)) for by in range(1, blocks)]
    near, tgt, edge_src, far_tgt = call(
        functools.partial(near_body, halo, scale),
        [
            ((leaves, 2 * cols, size), F32),
            ((leaves, wide, size), BF),
            ((2 * halo, size, wide), BF),
            ((leaves, wide, rank), BF),
        ],
        [SMEM] + [VMEM] * 5,
        (cnt, pts, tree_w, left_p, right_p, skel_order),
        [pltpu.VMEM((mine, size, wide), BF), pltpu.SMEM((mine + 1,), jnp.int32)],
        flops=14 * mega,
    )

    near_own, near_other = call(
        functools.partial(edge_body, halo, mine, rank, scale),
        [((cols, leaves * size), F32), ((cols, leaves * size), BF)],
        [SMEM] + [VMEM] * 5,
        (cnt, near, tgt, edge_src, pieces[0], pieces[-1]),
        [pltpu.VMEM((2 * halo, 2 * cols, size), BF), pltpu.SMEM((2 * halo + 2,), jnp.int32)],
        flops=6 * mega,
    )
    (near_back,) = from_others(near_other, "rhs")
    near_sum_own = (near_own + near_back.astype(F32)).astype(BF)
    near_parts = over_pair(near_sum_own, pair_n)
    piece_n = (blocks - 1) * mine
    far_src, far_w = call(
        functools.partial(sources_body, mine),
        [((piece_n, rank, wide), BF), ((piece_n, 2 * cols, rank), BF)],
        [VMEM] * (blocks + 1),
        (left_p, right_p, *pieces),
        flops=2 * mega,
    )
    far_own, far_other = call(
        functools.partial(far_body, scale),
        [((cols, leaves * rank), F32), ((cols, leaves * rank), BF)],
        [SMEM, VMEM, VMEM, VMEM, pl.BlockSpec(memory_space=pl.ANY)],
        (far_ids, far_src, far_w, far_tgt, near_sum_own),
        [pltpu.VMEM((leaves + 1, 2 * cols, rank), F32), pltpu.SMEM((leaves * pair_n * far_n + 16,), jnp.int32)],
        flops=4 * mega,
    )
    (far_back,) = from_others(far_other, "rhs")
    (comp,) = call(
        comp_body, [((1, leaves * size), jnp.int32)], [VMEM] * 2, (tree_order, skel_order), flops=mega
    )
    halves = call(
        sum_body,
        [((cols, leaves // 2 * rank), BF)] * 2,
        [VMEM, VMEM] + [pl.BlockSpec(memory_space=pl.ANY)] * pair_n,
        (far_own, far_back, comp, *near_parts[1:]),
    )
    first_parts, last_parts = (over_pair(half, pair_n) for half in halves)
    acc_shape = (leaves * size // 256 * cols, 256)
    (acc,) = call(
        place_near_body,
        [(acc_shape, F32)],
        [VMEM] * (1 + pair_n),
        (tree_order, *near_parts),
        flops=3 * mega,
    )
    (acc,) = call(
        place_first_body,
        [(acc_shape, F32)],
        [VMEM] * (3 + pair_n),
        (comp, interp, acc, *first_parts),
        [pltpu.VMEM((cols, leaves // 2 * size), F32)],
        flops=2 * mega,
    )
    (out,) = call(
        place_last_body,
        [((cols, leaves * size), F32)],
        [VMEM] * (3 + pair_n),
        (comp, interp, acc, *last_parts),
        [pltpu.VMEM(acc_shape, F32), pltpu.VMEM((cols, leaves // 2 * size), F32)],
        flops=2 * mega,
    )
    return out.T


def solution(mesh):
    return jax.shard_map(
        on_device,
        mesh=mesh,
        in_specs=(
            P(("groups", "leaf"), None, None),
            P(("groups", "leaf"), "rhs"),
            P(("groups", "leaf"), None, None),
            P(("groups", "leaf"), None),
            P(("groups", "leaf"), None),
            P(("groups", "leaf"), "pair"),
            P(("groups", "leaf"), "pair"),
        ),
        out_specs=P(("groups", "leaf"), "rhs"),
        check_vma=False,
    )
```

```python
import functools

import jax
import jax.numpy as jnp
from jax import lax
from jax.experimental import pallas as pl
from jax.experimental.pallas import tpu as pltpu
from jax.sharding import PartitionSpec as P

BF = jnp.bfloat16
F32 = jnp.float32
LOG2E = 1.4426950408889634
EXTRA = 16
GROUP = 8
VMEM = pl.BlockSpec(memory_space=pltpu.VMEM)
SMEM = pl.BlockSpec(memory_space=pltpu.SMEM)


def call(body, shapes, specs, args, scratch=(), flops=0, out_specs=None, grant=48):
    outs = [jax.ShapeDtypeStruct(s, d) for s, d in shapes]
    return pl.pallas_call(
        body,
        out_shape=outs,
        in_specs=specs,
        out_specs=out_specs or [VMEM] * len(outs),
        scratch_shapes=list(scratch),
        compiler_params=pltpu.CompilerParams(vmem_limit_bytes=grant << 20),
        cost_estimate=pl.CostEstimate(flops=flops, bytes_accessed=1 << 20, transcendentals=0),
    )(*args)


def extra_rows(feat, ones_first):
    wide = feat.astype(F32)
    half = -0.5 * jnp.sum(wide * wide, axis=0, keepdims=True)
    high = half.astype(BF).astype(F32)
    mid = (half - high).astype(BF).astype(F32)
    low = half - high - mid
    row = lax.broadcasted_iota(jnp.int32, (EXTRA, feat.shape[1]), 0)
    at = 3 if ones_first else 0
    ones = (row < 3) if ones_first else (row >= 3) & (row < 6)
    picked = jnp.where(row == at, high, jnp.where(row == at + 1, mid, jnp.where(row == at + 2, low, 0.0)))
    return jnp.where(ones, 1.0, picked).astype(BF)


def as_targets(feat):
    return jnp.concatenate([feat, extra_rows(feat, False)], axis=0)


def as_sources(feat):
    return jnp.concatenate([feat, extra_rows(feat, True)], axis=0).astype(F32).T.astype(BF)


def one_hot(row_ids, count):
    rows = lax.broadcasted_iota(jnp.int32, (count, row_ids.shape[1]), 0)
    return jnp.where(rows == row_ids, 1.0, 0.0).astype(BF)


def dot(a, b):
    return jnp.dot(a, b, preferred_element_type=F32)


def dot_last(a, b):
    return lax.dot_general(a, b, (((1,), (1,)), ((), ())), preferred_element_type=F32)


def gauss(sources, targets, scale):
    return jnp.exp2(dot(sources, targets) * scale).astype(BF)


def class_of():
    return lax.axis_index("pair") * lax.axis_size("rhs") + lax.axis_index("rhs")


def halo_body(classes, pts_ref, near_ref, far_ref, up_ref, down_ref, pairs_ref, near_buf, far_buf, sems):
    halo = up_ref.shape[0]
    half = pts_ref.shape[0] // 2
    copies = [
        pltpu.make_async_copy(near_ref, near_buf, sems.at[2 * halo]),
        pltpu.make_async_copy(far_ref, far_buf, sems.at[2 * halo + 1]),
    ]
    for j in range(halo):
        leaf = class_of() + j * classes
        copies.append(pltpu.make_async_copy(pts_ref.at[leaf + half], up_ref.at[j], sems.at[j]))
        copies.append(pltpu.make_async_copy(pts_ref.at[leaf], down_ref.at[j], sems.at[halo + j]))
    for copy in copies:
        copy.start()
    for copy in copies:
        copy.wait()
    near_n = near_ref.shape[0]
    pairs_ref[:near_n] = near_buf[...]
    pairs_ref[near_n:] = far_buf[...]


def weights_body(
    blocks, classes, near_n, span, halo, own_ref, other_ref, order_ref, skel_ref, interp_ref, pts_ref, *refs
):
    pair_refs = refs[:-14]
    tw_ref, up_ref, mid_ref, down_ref, cnt_ref, far_ref = refs[-14:-8]
    stack, own_buf, order_buf, skel_buf, interp_buf, pts_buf, hots, sems = refs[-8:]
    cols = own_ref.shape[0]
    step = 2 * cols
    width = stack.shape[1]
    turns = own_ref.shape[1] // width
    mine, _, size = tw_ref.shape
    rank = mid_ref.shape[1]
    dim = pts_ref.shape[1]
    cuts = size // rank
    leaves = pts_ref.shape[0]
    block, me = lax.axis_index("leaf"), class_of()
    base = block * leaves - span
    copies = [
        pltpu.make_async_copy(own_ref, own_buf, sems.at[0]),
        pltpu.make_async_copy(order_ref, order_buf, sems.at[1]),
        pltpu.make_async_copy(skel_ref, skel_buf, sems.at[2]),
    ]
    for j in range(mine):
        leaf = j * classes + me
        copies.append(pltpu.make_async_copy(interp_ref.at[leaf], interp_buf.at[j], sems.at[3 + 2 * j]))
        copies.append(pltpu.make_async_copy(pts_ref.at[leaf], pts_buf.at[j], sems.at[4 + 2 * j]))
    for copy in copies:
        copy.start()
    for e in range(cnt_ref.shape[0]):
        wanted = base + e * classes + me
        total = None
        for ref in pair_refs:
            part = jnp.sum(jnp.where(ref[:near_n] == wanted, 1, 0), axis=0, keepdims=True)
            total = part if total is None else total + part
        cnt_ref[e : e + 1] = total
    far_n = far_ref.shape[0] // len(pair_refs)
    for k, ref in enumerate(pair_refs):
        named = ref[near_n:]
        owner = lax.div(named, leaves)
        within = lax.rem(named, leaves)
        piece = lax.rem(block - owner + blocks, blocks) - 1
        target = lax.broadcasted_iota(jnp.int32, named.shape, 1)
        code = target * 256 + piece * mine + lax.div(within, classes)
        far_ref[k * far_n : (k + 1) * far_n] = jnp.where(lax.rem(within, classes) == me, code, -1)

    copies[0].wait()
    copies[1].wait()
    for hi in range(turns):
        span = slice(hi * width, (hi + 1) * width)
        stack[hi * step : hi * step + cols] = own_buf[:, span]
        stack[hi * step + cols : (hi + 1) * step] = other_ref[:, span]
    orders = {}
    for j in range(mine):
        leaf = j * classes + me
        ids = order_buf[:, pl.ds(pl.multiple_of(leaf * size, size), size)]
        hi_ids = lax.shift_right_logical(ids, width.bit_length() - 1)
        picked = dot(stack[...], one_hot(ids & (width - 1), width))
        total = jnp.zeros((step, size), F32)
        for hi in range(turns):
            total = total + jnp.where(hi_ids == hi, picked[hi * step : (hi + 1) * step], 0.0)
        tw_ref[j] = total.astype(BF)
    for copy in copies[2:]:
        copy.wait()
    for j in range(mine):
        hots[j] = one_hot(skel_buf[pl.ds(j * classes + me, 1), :], size)
    skel_ps = [dot(pts_buf[j], hots[j, :, :rank]).astype(BF) for j in range(mine)]
    ordereds = [dot(tw_ref[j], hots[j]) for j in range(mine)]
    combineds = [dot_last(ordereds[j][:, rank:].astype(BF), interp_buf[j]) for j in range(mine)]
    for j in range(mine):
        leaf = j * classes + me
        tree = tw_ref[j]
        skel_p = skel_ps[j]
        skel_w = (ordereds[j][:, :rank] + combineds[j]).astype(BF)
        for ref, low, high in ((up_ref, 0, mine - halo), (mid_ref, 0, mine), (down_ref, halo, mine)):
            weights_at, halo_at = (high - low) * dim, (high - low) * dim + mine * step
            if low <= j < high:
                ref[(j - low) * dim : (j - low + 1) * dim] = skel_p
            elif ref is not mid_ref:
                place = j - (mine - halo) if low == 0 else j
                for cut in range(cuts):
                    at = halo_at + (place * cuts + cut) * step
                    ref[at : at + step] = tree[:, cut * rank : (cut + 1) * rank]
                row = lax.broadcasted_iota(jnp.int32, (EXTRA, rank), 0)
                picks = skel_buf[pl.ds(leaf, 1), :rank]
                high_half = jnp.where(row == 2 * place, lax.shift_right_logical(picks, 8), 0)
                halves = jnp.where(row == 2 * place + 1, picks & 255, high_half).astype(F32)
                before = orders.get(id(ref))
                orders[id(ref)] = halves if before is None else before + halves
                ref[halo_at + halo * cuts * step :] = orders[id(ref)].astype(BF)
            ref[weights_at + j * step : weights_at + (j + 1) * step] = skel_w


def list_named(t, first, count, cnt_ref, slots, at):
    found = jnp.int32(0)
    for e in range(count):
        slots[at + found] = jnp.int32(e)
        found = found + jnp.where(cnt_ref[first + e, t] > 0, 1, 0)
    return found


def named_block(t, k, scale, slots, at, tgt, src, shift):
    names = [slots[at + j] for j in range(k)]
    return names, gauss(jnp.concatenate([src[s + shift] for s in names], axis=0), tgt[t], scale) if k else None


def named_product(t, first, cnt_ref, names, block, weights, shift, wide):
    total = jnp.zeros((weights.shape[1], wide), F32) if not names else None
    for j, s in enumerate(names):
        size = weights.shape[2]
        times = cnt_ref[first + s, t].astype(F32)
        part = dot(weights[s + shift], block[j * size : (j + 1) * size]) * times
        total = part if total is None else total + part
    return total


def near_body(
    halo, scale, cnt_ref, pts_ref, tw_ref, left_p, right_p, skel_ref,
    near_ref, tgt_ref, edge_src, far_tgt_ref, src, slots,
):
    leaves, _, size = pts_ref.shape
    mine = tw_ref.shape[0]
    classes = leaves // mine
    rank = far_tgt_ref.shape[2]

    def sources(j, _):
        src[j] = as_sources(pts_ref[j * classes + class_of()])
        return 0

    lax.fori_loop(0, mine, sources, 0)
    tgt_ref[0] = as_targets(pts_ref[0])

    def target(t, _):
        found = list_named(t, halo, mine, cnt_ref, slots, 0)
        for k in range(mine + 1):

            @pl.when(found == k)
            def _():
                names, block = named_block(t, k, scale, slots, 0, tgt_ref, src, 0)
                hot = one_hot(skel_ref[pl.ds(t, 1), :rank], size)
                far_tgt = as_targets(dot(pts_ref[t], hot).astype(BF))
                later = jnp.minimum(t + 1, leaves - 1)
                following = as_targets(pts_ref[later])
                near_ref[t] = named_product(t, halo, cnt_ref, names, block, tw_ref, 0, size)
                far_tgt_ref[t] = far_tgt
                tgt_ref[later] = following

        return 0

    lax.fori_loop(0, leaves, target, 0)
    for j in range(halo):
        edge_src[j] = as_sources(left_p[j])
        edge_src[halo + j] = as_sources(right_p[j])


def edge_body(
    halo, mine, rank, scale, cnt_ref, near_ref, tgt_ref, src, left_m, right_m, own_ref, other_ref, wts, slots
):
    leaves, cols2, size = near_ref.shape
    cols = cols2 // 2
    quarter = leaves // 4
    cuts = size // rank
    for side, message in enumerate((left_m, right_m)):
        for j in range(halo):
            for cut in range(cuts):
                at = message.shape[0] - EXTRA - (halo * cuts - j * cuts - cut) * cols2
                wts[side * halo + j, :, cut * rank : (cut + 1) * rank] = message[at : at + cols2]

    def targets(i, _):
        right = lax.div(i, quarter)
        first = right * (halo + mine)
        pair = (right * quarter + i, right * quarter + i + quarter)
        founds = [list_named(t, first, halo, cnt_ref, slots, n * (halo + 1)) for n, t in enumerate(pair)]
        for k in range((halo + 1) ** 2):
            counts = divmod(k, halo + 1)

            @pl.when((founds[0] == counts[0]) & (founds[1] == counts[1]))
            def _():
                blocks = [
                    named_block(t, c, scale, slots, n * (halo + 1), tgt_ref, src, right * halo)
                    for n, (t, c) in enumerate(zip(pair, counts))
                ]
                sums = [
                    named_product(t, first, cnt_ref, names, block, wts, right * halo, size)
                    for t, (names, block) in zip(pair, blocks)
                ]
                totals = [near_ref[t] + part for t, part in zip(pair, sums)]
                for t, total in zip(pair, totals):
                    span = pl.ds(pl.multiple_of(t * size, size), size)
                    own_ref[:, span] = total[:cols]
                    other_ref[:, span] = total[cols:].astype(BF)

        return 0

    lax.fori_loop(0, 2 * quarter, targets, 0)


def sources_body(mine, left_p, right_p, *refs):
    pieces = refs[:-2]
    far_src, far_w = refs[-2:]
    halo, dim, size = left_p.shape
    _, cols2, rank = far_w.shape
    for k, piece in enumerate(pieces):
        low, high, points = 0, mine, None
        if k == 0:
            high, points = mine - halo, left_p
        elif k == len(pieces) - 1:
            low, points = halo, right_p
        weights_at = (high - low) * dim
        for j in range(mine):
            if low <= j < high:
                skel_p = piece[(j - low) * dim : (j - low + 1) * dim]
            else:
                place = j - (mine - halo) if k == 0 else j
                order = piece[piece.shape[0] - EXTRA :].astype(F32)
                picks = (order[2 * place : 2 * place + 1] * 256.0 + order[2 * place + 1 : 2 * place + 2]).astype(jnp.int32)
                skel_p = dot(points[place], one_hot(picks, size)).astype(BF)
            far_src[k * mine + j] = as_sources(skel_p)
            far_w[k * mine + j] = piece[weights_at + j * cols2 : weights_at + (j + 1) * cols2]


def sum_body(own_ref, back_ref, *refs):
    first_ref, last_ref = refs[-2:]
    half = first_ref.shape[1]
    for ref, span in ((first_ref, slice(0, half)), (last_ref, slice(half, 2 * half))):
        ref[...] = (own_ref[:, span] + back_ref[:, span].astype(F32)).astype(BF)


def far_body(scale, far_ref, far_src, far_w, far_tgt, after_ref, own_ref, other_ref, field, names):
    found = jnp.int32(0)
    for t in range(far_ref.shape[1]):
        for i in range(far_ref.shape[0]):
            code = far_ref[i, t]
            names[1 + found] = code
            found = found + jnp.where(code >= 0, 1, 0)
    names[0] = found
    for j in range(GROUP):
        names[1 + found + j] = jnp.int32(far_ref.shape[1] * 256)
    leaves, _, rank = far_tgt.shape
    cols = own_ref.shape[0]
    field[...] = jnp.zeros_like(field)

    def far_group(g, _):
        codes = [names[1 + g * GROUP + j] for j in range(GROUP)]
        targets = [lax.shift_right_logical(c, 8) for c in codes]
        blocks = [gauss(far_src[c & 255], far_tgt[t & (leaves - 1)], scale) for c, t in zip(codes, targets)]
        parts = [dot(far_w[c & 255], block) for c, block in zip(codes, blocks)]
        for t, part in zip(targets, parts):
            field[t] += part
        return 0

    lax.fori_loop(0, lax.div(names[0] + GROUP - 1, GROUP), far_group, 0)
    for t in range(leaves):
        own_ref[:, t * rank : (t + 1) * rank] = field[t, :cols]
        other_ref[:, t * rank : (t + 1) * rank] = field[t, cols:].astype(BF)


def scatter(ids, value, width, turns):
    hi_ids = lax.shift_right_logical(ids, width.bit_length() - 1)
    masked = [jnp.where(hi_ids == hi, value, 0.0).astype(BF) for hi in range(turns)]
    return dot_last(jnp.concatenate(masked, axis=0), one_hot(ids & (width - 1), width))


def place_near_body(order_ref, *refs):
    near, acc = refs[:-1], refs[-1]
    total = order_ref.shape[1]
    width = acc.shape[1]
    chunk = 1024
    for at in range(0, total, chunk):
        span = slice(at, at + chunk)
        value = sum(ref[:, span].astype(F32) for ref in near)
        part = scatter(order_ref[:, span], value, width, total // width)
        acc[...] = part if at == 0 else acc[...] + part


def comp_body(order_ref, skel_ref, comp_ref):
    leaves, size = skel_ref.shape
    for t in range(leaves):
        span = slice(t * size, (t + 1) * size)
        ids = order_ref[:, span]
        row = lax.broadcasted_iota(jnp.int32, (16, size), 0)
        halves = jnp.where(row == 0, lax.shift_right_logical(ids, 8), jnp.where(row == 1, ids & 255, 0))
        moved = dot(halves.astype(F32).astype(BF), one_hot(skel_ref[t : t + 1], size))
        comp_ref[:, span] = (moved[:1] * 256.0 + moved[1:2]).astype(jnp.int32)


def place_far(first, comp_ref, interp_ref, start_ref, far, acc, buf):
    cols = far[0].shape[0]
    width = acc.shape[1]
    turns = acc.shape[0] // cols
    _, rank, rest = interp_ref.shape
    size = rank + rest
    for t in range(far[0].shape[1] // rank):
        skel = sum(ref[:, t * rank : (t + 1) * rank].astype(F32) for ref in far).astype(BF)
        buf[:, t * size : t * size + rank] = skel.astype(F32)
        buf[:, t * size + rank : (t + 1) * size] = dot(skel, interp_ref[first + t])
    chunk = 1024
    for at in range(0, buf.shape[1], chunk):
        ids = comp_ref[:, first * size + at : first * size + at + chunk]
        part = scatter(ids, buf[:, at : at + chunk], width, turns)
        acc[...] = (start_ref if at == 0 else acc)[...] + part


def place_first_body(comp_ref, interp_ref, start_ref, *refs):
    place_far(0, comp_ref, interp_ref, start_ref, refs[:-2], refs[-2], refs[-1])


def place_last_body(comp_ref, interp_ref, start_ref, *refs):
    far, out_ref, acc, buf = refs[:-3], refs[-3], refs[-2], refs[-1]
    place_far(interp_ref.shape[0] // 2, comp_ref, interp_ref, start_ref, far, acc, buf)
    cols, total = out_ref.shape
    width = acc.shape[1]
    for hi in range(total // width):
        out_ref[:, hi * width : (hi + 1) * width] = acc[hi * cols : (hi + 1) * cols]


def pin(value):
    return pltpu.with_memory_space_constraint(value, pltpu.HBM)


def ring(count, by):
    return [(i, (i + by) % count) for i in range(count)]


def from_others(value, axis):
    count = lax.axis_size(axis)
    return [lax.ppermute(value, axis, ring(count, by)) for by in range(1, count)]


def over_pair(value, pair_n):
    if pair_n == 2:
        return [value] + from_others(value, "pair")
    return list(lax.all_gather(value, "pair"))


def on_device(points, weights, interp, tree_order, skel_order, near_pairs, far_pairs):
    leaves, size, dim = points.shape
    rank = interp.shape[1]
    cols = weights.shape[1]
    blocks, pair_n, rhs_n = (lax.axis_size(a) for a in ("leaf", "pair", "rhs"))
    classes = pair_n * rhs_n
    mine = leaves // classes
    span = min(8, leaves)
    halo = span // classes
    scale = 2.0 * 2.5 / dim * LOG2E
    near_n, far_n = near_pairs.shape[1], far_pairs.shape[1]
    wide = dim + EXTRA
    mega = 10 ** 9
    pts = points.transpose(0, 2, 1)
    wts = weights.T
    (other_wts,) = from_others(wts, "rhs")
    hbm = pl.BlockSpec(memory_space=pltpu.HBM)
    up_p, down_p, pairs = call(
        functools.partial(halo_body, classes),
        [((halo, dim, size), BF), ((halo, dim, size), BF), ((near_n + far_n, leaves), jnp.int32)],
        [hbm, hbm, hbm],
        (pin(pts), pin(near_pairs.T), pin(far_pairs.T)),
        [
            pltpu.VMEM((near_n, leaves), jnp.int32),
            pltpu.VMEM((far_n, leaves), jnp.int32),
            pltpu.SemaphoreType.DMA((2 * halo + 2,)),
        ],
        out_specs=[hbm, hbm, VMEM],
        grant=48,
    )
    every = [pairs] + from_others(pairs, "pair")
    left_p = lax.ppermute(up_p, "leaf", ring(blocks, 1))
    right_p = lax.ppermute(down_p, "leaf", ring(blocks, blocks - 1))
    tall = mine * (dim + 2 * cols)
    ends = tall - halo * dim + halo * (size // rank) * 2 * cols + EXTRA
    tree_w, up_m, mid_m, down_m, cnt, far_ids = call(
        functools.partial(weights_body, blocks, classes, near_n, span, halo),
        [
            ((mine, 2 * cols, size), BF),
            ((ends, rank), BF),
            ((tall, rank), BF),
            ((ends, rank), BF),
            ((2 * halo + mine, leaves), jnp.int32),
            ((pair_n * far_n, leaves), jnp.int32),
        ],
        [hbm, VMEM] + [hbm] * 4 + [VMEM] * pair_n,
        (pin(wts), other_wts, pin(tree_order), pin(skel_order), pin(interp), pin(pts), *every),
        [
            pltpu.VMEM((2 * cols * (leaves * size // 256), 256), BF),
            pltpu.VMEM((cols, leaves * size), BF),
            pltpu.VMEM((1, leaves * size), jnp.int32),
            pltpu.VMEM((leaves, size), jnp.int32),
            pltpu.VMEM((mine, rank, size - rank), BF),
            pltpu.VMEM((mine, dim, size), BF),
            pltpu.VMEM((mine, size, size), BF),
            pltpu.SemaphoreType.DMA((3 + 2 * mine,)),
        ],
        flops=3 * mega,
        grant=48,
    )
    outgoing = {by: mid_m for by in range(1, blocks)} | {1: up_m, blocks - 1: down_m}
    pieces = [lax.ppermute(outgoing[by], "leaf", ring(blocks, by)) for by in range(1, blocks)]
    near, tgt, edge_src, far_tgt = call(
        functools.partial(near_body, halo, scale),
        [
            ((leaves, 2 * cols, size), F32),
            ((leaves, wide, size), BF),
            ((2 * halo, size, wide), BF),
            ((leaves, wide, rank), BF),
        ],
        [SMEM] + [VMEM] * 5,
        (cnt, pts, tree_w, left_p, right_p, skel_order),
        [pltpu.VMEM((mine, size, wide), BF), pltpu.SMEM((mine + 1,), jnp.int32)],
        flops=14 * mega,
    )

    near_own, near_other = call(
        functools.partial(edge_body, halo, mine, rank, scale),
        [((cols, leaves * size), F32), ((cols, leaves * size), BF)],
        [SMEM] + [VMEM] * 5,
        (cnt, near, tgt, edge_src, pieces[0], pieces[-1]),
        [pltpu.VMEM((2 * halo, 2 * cols, size), BF), pltpu.SMEM((2 * halo + 2,), jnp.int32)],
        flops=6 * mega,
    )
    (near_back,) = from_others(near_other, "rhs")
    near_sum_own = (near_own + near_back.astype(F32)).astype(BF)
    near_parts = over_pair(near_sum_own, pair_n)
    piece_n = (blocks - 1) * mine
    far_src, far_w = call(
        functools.partial(sources_body, mine),
        [((piece_n, rank, wide), BF), ((piece_n, 2 * cols, rank), BF)],
        [VMEM] * (blocks + 1),
        (left_p, right_p, *pieces),
        flops=2 * mega,
    )
    far_own, far_other = call(
        functools.partial(far_body, scale),
        [((cols, leaves * rank), F32), ((cols, leaves * rank), BF)],
        [SMEM, VMEM, VMEM, VMEM, pl.BlockSpec(memory_space=pl.ANY)],
        (far_ids, far_src, far_w, far_tgt, near_sum_own),
        [pltpu.VMEM((leaves + 1, 2 * cols, rank), F32), pltpu.SMEM((leaves * pair_n * far_n + 16,), jnp.int32)],
        flops=4 * mega,
    )
    (far_back,) = from_others(far_other, "rhs")
    (comp,) = call(
        comp_body, [((1, leaves * size), jnp.int32)], [VMEM] * 2, (tree_order, skel_order), flops=mega
    )
    halves = call(
        sum_body,
        [((cols, leaves // 2 * rank), BF)] * 2,
        [VMEM, VMEM] + [pl.BlockSpec(memory_space=pl.ANY)] * pair_n,
        (far_own, far_back, comp, *near_parts[1:]),
    )
    first_parts, last_parts = (over_pair(half, pair_n) for half in halves)
    acc_shape = (leaves * size // 256 * cols, 256)
    (acc,) = call(
        place_near_body,
        [(acc_shape, F32)],
        [VMEM] * (1 + pair_n),
        (tree_order, *near_parts),
        flops=3 * mega,
    )
    (acc,) = call(
        place_first_body,
        [(acc_shape, F32)],
        [VMEM] * (3 + pair_n),
        (comp, interp, acc, *first_parts),
        [pltpu.VMEM((cols, leaves // 2 * size), F32)],
        flops=2 * mega,
    )
    (out,) = call(
        place_last_body,
        [((cols, leaves * size), F32)],
        [VMEM] * (3 + pair_n),
        (comp, interp, acc, *last_parts),
        [pltpu.VMEM(acc_shape, F32), pltpu.VMEM((cols, leaves // 2 * size), F32)],
        flops=2 * mega,
    )
    return out.T


def solution(mesh):
    return jax.shard_map(
        on_device,
        mesh=mesh,
        in_specs=(
            P(("groups", "leaf"), None, None),
            P(("groups", "leaf"), "rhs"),
            P(("groups", "leaf"), None, None),
            P(("groups", "leaf"), None),
            P(("groups", "leaf"), None),
            P(("groups", "leaf"), "pair"),
            P(("groups", "leaf"), "pair"),
        ),
        out_specs=P(("groups", "leaf"), "rhs"),
        check_vma=False,
    )
```
